512 devices in a mesh: cond: 32 (over y_lo, z), grid: 16 (over x, y_hi, core).
Axes of the slice: x: 4, y: 8 (y_hi: 2, y_lo: 4; y = y_hi * 4 + y_lo), z: 8, core: 2. Of those that a mesh axis runs over, the one named last changes fastest.
Arguments:
- adjoint_source: float32 [64, 5, 32, 64, 128], P('cond', None, 'grid'), may hold values from -6 to 6
- adjoint_start: float32 [64, 5, 32, 64, 128], P('cond', None, 'grid'), may hold values from -4 to 4
- spectral_radius: float32 [32, 64, 128], P('grid'), may hold values from 0.5 to 2
- coupling: float32 [64, 5, 5], P('cond'), may hold values from -0.6 to 1.4, as said below
- left_vectors: float32 [64, 5, 5], P('cond'), may hold values from -0.6 to 1.4, as said below
- right_vectors: float32 [64, 5, 5], P('cond'), may hold values from -0.6 to 1.4, as said below
- implicit_scales: float32 [64, 5, 3], P('cond'), may hold values from 1 to 200
- sensitivity_map: float32 [64, 3, 5], P('cond'), may hold values from -4 to 4
- condition_weights: int32 [64], P('cond'), may hold values from 1 to 8
Outputs:
- adjoint: float32 [64, 5, 32, 64, 128], P('cond', None, 'grid')
- mesh_sensitivity: float32 [3, 32, 64, 128], P(None, 'grid')
The draws below stay inside these ranges and needn't reach their ends.
Inputs may be any that keep to these rules, and one draw needn't show every extreme that they name: `coupling`: mixing coefficients among the 5 flow variables. `left_vectors`: mixing coefficients among the 5 flow variables. `right_vectors`: mixing coefficients among the 5 flow variables.
All inputs are finite; a program needn't handle non-finite values.
Results may differ from the reference program's by a relative error of at most 0.0001.
Values sent between devices are 32-bit elements; how exact they have to be, the bound alone decides.
No kernel may reach another device: no remote copies, remote signals or barrier semaphores. Data moves between devices by JAX's collectives and lax.ppermute only.
A program may use at most 64 MiB of HBM per device.

```python
import math
import jax
import jax.numpy as jnp
from jax import lax

FIELDS = 5
NY = 64
NZ = 128
ITERS = 2
CONDS = 64
NX = 32


def mixing_matrix(key, offset):
    key = jax.random.fold_in(key, offset)
    key_diag, key_off = jax.random.split(key)
    off_part = jnp.clip(0.25 * jax.random.normal(key_off, (CONDS, FIELDS, FIELDS), jnp.float32), -0.6, 0.6)
    diag_part = jax.random.uniform(key_diag, (CONDS, FIELDS), jnp.float32, 0.6, 1.4)
    ident = jnp.eye(FIELDS, dtype=jnp.float32)
    return off_part * (1.0 - ident)[None] + ident[None] * diag_part[:, :, None]


def draw_coupling(key, part):
    return mixing_matrix(key, 11)


def draw_left_vectors(key, part):
    return mixing_matrix(key, 23)


def draw_right_vectors(key, part):
    return mixing_matrix(key, 37)


def set_ends(array, rng, smallest, high):
    longest = array.shape.index(max(array.shape))
    spots = []
    for shift in (0, 1):
        where = [jax.random.randint(jax.random.fold_in(rng, axis), (), 0, length) for axis, length in enumerate(array.shape)]
        where[longest] = (where[longest] + shift) % array.shape[longest]
        spots.append(tuple(where))
    return array.at[spots[0]].set(smallest).at[spots[1]].set(high)


def steps_of(own_key, shape, pieces, least, high):
    def one(position, blocks):
        draws = jax.random.uniform(jax.random.fold_in(jax.random.fold_in(own_key, 6), position), (blocks,), jnp.float32, least / len(pieces), high / len(pieces))
        return jnp.repeat(jnp.exp(draws), shape[position] // blocks).reshape((-1,) + (1,) * (len(shape) - position - 1))

    level = one(*pieces[0])
    for cut in pieces[1:]:
        level = level * one(*cut)
    return level


def noise(rng, shape, width, limit, shards=(), kind=jnp.bfloat16):
    level = steps_of(rng, shape, shards, -0.22, 0.18) if shards else 1.0
    array = jax.random.normal(rng, shape, jnp.float32) * width * level
    return jnp.minimum(jnp.maximum(array, -limit), limit).astype(kind)


def setup_inputs(seed: int = 0) -> dict:
    key_of = jax.random.split(jax.random.key(seed), 10)
    adjoint_source = noise(key_of[0], (CONDS, FIELDS, NX, NY, NZ), 1.0, 6.0, ((0, 32), (2, 16)), jnp.float32)
    adjoint_start = noise(key_of[1], (CONDS, FIELDS, NX, NY, NZ), 0.5, 4.0, ((0, 32), (2, 16)), jnp.float32)
    spectral_radius = jnp.clip(0.5 + 1.5 * jax.random.uniform(key_of[2], (NX, NY, NZ), jnp.float32) ** steps_of(key_of[2], (NX, NY, NZ), ((0, 16),), -0.2, 0.2), 0.5, 2.0)
    coupling = draw_coupling(jax.random.fold_in(key_of[9], 71), 0)
    left_vectors = draw_left_vectors(jax.random.fold_in(key_of[9], 71), 0)
    right_vectors = draw_right_vectors(jax.random.fold_in(key_of[9], 71), 0)
    implicit_scales = jnp.clip(jnp.exp(math.log(200.0) - 5.2983174 * jax.random.uniform(key_of[6], (CONDS, FIELDS, 3), jnp.float32) ** steps_of(key_of[6], (CONDS, FIELDS, 3), ((0, 32),), -0.2, 0.2)), 1.0, 200.0)
    sensitivity_map = noise(key_of[7], (CONDS, 3, FIELDS), 1.0, 4.0, ((0, 32),), jnp.float32)
    condition_weights = set_ends(jax.random.randint(key_of[8], (CONDS,), 1, 9), jax.random.fold_in(key_of[8], 1), 1, 8).astype(jnp.int32)
    return {"adjoint_source": adjoint_source, "adjoint_start": adjoint_start, "spectral_radius": spectral_radius, "coupling": coupling, "left_vectors": left_vectors, "right_vectors": right_vectors, "implicit_scales": implicit_scales, "sensitivity_map": sensitivity_map, "condition_weights": condition_weights}


HIGH = lax.Precision.HIGHEST

def sine_tables(length):
    counter = jnp.arange(length, dtype=jnp.int32) + 1
    product = (counter[:, None] * counter[None, :]).astype(jnp.float32)
    sine_table = math.sqrt(2.0 / (length + 1)) * jnp.sin(product * (math.pi / (length + 1)))
    spectrum = 2.0 - 2.0 * jnp.cos(counter.astype(jnp.float32) * (math.pi / (length + 1)))
    return (sine_table, spectrum)

def laplace(values):
    padded = jnp.pad(values, ((0, 0), (1, 1), (1, 1), (1, 1)))
    beside = padded[:, 2:, 1:-1, 1:-1] + padded[:, :-2, 1:-1, 1:-1]
    beside = beside + padded[:, 1:-1, 2:, 1:-1] + padded[:, 1:-1, :-2, 1:-1]
    beside = beside + padded[:, 1:-1, 1:-1, 2:] + padded[:, 1:-1, 1:-1, :-2]
    return 6.0 * values - beside

def reference(adjoint_source, adjoint_start, spectral_radius, coupling, left_vectors, right_vectors, implicit_scales, sensitivity_map, condition_weights):
    table_x, spec_x = sine_tables(NX)
    table_y, spec_y = sine_tables(NY)
    table_z, spec_z = sine_tables(NZ)

    def one_condition(items):
        source, adjoint, coup, left, right, rates = items
        for repeat in range(ITERS):
            residual = source - spectral_radius[None] * adjoint - jnp.einsum('fg,gxyz->fxyz', coup, laplace(adjoint), precision=HIGH)
            charac = jnp.einsum('fg,gxyz->fxyz', left, residual, precision=HIGH)
            denom = 1.0 + rates[:, 0:1] * (spec_x + spec_x * spec_x)[None, :]
            charac = jnp.einsum('jk,fkyz->fjyz', table_x, charac, precision=HIGH) / denom[:, :, None, None]
            charac = jnp.einsum('jk,fkyz->fjyz', table_x, charac, precision=HIGH)
            denom = 1.0 + rates[:, 1:2] * (spec_y + spec_y * spec_y)[None, :]
            charac = jnp.einsum('jk,fxkz->fxjz', table_y, charac, precision=HIGH) / denom[:, None, :, None]
            charac = jnp.einsum('jk,fxkz->fxjz', table_y, charac, precision=HIGH)
            denom = 1.0 + rates[:, 2:3] * (spec_z + spec_z * spec_z)[None, :]
            charac = jnp.einsum('jk,fxyk->fxyj', table_z, charac, precision=HIGH) / denom[:, None, None, :]
            charac = jnp.einsum('jk,fxyk->fxyj', table_z, charac, precision=HIGH)
            adjoint = adjoint + jnp.einsum('fg,gxyz->fxyz', right, charac, precision=HIGH)
        return adjoint
    adjoint = lax.map(one_condition, (adjoint_source, adjoint_start, coupling, left_vectors, right_vectors, implicit_scales))

    def one_term(items):
        values, smap = items
        padded = jnp.pad(values, ((0, 0), (1, 1), (1, 1), (1, 1)))
        diff_x = padded[:, 2:, 1:-1, 1:-1] - padded[:, :-2, 1:-1, 1:-1]
        diff_y = padded[:, 1:-1, 2:, 1:-1] - padded[:, 1:-1, :-2, 1:-1]
        diff_z = padded[:, 1:-1, 1:-1, 2:] - padded[:, 1:-1, 1:-1, :-2]
        stacked = jnp.stack([values * diff_x, values * diff_y, values * diff_z], axis=0)
        return jnp.einsum('kf,kfxyz->kxyz', smap, stacked, precision=HIGH)
    terms = lax.map(one_term, (adjoint, sensitivity_map))
    weights = condition_weights.astype(jnp.float32)
    total = jnp.einsum('c,ckxyz->kxyz', weights, terms, precision=HIGH)
    return (adjoint, total / CONDS)
```

```python
import functools
import math

import jax
import jax.numpy as jnp
import numpy as np
from jax import lax
from jax.experimental import pallas as pl
from jax.experimental.pallas import tpu as pltpu
from jax.sharding import PartitionSpec as P

HIGH = lax.Precision.HIGHEST
F32 = jnp.float32
FIELDS = 5
VMEM = pl.BlockSpec(memory_space=pltpu.VMEM)
SMEM = pl.BlockSpec(memory_space=pltpu.SMEM)
LIMIT = 40 * 1024 * 1024


def dot(a, b):
    return jnp.dot(a, b, precision=HIGH, preferred_element_type=F32)


def sine_tables(length):
    counter = np.arange(1, length + 1, dtype=np.float64)
    sine = math.sqrt(2.0 / (length + 1)) * np.sin(
        counter[:, None] * counter[None, :] * (math.pi / (length + 1))
    )
    spectrum = 2.0 - 2.0 * np.cos(counter * (math.pi / (length + 1)))
    return sine.astype(np.float32), (spectrum + spectrum * spectrum).astype(np.float32)


def call(kernel, outs, in_specs, flops, name, scratch=()):
    return pl.pallas_call(
        kernel,
        out_shape=outs,
        in_specs=in_specs,
        out_specs=jax.tree.map(lambda _: VMEM, outs),
        scratch_shapes=list(scratch),
        compiler_params=pltpu.CompilerParams(vmem_limit_bytes=LIMIT),
        cost_estimate=pl.CostEstimate(flops=flops, bytes_accessed=4_000_000, transcendentals=0),
        name=name,
    )


def shape(*dims):
    return jax.ShapeDtypeStruct(dims, F32)


def shifted(v, axis, step):
    size = v.shape[axis]
    rolled = pltpu.roll(v, (-step) % size, axis)
    at = lax.broadcasted_iota(jnp.int32, v.shape, axis)
    return jnp.where(at == (size - 1 if step > 0 else 0), 0.0, rolled)


def tables_kernel(rates, side, sine_z, spec_z, sine_y, spec_y, left_x, right_x, spec_x,
                  solve_z, solve_y, solve_x, solve_zb):
    for c in range(2):
        for f in range(FIELDS):
            denom = 1.0 + rates[c, f, 2] * spec_z[...]
            solve_z[c, f] = dot(sine_z[...] / denom, sine_z[...])
            denom = 1.0 + rates[c, f, 1] * spec_y[...]
            solve_y[c, f] = dot(sine_y[...] / denom, sine_y[...])
    mine = side[0]
    n = left_x.shape[0]
    row = lax.broadcasted_iota(jnp.int32, (n, n), 0)
    col = lax.broadcasted_iota(jnp.int32, (n, n), 1)
    same = (row & 7) == (col & 7)
    for f in range(FIELDS):
        denom = 1.0 + rates[mine, f, 0] * spec_x[...]
        solve_x[f] = jnp.where(same, dot(left_x[...] / denom, right_x[...]), 0.0)
        solve_zb[f] = solve_z[mine, f]


def first_kernel(coupling, left, adjoint, low, high, source, radius, solve_z, solve_y, out, lapped):
    blocks = adjoint.shape[3] // 8
    for c in range(2):
        for x in range(2):
            for f in range(FIELDS):
                v = adjoint[c, f, x]
                beside = (low[c, f] if x == 0 else adjoint[c, f, 0]) + (
                    adjoint[c, f, 1] if x == 0 else high[c, f]
                )
                beside = beside + shifted(v, 0, 1) + shifted(v, 0, -1)
                beside = beside + shifted(v, 1, 1) + shifted(v, 1, -1)
                lapped[f] = 6.0 * v - beside
            sr = radius[x]
            residual = []
            for f in range(FIELDS):
                r = source[c, f, x] - sr * adjoint[c, f, x]
                for g in range(FIELDS):
                    r = r - coupling[c, f, g] * lapped[g]
                residual.append(r)
            for f in range(FIELDS):
                r = left[c, f, 0] * residual[0]
                for g in range(1, FIELDS):
                    r = r + left[c, f, g] * residual[g]
                r = dot(solve_y[c, f], dot(r, solve_z[c, f]))
                for b in range(blocks):
                    out[(b // 2) * 4 + c * 2 + b % 2, f, x] = r[8 * b : 8 * b + 8]
            for b in range(blocks):
                out[(b // 2) * 4 + c * 2 + b % 2, FIELDS, x] = sr[8 * b : 8 * b + 8]


def across_kernel(lines, solve_x, solved, to_prev, to_next):
    n = solve_x.shape[1]
    for f in range(FIELDS):
        u = dot(solve_x[f], lines[:, f].reshape(n, 128)).reshape(n // 8, 8, 128)
        solved[f] = u
        quad = u.reshape(n // 32, 4, 8, 128)
        for j in range(4):
            to_prev[f, :, 2 * j : 2 * j + 2, :] = quad[:, j, 0:2, :]
            to_next[f, :, 2 * j : 2 * j + 2, :] = quad[:, j, 6:8, :]


def second_kernel(rates, inner, both, both_lap, solved, from_prev, from_next, lines, solve_x, solve_z,
                  out, lapped, kept):
    nx = solved.shape[1]
    full = (nx, 8, 128)
    row = lax.broadcasted_iota(jnp.int32, full, 1)
    has_prev, has_next = inner[0], inner[1]
    for f in range(FIELDS):
        u = solved[f]
        spread = lambda ref, at: jnp.stack(
            [pltpu.roll(ref[f], (at - 2 * j) % 8, 1) for j in range(4)], axis=1
        ).reshape(full)
        before, after = spread(from_prev, 6), spread(from_next, 0)
        up, down = pltpu.roll(u, 7, 1), pltpu.roll(u, 1, 1)
        nexts = jnp.where(row == 7, pltpu.roll(after, 7, 1), up)
        prevs = jnp.where(row == 0, pltpu.roll(before, 1, 1), down)
        ku = 2.0 * u - nexts - prevs
        k_before = (2.0 * before - pltpu.roll(before, 1, 1) - up) * has_prev
        k_after = (2.0 * after - pltpu.roll(after, 7, 1) - down) * has_next
        k_nexts = jnp.where(row == 7, pltpu.roll(k_after, 7, 1), pltpu.roll(ku, 7, 1))
        k_prevs = jnp.where(row == 0, pltpu.roll(k_before, 1, 1), pltpu.roll(ku, 1, 1))
        kku = 2.0 * ku - k_nexts - k_prevs
        kept[f] = 2.0 * (u + rates[f, 1] * (ku + kku))
        zero = jnp.zeros((1, 8, 128), F32)
        beside = jnp.concatenate([zero, u[:-1]], axis=0) + jnp.concatenate([u[1:], zero], axis=0)
        flat = u.reshape(nx * 8, 128)
        beside = beside + (shifted(flat, 1, 1) + shifted(flat, 1, -1)).reshape(full)
        lapped[f] = 4.0 * u + ku - beside
    sr = lines[:, FIELDS].reshape(full)
    for f in range(FIELDS):
        near = both[f, 0] * solved[0]
        far = both_lap[f, 0] * lapped[0]
        for g in range(1, FIELDS):
            near = near + both[f, g] * solved[g]
            far = far + both_lap[f, g] * lapped[g]
        v = (sr * near + far).reshape(nx * 8, 128)
        v = dot(solve_x[f], dot(v, solve_z[f]))
        out[:, f] = (kept[f] - v.reshape(full)).reshape(nx // 2, 2, 8, 128)


def update_kernel(right, adjoint, solved, solve_y, out, first, last, step):
    blocks = adjoint.shape[3] // 8
    for c in range(2):
        for x in range(2):
            for f in range(FIELDS):
                q = jnp.concatenate(
                    [solved[(b // 2) * 4 + c * 2 + b % 2, f, x] for b in range(blocks)], axis=0
                )
                step[f] = dot(solve_y[c, f], q)
            for f in range(FIELDS):
                a = adjoint[c, f, x]
                for g in range(FIELDS):
                    a = a + right[c, f, g] * step[g]
                out[c, f, x] = a
                if x == 0:
                    first[c, f] = a
                else:
                    last[c, f] = a


def terms_kernel(smap, weights, adjoint, low, high, out):
    for x in range(2):
        total = [None, None, None]
        for c in range(2):
            w = weights[c].astype(F32)
            for f in range(FIELDS):
                v = adjoint[c, f, x]
                diffs = (
                    (adjoint[c, f, 1] - low[c, f]) if x == 0 else (high[c, f] - adjoint[c, f, 0]),
                    shifted(v, 0, 1) - shifted(v, 0, -1),
                    shifted(v, 1, 1) - shifted(v, 1, -1),
                )
                for k in range(3):
                    t = (w * smap[c, k, f]) * (v * diffs[k])
                    total[k] = t if total[k] is None else total[k] + t
        for k in range(3):
            out[k, x] = total[k]


def sum_kernel(scale, pieces, out):
    total = pieces[0]
    for i in range(1, pieces.shape[0]):
        total = total + pieces[i]
    total = total * scale
    for i in range(out.shape[0]):
        out[i] = total


def exchange(first, last, axis, up, down):
    return lax.ppermute(last, axis, up), lax.ppermute(first, axis, down)


def body(
    adjoint_source,
    adjoint_start,
    spectral_radius,
    coupling,
    left_vectors,
    right_vectors,
    implicit_scales,
    sensitivity_map,
    condition_weights,
):
    peers = lax.axis_size("grid")
    conds = lax.axis_size("cond")
    _, fields, planes, ny, nz = adjoint_start.shape
    nx = peers * planes
    rows_b = nx * 8

    me = lax.axis_index("grid")
    side = (me // 2) % 2
    place = (me // 4) * 2 + me % 2

    sine_z, spec_z = sine_tables(nz)
    sine_y, spec_y = sine_tables(ny)
    sine_x, spec_x = sine_tables(nx)
    left_x = np.repeat(sine_x, 8, axis=0)

    up = [(i, i + 1) for i in range(peers - 1)]
    down = [(j, i) for i, j in up]
    low, high = exchange(adjoint_start[:, :, 0], adjoint_start[:, :, planes - 1], "grid", up, down)

    solve_z, solve_y, solve_x, solve_zb = call(
        tables_kernel,
        (shape(2, fields, nz, nz), shape(2, fields, ny, ny), shape(fields, rows_b, rows_b), shape(fields, nz, nz)),
        [SMEM, SMEM] + [VMEM] * 7,
        100_000_000,
        "solve_tables",
    )(
        implicit_scales,
        side.reshape(1).astype(jnp.int32),
        jnp.asarray(sine_z),
        jnp.asarray(spec_z[None, :]),
        jnp.asarray(sine_y),
        jnp.asarray(spec_y[None, :]),
        jnp.asarray(left_x),
        jnp.asarray(left_x.T.copy()),
        jnp.asarray(spec_x[None, :]),
    )

    lines = call(
        first_kernel,
        shape(peers, fields + 1, planes, 8, nz),
        [SMEM, SMEM] + [VMEM] * 7,
        200_000_000,
        "first_residual",
        [pltpu.VMEM((fields, ny, nz), F32)],
    )(coupling, left_vectors, adjoint_start, low, high, adjoint_source, spectral_radius, solve_z, solve_y)

    lines = lax.all_to_all(lines, "grid", 0, 0, tiled=True)

    solved, to_prev, to_next = call(
        across_kernel,
        (shape(fields, nx, 8, nz), shape(fields, nx // 4, 8, nz), shape(fields, nx // 4, 8, nz)),
        [VMEM, VMEM],
        100_000_000,
        "solve_across",
    )(lines, solve_x)

    spot = lambda s, b: (b // 2) * 4 + s * 2 + b % 2
    blocks = peers // 2
    up_b = [(spot(s, b), spot(s, b + 1)) for s in range(2) for b in range(blocks - 1)]
    down_b = [(j, i) for i, j in up_b]
    from_prev, from_next = exchange(to_prev, to_next, "grid", up_b, down_b)

    pick = lambda v: lax.dynamic_index_in_dim(v, side, 0, keepdims=False)
    left_b, coup_b, right_b = pick(left_vectors), pick(coupling), pick(right_vectors)
    both = jnp.sum(left_b[:, :, None] * right_b[None, :, :], axis=1)
    inner_mix = jnp.sum(coup_b[:, :, None] * right_b[None, :, :], axis=1)
    both_lap = jnp.sum(left_b[:, :, None] * inner_mix[None, :, :], axis=1)
    inner = jnp.stack([place > 0, place < blocks - 1]).astype(F32)

    step = call(
        second_kernel,
        shape(peers, fields, planes, 8, nz),
        [SMEM] * 4 + [VMEM] * 6,
        300_000_000,
        "second_residual",
        [pltpu.VMEM((fields, nx, 8, nz), F32), pltpu.VMEM((fields, nx, 8, nz), F32)],
    )(pick(implicit_scales), inner, both, both_lap, solved, from_prev, from_next, lines, solve_x, solve_zb)

    step = lax.all_to_all(step, "grid", 0, 0, tiled=True)

    adjoint, first, last = call(
        update_kernel,
        (shape(2, fields, planes, ny, nz), shape(2, fields, ny, nz), shape(2, fields, ny, nz)),
        [SMEM] + [VMEM] * 3,
        60_000_000,
        "update",
        [pltpu.VMEM((fields, ny, nz), F32)],
    )(right_vectors, adjoint_start, step, solve_y)

    low, high = exchange(first, last, "grid", up, down)

    terms = call(
        terms_kernel,
        shape(3, planes, ny, nz),
        [SMEM, SMEM] + [VMEM] * 3,
        10_000_000,
        "terms",
    )(sensitivity_map, condition_weights, adjoint, low, high)

    tiles = 3 * planes * ny // 8
    each = -(-tiles // conds)
    pieces = terms.reshape(tiles * 8, nz)
    pieces = jnp.pad(pieces, ((0, (conds * each - tiles) * 8), (0, 0))).reshape(conds, each * 8, nz)
    pieces = lax.all_to_all(pieces, "cond", 0, 0, tiled=True)
    scale = 1.0 / (conds * condition_weights.shape[0])
    pieces = call(
        functools.partial(sum_kernel, scale),
        shape(conds, each * 8, nz),
        [VMEM],
        1_000_000,
        "sum_conditions",
    )(pieces)
    pieces = lax.all_to_all(pieces, "cond", 0, 0, tiled=True)
    total = pieces.reshape(conds * each * 8, nz)[: tiles * 8].reshape(3, planes, ny, nz)
    return (adjoint, total)


def solution(mesh):
    in_specs = (
        P("cond", None, "grid", None, None),
        P("cond", None, "grid", None, None),
        P("grid", None, None),
        P("cond", None, None),
        P("cond", None, None),
        P("cond", None, None),
        P("cond", None, None),
        P("cond", None, None),
        P("cond"),
    )
    out_specs = (P("cond", None, "grid", None, None), P(None, "grid", None, None))
    return jax.shard_map(body, mesh=mesh, in_specs=in_specs, out_specs=out_specs, check_vma=False)
```

```python
import functools
import math

import jax
import jax.numpy as jnp
import numpy as np
from jax import lax
from jax.experimental import pallas as pl
from jax.experimental.pallas import tpu as pltpu
from jax.sharding import PartitionSpec as P

HIGH = lax.Precision.HIGHEST
F32 = jnp.float32
FIELDS = 5
VMEM = pl.BlockSpec(memory_space=pltpu.VMEM)
SMEM = pl.BlockSpec(memory_space=pltpu.SMEM)
LIMIT = 20 * 1024 * 1024


def dot(a, b):
    return jnp.dot(a, b, precision=HIGH, preferred_element_type=F32)


def sine_tables(length):
    counter = np.arange(1, length + 1, dtype=np.float64)
    sine = math.sqrt(2.0 / (length + 1)) * np.sin(
        counter[:, None] * counter[None, :] * (math.pi / (length + 1))
    )
    spectrum = 2.0 - 2.0 * np.cos(counter * (math.pi / (length + 1)))
    return sine.astype(np.float32), (spectrum + spectrum * spectrum).astype(np.float32)


def call(kernel, outs, in_specs, flops, name, scratch=()):
    return pl.pallas_call(
        kernel,
        out_shape=outs,
        in_specs=in_specs,
        out_specs=jax.tree.map(lambda _: VMEM, outs),
        scratch_shapes=list(scratch),
        compiler_params=pltpu.CompilerParams(vmem_limit_bytes=LIMIT),
        cost_estimate=pl.CostEstimate(flops=flops, bytes_accessed=4_000_000, transcendentals=0),
        name=name,
    )


def shape(*dims):
    return jax.ShapeDtypeStruct(dims, F32)


def shifted(v, axis, step):
    size = v.shape[axis]
    rolled = pltpu.roll(v, (-step) % size, axis)
    at = lax.broadcasted_iota(jnp.int32, v.shape, axis)
    return jnp.where(at == (size - 1 if step > 0 else 0), 0.0, rolled)


def tables_kernel(rates, side, sine_z, spec_z, sine_y, spec_y, left_x, right_x, spec_x,
                  solve_z, solve_y, solve_x, solve_zb):
    for c in range(2):
        for f in range(FIELDS):
            denom = 1.0 + rates[c, f, 2] * spec_z[...]
            solve_z[c, f] = dot(sine_z[...] / denom, sine_z[...])
            denom = 1.0 + rates[c, f, 1] * spec_y[...]
            solve_y[c, f] = dot(sine_y[...] / denom, sine_y[...])
    mine = side[0]
    n = left_x.shape[0]
    row = lax.broadcasted_iota(jnp.int32, (n, n), 0)
    col = lax.broadcasted_iota(jnp.int32, (n, n), 1)
    same = (row & 7) == (col & 7)
    for f in range(FIELDS):
        denom = 1.0 + rates[mine, f, 0] * spec_x[...]
        solve_x[f] = jnp.where(same, dot(left_x[...] / denom, right_x[...]), 0.0)
        solve_zb[f] = solve_z[mine, f]


def spot(c, b):
    return (b // 2) * 4 + c * 2 + b % 2


def first_kernel(
    core, coupling, left, left_coup, adjoint, inner, source, radius, solve_z, solve_y, out, lapped, stage
):
    ny = adjoint.shape[3]
    blocks = ny // 8
    me = core[0]
    before, after = me.astype(F32), (1 - me).astype(F32)
    for c in range(2):
        for x in range(2):
            for f in range(FIELDS):
                v = adjoint[c, f, x]
                beside = adjoint[c, f, 1 - x] + inner[c, f] * (before if x == 0 else after)
                beside = beside + shifted(v, 0, 1) + shifted(v, 0, -1)
                beside = beside + shifted(v, 1, 1) + shifted(v, 1, -1)
                lapped[f] = 6.0 * v - beside
            sr = radius[x]
            residual = []
            for f in range(FIELDS):
                r = source[c, f, x] - sr * adjoint[c, f, x]
                for g in range(FIELDS):
                    r = r - coupling[c, f, g] * lapped[g]
                residual.append(r)
            for f in range(FIELDS):
                r = left[c, f, 0] * residual[0]
                for g in range(1, FIELDS):
                    r = r + left[c, f, g] * residual[g]
                stage[f, x * ny : x * ny + ny] = r
        outer = [adjoint[c, g, me] for g in range(FIELDS)]
        for f in range(FIELDS):
            r = left_coup[c, f, 0] * outer[0]
            for g in range(1, FIELDS):
                r = r + left_coup[c, f, g] * outer[g]
            stage[f, 2 * ny : 3 * ny] = r
        for f in range(FIELDS):
            r = dot(stage[f], solve_z[c, f])
            for p in range(3):
                s = dot(solve_y[c, f], r[p * ny : p * ny + ny])
                for b in range(blocks):
                    out[spot(c, b), 3 * f + p] = s[8 * b : 8 * b + 8]
        for x in range(2):
            for b in range(blocks):
                out[spot(c, b), 3 * FIELDS + x] = radius[x, 8 * b : 8 * b + 8]


def across_kernel(core, lines, solve_x, adjoint, solved, to_prev, to_next, outer):
    n = solve_x.shape[1]
    peers = lines.shape[0]
    zero = jnp.zeros((1, 8, 128), F32)
    for f in range(FIELDS):
        w = lines[:, 3 * f : 3 * f + 3].reshape(peers // 2, 6, 8, 128)
        plane_0 = w[:, 0] + jnp.concatenate([zero, w[:-1, 5]], axis=0)
        plane_3 = w[:, 4] + jnp.concatenate([w[1:, 2], zero], axis=0)
        w = jnp.stack([plane_0, w[:, 1], w[:, 3], plane_3], axis=1).reshape(n, 128)
        u = dot(solve_x[f], w).reshape(n // 8, 8, 128)
        solved[f] = u
        quad = u.reshape(n // 32, 4, 8, 128)
        for j in range(4):
            to_prev[f, :, 2 * j : 2 * j + 2, :] = quad[:, j, 0:2, :]
            to_next[f, :, 2 * j : 2 * j + 2, :] = quad[:, j, 6:8, :]
    for c in range(2):
        for f in range(FIELDS):
            outer[c, f] = adjoint[c, f, core[0]]


def second_kernel(rates, inner, both, both_lap, solved, from_prev, from_next, lines, solve_x, solve_z,
                  out, lapped, kept):
    nx = solved.shape[1]
    full = (nx, 8, 128)
    row = lax.broadcasted_iota(jnp.int32, full, 1)
    has_prev, has_next = inner[0], inner[1]
    for f in range(FIELDS):
        u = solved[f]
        spread = lambda ref, at: jnp.stack(
            [pltpu.roll(ref[f], (at - 2 * j) % 8, 1) for j in range(4)], axis=1
        ).reshape(full)
        before, after = spread(from_prev, 6), spread(from_next, 0)
        up, down = pltpu.roll(u, 7, 1), pltpu.roll(u, 1, 1)
        nexts = jnp.where(row == 7, pltpu.roll(after, 7, 1), up)
        prevs = jnp.where(row == 0, pltpu.roll(before, 1, 1), down)
        ku = 2.0 * u - nexts - prevs
        k_before = (2.0 * before - pltpu.roll(before, 1, 1) - up) * has_prev
        k_after = (2.0 * after - pltpu.roll(after, 7, 1) - down) * has_next
        k_nexts = jnp.where(row == 7, pltpu.roll(k_after, 7, 1), pltpu.roll(ku, 7, 1))
        k_prevs = jnp.where(row == 0, pltpu.roll(k_before, 1, 1), pltpu.roll(ku, 1, 1))
        kku = 2.0 * ku - k_nexts - k_prevs
        kept[f] = 2.0 * (u + rates[f, 1] * (ku + kku))
        zero = jnp.zeros((1, 8, 128), F32)
        beside = jnp.concatenate([zero, u[:-1]], axis=0) + jnp.concatenate([u[1:], zero], axis=0)
        flat = u.reshape(nx * 8, 128)
        beside = beside + (shifted(flat, 1, 1) + shifted(flat, 1, -1)).reshape(full)
        lapped[f] = 4.0 * u + ku - beside
    sr = lines[:, 3 * FIELDS :].reshape(full)
    for f in range(FIELDS):
        near = both[f, 0] * solved[0]
        far = both_lap[f, 0] * lapped[0]
        for g in range(1, FIELDS):
            near = near + both[f, g] * solved[g]
            far = far + both_lap[f, g] * lapped[g]
        v = (sr * near + far).reshape(nx * 8, 128)
        v = dot(solve_x[f], dot(v, solve_z[f]))
        q = kept[f] - v.reshape(full)
        chips = q.reshape(nx // 4, 4, 8, 128)
        zero = jnp.zeros((1, 8, 128), F32)
        outer_0 = jnp.concatenate([zero, chips[:-1, 3]], axis=0)
        outer_1 = jnp.concatenate([chips[1:, 0], zero], axis=0)
        out[:, 3 * f : 3 * f + 3] = jnp.stack(
            [chips[:, 0], chips[:, 1], outer_0, chips[:, 2], chips[:, 3], outer_1], axis=1
        ).reshape(nx // 2, 3, 8, 128)


def gathered(solved, c, tile, blocks):
    return jnp.concatenate([solved[spot(c, b), tile] for b in range(blocks)], axis=0)


def update_kernel(core, right, adjoint, solved, solve_y, out, inner, step):
    blocks = adjoint.shape[3] // 8
    me = core[0]
    for c in range(2):
        for x in range(2):
            for f in range(FIELDS):
                step[x, f] = dot(solve_y[c, f], gathered(solved, c, 3 * f + x, blocks))
        for f in range(FIELDS):
            planes = []
            for x in range(2):
                a = adjoint[c, f, x]
                for g in range(FIELDS):
                    a = a + right[c, f, g] * step[x, g]
                out[c, f, x] = a
                planes.append(a)
            inner[c, f] = jnp.where(me == 0, planes[1], planes[0])


def inside_kernel(right, smap, weights, adjoint, start_outer, solved, solve_y, outer, terms, step):
    blocks = adjoint.shape[3] // 8
    for c in range(2):
        for f in range(FIELDS):
            step[f] = dot(solve_y[c, f], gathered(solved, c, 3 * f + 2, blocks))
        for f in range(FIELDS):
            a = start_outer[c, f]
            for g in range(FIELDS):
                a = a + right[c, f, g] * step[g]
            outer[c, f] = a
    for x in range(2):
        total = [None, None]
        for c in range(2):
            w = weights[c].astype(F32)
            for f in range(FIELDS):
                v = adjoint[c, f, x]
                for k in range(2):
                    diff = shifted(v, k, 1) - shifted(v, k, -1)
                    t = (w * smap[c, k + 1, f]) * (v * diff)
                    total[k] = t if total[k] is None else total[k] + t
        for k in range(2):
            terms[k, x] = total[k]


def terms_kernel(core, smap, weights, adjoint, inner, outer, inside, out):
    me = core[0]
    ny = adjoint.shape[3]
    each = out.shape[1] // 8

    def store(k, x, v):
        for i in range(ny // 8):
            piece, at = divmod((k * 2 + x) * (ny // 8) + i, each)
            out[piece, 8 * at : 8 * at + 8] = v[8 * i : 8 * i + 8]

    totals = [None, None]
    for c in range(2):
        w = weights[c].astype(F32)
        for f in range(FIELDS):
            low = jnp.where(me == 0, outer[c, f], inner[c, f])
            high = jnp.where(me == 0, inner[c, f], outer[c, f])
            s = w * smap[c, 0, f]
            t = (
                s * (adjoint[c, f, 0] * (adjoint[c, f, 1] - low)),
                s * (adjoint[c, f, 1] * (high - adjoint[c, f, 0])),
            )
            totals = [t[x] if totals[x] is None else totals[x] + t[x] for x in range(2)]
    for x in range(2):
        store(0, x, totals[x])
        for k in range(2):
            store(k + 1, x, inside[k, x])
    for tile in range(6 * ny // 8, out.shape[0] * each):
        piece, at = divmod(tile, each)
        out[piece, 8 * at : 8 * at + 8] = jnp.zeros((8, out.shape[2]), F32)


def sum_kernel(scale, pieces, out):
    total = pieces[0]
    for i in range(1, pieces.shape[0]):
        total = total + pieces[i]
    total = total * scale
    for i in range(out.shape[0]):
        out[i] = total


def body(
    adjoint_source,
    adjoint_start,
    spectral_radius,
    coupling,
    left_vectors,
    right_vectors,
    implicit_scales,
    sensitivity_map,
    condition_weights,
):
    peers = lax.axis_size("grid")
    conds = lax.axis_size("cond")
    _, fields, planes, ny, nz = adjoint_start.shape
    nx = peers * planes
    rows_b = nx * 8

    me = lax.axis_index("grid")
    side = (me // 2) % 2
    place = (me // 4) * 2 + me % 2

    sine_z, spec_z = sine_tables(nz)
    sine_y, spec_y = sine_tables(ny)
    sine_x, spec_x = sine_tables(nx)
    left_x = np.repeat(sine_x, 8, axis=0)

    core = me % 2
    core_arg = core.reshape(1).astype(jnp.int32)
    cores = [(i, i ^ 1) for i in range(peers)]
    chips = [(i, i + 1) for i in range(1, peers - 1, 2)]
    chips = chips + [(j, i) for i, j in chips]
    inner = lax.dynamic_index_in_dim(adjoint_start, 1 - core, 2, keepdims=False)
    inner = lax.ppermute(inner, "grid", cores)

    solve_z, solve_y, solve_x, solve_zb = call(
        tables_kernel,
        (shape(2, fields, nz, nz), shape(2, fields, ny, ny), shape(fields, rows_b, rows_b), shape(fields, nz, nz)),
        [SMEM, SMEM] + [VMEM] * 7,
        100_000_000,
        "solve_tables",
    )(
        implicit_scales,
        side.reshape(1).astype(jnp.int32),
        jnp.asarray(sine_z),
        jnp.asarray(spec_z[None, :]),
        jnp.asarray(sine_y),
        jnp.asarray(spec_y[None, :]),
        jnp.asarray(left_x),
        jnp.asarray(left_x.T.copy()),
        jnp.asarray(spec_x[None, :]),
    )

    mix = lambda a, b: jnp.sum(a[..., :, :, None] * b[..., None, :, :], axis=-2)
    left_coup = mix(left_vectors, coupling)

    lines = call(
        first_kernel,
        shape(peers, 3 * fields + planes, 8, nz),
        [SMEM] * 4 + [VMEM] * 6,
        200_000_000,
        "first_residual",
        [pltpu.VMEM((fields, ny, nz), F32), pltpu.VMEM((fields, 3 * ny, nz), F32)],
    )(
        core_arg, coupling, left_vectors, left_coup,
        adjoint_start, inner, adjoint_source, spectral_radius, solve_z, solve_y,
    )

    lines = lax.all_to_all(lines, "grid", 0, 0, tiled=True)

    solved, to_prev, to_next, outer = call(
        across_kernel,
        (
            shape(fields, nx, 8, nz),
            shape(fields, nx // 4, 8, nz),
            shape(fields, nx // 4, 8, nz),
            shape(2, fields, ny, nz),
        ),
        [SMEM, VMEM, VMEM, VMEM],
        100_000_000,
        "solve_across",
    )(core_arg, lines, solve_x, adjoint_start)

    blocks = peers // 2
    up = [(spot(s, b), spot(s, b + 1)) for s in range(2) for b in range(blocks - 1)]
    down = [(j, i) for i, j in up]
    from_prev = lax.ppermute(to_next, "grid", up)
    from_next = lax.ppermute(to_prev, "grid", down)
    outer = lax.ppermute(outer, "grid", chips)

    pick = lambda v: lax.dynamic_index_in_dim(v, side, 0, keepdims=False)
    both = mix(pick(left_vectors), pick(right_vectors))
    both_lap = mix(pick(left_coup), pick(right_vectors))
    ends = jnp.stack([place > 0, place < blocks - 1]).astype(F32)

    step = call(
        second_kernel,
        shape(peers, 3 * fields, 8, nz),
        [SMEM] * 4 + [VMEM] * 6,
        300_000_000,
        "second_residual",
        [pltpu.VMEM((fields, nx, 8, nz), F32), pltpu.VMEM((fields, nx, 8, nz), F32)],
    )(pick(implicit_scales), ends, both, both_lap, solved, from_prev, from_next, lines, solve_x, solve_zb)

    step = lax.all_to_all(step, "grid", 0, 0, tiled=True)

    adjoint, inner = call(
        update_kernel,
        (shape(2, fields, planes, ny, nz), shape(2, fields, ny, nz)),
        [SMEM, SMEM] + [VMEM] * 3,
        60_000_000,
        "update",
        [pltpu.VMEM((2, fields, ny, nz), F32)],
    )(core_arg, right_vectors, adjoint_start, step, solve_y)

    inner = lax.ppermute(inner, "grid", cores)

    outer, inside = call(
        inside_kernel,
        (shape(2, fields, ny, nz), shape(2, planes, ny, nz)),
        [SMEM] * 3 + [VMEM] * 4,
        60_000_000,
        "inside_terms",
        [pltpu.VMEM((fields, ny, nz), F32)],
    )(right_vectors, sensitivity_map, condition_weights, adjoint, outer, step, solve_y)

    tiles = 3 * planes * ny // 8
    each = -(-tiles // conds)
    pieces = call(
        terms_kernel,
        shape(conds, each * 8, nz),
        [SMEM] * 3 + [VMEM] * 4,
        10_000_000,
        "terms",
    )(core_arg, sensitivity_map, condition_weights, adjoint, inner, outer, inside)
    pieces = lax.all_to_all(pieces, "cond", 0, 0, tiled=True)
    scale = 1.0 / (conds * condition_weights.shape[0])
    pieces = call(
        functools.partial(sum_kernel, scale),
        shape(conds, each * 8, nz),
        [VMEM],
        1_000_000,
        "sum_conditions",
    )(pieces)
    pieces = lax.all_to_all(pieces, "cond", 0, 0, tiled=True)
    total = pieces.reshape(conds * each * 8, nz)[: tiles * 8].reshape(3, planes, ny, nz)
    return (adjoint, total)


def solution(mesh):
    in_specs = (
        P("cond", None, "grid", None, None),
        P("cond", None, "grid", None, None),
        P("grid", None, None),
        P("cond", None, None),
        P("cond", None, None),
        P("cond", None, None),
        P("cond", None, None),
        P("cond", None, None),
        P("cond"),
    )
    out_specs = (P("cond", None, "grid", None, None), P(None, "grid", None, None))
    return jax.shard_map(body, mesh=mesh, in_specs=in_specs, out_specs=out_specs, check_vma=False)
```

```python
import functools
import math

import jax
import jax.numpy as jnp
import numpy as np
from jax import lax
from jax.experimental import pallas as pl
from jax.experimental.pallas import tpu as pltpu
from jax.sharding import PartitionSpec as P

F32 = jnp.float32
FIELDS = 5
VMEM = pl.BlockSpec(memory_space=pltpu.VMEM)
SMEM = pl.BlockSpec(memory_space=pltpu.SMEM)
LIMIT = 20 * 1024 * 1024
ANY = pl.BlockSpec(memory_space=pl.ANY)
COUP, LEFT, RIGHT, RATE, SENS = 0, 5, 10, 15, 18


def split(v):
    high = v.astype(jnp.bfloat16)
    return high, (v - high.astype(F32)).astype(jnp.bfloat16)


def dot(a, b):
    one = functools.partial(jnp.dot, preferred_element_type=F32)
    (a_high, a_low), (b_high, b_low) = split(a), split(b)
    return one(a_high, b_high) + (one(a_high, b_low) + one(a_low, b_high))


def exact(a, b):
    return jnp.dot(a, b, precision=lax.Precision.HIGHEST, preferred_element_type=F32)


def sine_tables(length):
    counter = np.arange(1, length + 1, dtype=np.float64)
    sine = math.sqrt(2.0 / (length + 1)) * np.sin(
        counter[:, None] * counter[None, :] * (math.pi / (length + 1))
    )
    spectrum = 2.0 - 2.0 * np.cos(counter * (math.pi / (length + 1)))
    return sine.astype(np.float32), (spectrum + spectrum * spectrum).astype(np.float32)


def call(kernel, outs, in_specs, flops, name, scratch=(), out_specs=None):
    return pl.pallas_call(
        kernel,
        out_shape=outs,
        in_specs=in_specs,
        out_specs=out_specs or jax.tree.map(lambda _: VMEM, outs),
        scratch_shapes=list(scratch),
        compiler_params=pltpu.CompilerParams(vmem_limit_bytes=LIMIT),
        cost_estimate=pl.CostEstimate(flops=flops, bytes_accessed=4_000_000, transcendentals=0),
        name=name,
    )


def shape(*dims):
    return jax.ShapeDtypeStruct(dims, F32)


def vmem(*dims):
    return pltpu.VMEM(dims, F32)


def fetch(sources, targets, sems):
    copies = [pltpu.make_async_copy(a, b, sems.at[i]) for i, (a, b) in enumerate(zip(sources, targets))]
    for copy in copies:
        copy.start()
    return copies


def shifted(v, axis, step):
    size = v.shape[axis]
    rolled = pltpu.roll(v, (-step) % size, axis)
    at = lax.broadcasted_iota(jnp.int32, v.shape, axis)
    return jnp.where(at == (size - 1 if step > 0 else 0), 0.0, rolled)


def mixed(weight, values):
    total = weight(0) * values[0]
    for g in range(1, FIELDS):
        total = total + weight(g) * values[g]
    return total


def spot(c, b):
    return (b // 2) * 4 + c * 2 + b % 2


def tables_kernel(pack, sine_z_in, sine_y_in, spec_in, solve_z, solve_y, sine_z, sine_y, spec, sems):
    for copy in fetch((sine_z_in, sine_y_in, spec_in), (sine_z, sine_y, spec), sems):
        copy.wait()
    ny = sine_y.shape[0]
    for c in range(2):
        for f in range(FIELDS):
            denom = 1.0 + pack[c, f, RATE + 2] * spec[0:1]
            solve_z[c, f] = exact(sine_z[...] / denom, sine_z[...])
            denom = 1.0 + pack[c, f, RATE + 1] * spec[1:2, :ny]
            solve_y[c, f] = exact(sine_y[...] / denom, sine_y[...])


def tables_y_kernel(pack, token, sine_y_in, spec_in, solve_y, sine_y, spec, sems):
    for copy in fetch((sine_y_in, spec_in), (sine_y, spec), sems):
        copy.wait()
    ny = sine_y.shape[0]
    for c in range(2):
        for f in range(FIELDS):
            denom = 1.0 + pack[c, f, RATE + 1] * spec[1:2, :ny]
            solve_y[c, f] = exact(sine_y[...] / denom, sine_y[...])


def tables_b_kernel(info, pack, token, sine_z_in, left_in, right_in, right_2_in, spec_in,
                    solve_x, ends_prev, ends_next, halo_prev, halo_next, solve_z, mixes,
                    sine_z, left, right, right_2, spec, sems):
    copies = fetch(
        (sine_z_in, left_in, right_in, right_2_in, spec_in), (sine_z, left, right, right_2, spec), sems
    )
    mine = info[1]
    for f in range(FIELDS):
        for g in range(FIELDS):
            near, far = 0.0, 0.0
            for h in range(FIELDS):
                near = near + pack[mine, f, LEFT + h] * pack[mine, h, RIGHT + g]
                inner = 0.0
                for i in range(FIELDS):
                    inner = inner + pack[mine, h, COUP + i] * pack[mine, i, RIGHT + g]
                far = far + pack[mine, f, LEFT + h] * inner
            mixes[0, f, g] = near
            mixes[1, f, g] = far
        mixes[2, f, 0] = pack[mine, f, RATE + 1]
    for copy in copies:
        copy.wait()
    n, nx = left.shape
    row, col = (lax.broadcasted_iota(jnp.int32, (n, n), i) for i in range(2))
    same = (row & 7) == (col & 7)
    row, col = (lax.broadcasted_iota(jnp.int32, (2 * nx, n), i) for i in range(2))
    prev_rows = (row & 1) == (col & 7)
    next_rows = (row & 1) + 6 == (col & 7)
    row, col = (lax.broadcasted_iota(jnp.int32, (2 * nx, 2 * nx), i) for i in range(2))
    from_last = ((row & 1) == 0) & ((col & 1) == 1)
    from_first = ((row & 1) == 1) & ((col & 1) == 0)
    for f in range(FIELDS):
        denom = 1.0 + pack[mine, f, RATE] * spec[2:3, :nx]
        scaled = left[...] / denom
        solve_x[f] = jnp.where(same, exact(scaled, right[...]), 0.0)
        scaled_2 = right_2[...].T / denom
        both = exact(scaled_2, right[...])
        ends_prev[f] = jnp.where(prev_rows, both, 0.0)
        ends_next[f] = jnp.where(next_rows, both, 0.0)
        both = exact(scaled_2, right_2[...])
        halo_prev[f] = jnp.where(from_last, both, 0.0)
        halo_next[f] = jnp.where(from_first, both, 0.0)
        denom = 1.0 + pack[mine, f, RATE + 2] * spec[0:1]
        solve_z[f] = exact(sine_z[...] / denom, sine_z[...])


def first_kernel(info, pack, adjoint, other, source_in, radius, solve_z, solve_y, out, token,
                 source, made, lapped, stage, sems, out_sems):
    copies = fetch([source_in.at[c] for c in range(2)], [source.at[c] for c in range(2)], sems)
    ny = adjoint.shape[3]
    blocks = ny // 8
    me = info[0]
    before, after = me.astype(F32), (1 - me).astype(F32)
    token[...] = jnp.zeros(token.shape, F32)
    stores = []
    for c in range(2):
        residual = {}
        for x in range(2):
            for f in range(FIELDS):
                v = adjoint[c, f, x]
                beside = adjoint[c, f, 1 - x]
                beside = beside + (other[c, f, 1] * before if x == 0 else other[c, f, 0] * after)
                beside = beside + shifted(v, 0, 1) + shifted(v, 0, -1)
                beside = beside + shifted(v, 1, 1) + shifted(v, 1, -1)
                lapped[x, f] = 6.0 * v - beside
        copies[c].wait()
        for x in range(2):
            sr = radius[x]
            residual = []
            for f in range(FIELDS):
                r = source[c, f, x] - sr * adjoint[c, f, x]
                for g in range(FIELDS):
                    r = r - pack[c, f, COUP + g] * lapped[x, g]
                residual.append(r)
            for f in range(FIELDS):
                stage[f, x * ny : x * ny + ny] = mixed(lambda g: pack[c, f, LEFT + g], residual)
        outer = [adjoint[c, g, me] for g in range(FIELDS)]
        outer = [mixed(lambda g: pack[c, f, COUP + g], outer) for f in range(FIELDS)]
        for f in range(FIELDS):
            stage[f, 2 * ny : 3 * ny] = mixed(lambda g: pack[c, f, LEFT + g], outer)
        for f in range(FIELDS):
            r = dot(stage[f], solve_z[c, f])
            r = jnp.concatenate([r[p * ny : p * ny + ny] for p in range(3)], axis=1)
            r = dot(solve_y[c, f], r)
            for p in range(3):
                for b in range(blocks):
                    made[b // 2, c, b % 2, 3 * f + p] = r[8 * b : 8 * b + 8, 128 * p : 128 * p + 128]
        for x in range(2):
            for b in range(blocks):
                made[b // 2, c, b % 2, 3 * FIELDS + x] = radius[x, 8 * b : 8 * b + 8]
        stores.append(pltpu.make_async_copy(made.at[:, c], out.at[:, c], out_sems.at[c]))
        stores[-1].start()
    for copy in stores:
        copy.wait()


def assembled(lines, f):
    zero = jnp.zeros((1, 8, 128), F32)
    w = lines[:, 3 * f : 3 * f + 3].reshape(lines.shape[0] // 2, 6, 8, 128)
    plane_0 = w[:, 0] + jnp.concatenate([zero, w[:-1, 5]], axis=0)
    plane_3 = w[:, 4] + jnp.concatenate([w[1:, 2], zero], axis=0)
    return jnp.stack([plane_0, w[:, 1], w[:, 3], plane_3], axis=1)


def ends_kernel(lines, ends_prev, ends_next, to_prev, to_next):
    for f in range(FIELDS):
        w = assembled(lines, f).reshape(-1, 128)
        to_prev[f] = dot(ends_prev[f], w)
        to_next[f] = dot(ends_next[f], w)


def second_kernel(info, mixes, lines, solve_x, solve_z, out, solved, lapped, kept):
    nx = out.shape[1]
    full = (nx, 8, 128)
    row = lax.broadcasted_iota(jnp.int32, full, 1)
    has_prev, has_next = info[2].astype(F32), info[3].astype(F32)
    zero = jnp.zeros((1, 8, 128), F32)
    for f in range(FIELDS):
        u = dot(solve_x[f], assembled(lines, f).reshape(nx * 8, 128)).reshape(full)
        solved[f] = u
        up = jnp.where(row == 7, 0.0, pltpu.roll(u, 7, 1))
        down = jnp.where(row == 0, 0.0, pltpu.roll(u, 1, 1))
        ku = 2.0 * u - up - down
        k_up = jnp.where(row == 7, -has_next * u, pltpu.roll(ku, 7, 1))
        k_down = jnp.where(row == 0, -has_prev * u, pltpu.roll(ku, 1, 1))
        kku = 2.0 * ku - k_up - k_down
        kept[f] = 2.0 * (u + mixes[2, f, 0] * (ku + kku))
        beside = jnp.concatenate([zero, u[:-1]], axis=0) + jnp.concatenate([u[1:], zero], axis=0)
        flat = u.reshape(nx * 8, 128)
        beside = beside + (shifted(flat, 1, 1) + shifted(flat, 1, -1)).reshape(full)
        lapped[f] = 4.0 * u + ku - beside
    sr = lines[:, 3 * FIELDS :].reshape(full)
    for f in range(FIELDS):
        near = mixed(lambda g: mixes[0, f, g], solved)
        far = mixed(lambda g: mixes[1, f, g], lapped)
        v = (sr * near + far).reshape(nx * 8, 128)
        v = dot(solve_x[f], dot(v, solve_z[f]))
        out[f] = kept[f] - v.reshape(full)


def halo_kernel(mixes, local, from_prev, from_next, halo_prev, halo_next, solve_z, out, token, made, sems):
    nx = local.shape[1]
    full = (nx, 8, 128)
    row = lax.broadcasted_iota(jnp.int32, full, 1)
    odd = (lax.broadcasted_iota(jnp.int32, (2 * nx, 128), 0) & 1) == 1
    zero = jnp.zeros((1, 8, 128), F32)
    token[...] = jnp.zeros(token.shape, F32)
    stores = []
    for f in range(FIELDS):
        first, last = from_prev[f], from_next[f]
        far = jnp.concatenate(
            [mixed(lambda g: mixes[1, f, g], from_prev), mixed(lambda g: mixes[1, f, g], from_next)], axis=0
        )
        far = dot(far, solve_z[f])
        far_prev, far_next = far[: 2 * nx], far[2 * nx :]
        scale = 2.0 * mixes[2, f, 0]
        add_prev = jnp.where(odd, first, first - 5.0 * pltpu.roll(first, 2 * nx - 1, 0))
        add_next = jnp.where(odd, last - 5.0 * pltpu.roll(last, 1, 0), last)
        add_prev = scale * add_prev + dot(halo_prev[f], far_prev)
        add_next = scale * add_next + dot(halo_next[f], far_next)
        spread = lambda v, at: jnp.stack(
            [pltpu.roll(v.reshape(nx // 4, 8, 128), (at - 2 * j) % 8, 1) for j in range(4)], axis=1
        ).reshape(full)
        q = local[f] + jnp.where(
            row < 2, spread(add_prev, 0), jnp.where(row >= 6, spread(add_next, 6), 0.0)
        )
        chips = q.reshape(nx // 4, 4, 8, 128)
        outer_0 = jnp.concatenate([zero, chips[:-1, 3]], axis=0)
        outer_1 = jnp.concatenate([chips[1:, 0], zero], axis=0)
        made[:, 3 * f : 3 * f + 3] = jnp.stack(
            [chips[:, 0], chips[:, 1], outer_0, chips[:, 2], chips[:, 3], outer_1], axis=1
        ).reshape(nx // 2, 3, 8, 128)
        part = pl.ds(3 * f, 3)
        stores.append(pltpu.make_async_copy(made.at[:, part], out.at[:, part], sems.at[f]))
        stores[-1].start()
    for copy in stores:
        copy.wait()


def gathered(solved, c, tile, blocks):
    return jnp.concatenate([solved[spot(c, b), tile] for b in range(blocks)], axis=0)


def update_kernel(info, pack, adjoint, solved, solve_y, out, inner, step):
    ny = adjoint.shape[3]
    me = info[0]
    for c in range(2):
        for f in range(FIELDS):
            q = jnp.concatenate([gathered(solved, c, 3 * f + x, ny // 8) for x in range(2)], axis=1)
            step[f] = dot(solve_y[c, f], q)
        steps = [[step[g, :, 128 * x : 128 * x + 128] for g in range(FIELDS)] for x in range(2)]
        for f in range(FIELDS):
            planes = [
                adjoint[c, f, x] + mixed(lambda g: pack[c, f, RIGHT + g], steps[x]) for x in range(2)
            ]
            for x in range(2):
                out[c, f, x] = planes[x]
            inner[c, f] = jnp.where(me == 0, planes[1], planes[0])


def inside_kernel(info, pack, adjoint, start_outer, solved, solve_y, terms, step):
    ny = adjoint.shape[3]
    me = info[0]
    totals = [[0.0, 0.0] for _ in range(3)]
    for c in range(2):
        for f in range(FIELDS):
            step[f] = dot(solve_y[c, f], gathered(solved, c, 3 * f + 2, ny // 8))
        for f in range(FIELDS):
            outer = start_outer[c, f] + mixed(lambda g: pack[c, f, RIGHT + g], step)
            w = [pack[c, f, SENS + k] for k in range(3)]
            v = [adjoint[c, f, x] for x in range(2)]
            pair = v[0] * v[1]
            edge = jnp.where(me == 0, v[0], v[1]) * outer
            at_0, at_1 = jnp.where(me == 0, edge, 0.0), jnp.where(me == 0, 0.0, edge)
            totals[0][0] += w[0] * (pair - at_0)
            totals[0][1] += w[0] * (at_1 - pair)
            for x in range(2):
                for k in range(2):
                    totals[k + 1][x] += w[k + 1] * (v[x] * (shifted(v[x], k, 1) - shifted(v[x], k, -1)))
    for k in range(3):
        for x in range(2):
            terms[k, x] = totals[k][x]


def terms_kernel(info, pack, mine, other, inside, out):
    me = info[0]
    ny = mine.shape[2]
    each = out.shape[1] // 8

    def store(k, x, v):
        for i in range(ny // 8):
            piece, at = divmod((k * 2 + x) * (ny // 8) + i, each)
            out[piece, 8 * at : 8 * at + 8] = v[8 * i : 8 * i + 8]

    total = 0.0
    for c in range(2):
        for f in range(FIELDS):
            total += pack[c, f, SENS] * (mine[c, f] * other[c, f])
    store(0, 0, inside[0, 0] - jnp.where(me == 0, 0.0, total))
    store(0, 1, inside[0, 1] + jnp.where(me == 0, total, 0.0))
    for k in range(1, 3):
        for x in range(2):
            store(k, x, inside[k, x])
    for tile in range(6 * ny // 8, out.shape[0] * each):
        piece, at = divmod(tile, each)
        out[piece, 8 * at : 8 * at + 8] = jnp.zeros((8, out.shape[2]), F32)


def sum_kernel(scale, pieces, out):
    total = pieces[0]
    for i in range(1, pieces.shape[0]):
        total = total + pieces[i]
    total = total * scale
    for i in range(out.shape[0]):
        out[i] = total


def body(
    adjoint_source,
    adjoint_start,
    spectral_radius,
    coupling,
    left_vectors,
    right_vectors,
    implicit_scales,
    sensitivity_map,
    condition_weights,
):
    peers = lax.axis_size("grid")
    conds = lax.axis_size("cond")
    _, fields, planes, ny, nz = adjoint_start.shape
    nx = peers * planes
    rows_b = nx * 8
    blocks = peers // 2
    sems = lambda n: pltpu.SemaphoreType.DMA((n,))

    me = lax.axis_index("grid")
    core = me % 2
    side = (me // 2) % 2
    place = (me // 4) * 2 + core
    info = jnp.stack([core, side, place > 0, place < blocks - 1]).astype(jnp.int32)

    cores = [(i, i ^ 1) for i in range(peers)]
    chips = [(i, i + 1) for i in range(1, peers - 1, 2)]
    chips = chips + [(j, i) for i, j in chips]
    other = lax.ppermute(adjoint_start, "grid", cores)
    outer = lax.dynamic_index_in_dim(adjoint_start, core, 2, keepdims=False)
    outer = lax.ppermute(outer, "grid", chips)

    sine_z, spec_z = sine_tables(nz)
    sine_y, spec_y = sine_tables(ny)
    sine_x, spec_x = sine_tables(nx)
    spec = np.zeros((8, nz), np.float32)
    spec[0], spec[1, :ny], spec[2, :nx] = spec_z, spec_y, spec_x
    left_x = np.repeat(sine_x, 8, axis=0)
    right_2 = np.repeat(sine_x, 2, axis=0).T.copy()
    spec, sine_z, sine_y = jnp.asarray(spec), jnp.asarray(sine_z), jnp.asarray(sine_y)

    weights = condition_weights.astype(F32)[:, None, None]
    pack = jnp.concatenate(
        [
            coupling,
            left_vectors,
            right_vectors,
            implicit_scales,
            jnp.swapaxes(sensitivity_map, 1, 2) * weights,
        ],
        axis=2,
    )

    solve_z, solve_y = call(
        tables_kernel,
        (shape(2, fields, nz, nz), shape(2, fields, ny, ny)),
        [SMEM, ANY, ANY, ANY],
        100_000_000,
        "solve_tables",
        [vmem(nz, nz), vmem(ny, ny), vmem(8, nz), sems(3)],
    )(pack, sine_z, sine_y, spec)

    lines, token = call(
        first_kernel,
        (shape(blocks // 2, 2, 2, 3 * fields + planes, 8, nz), shape(8, nz)),
        [SMEM, SMEM, VMEM, VMEM, ANY, VMEM, VMEM, VMEM],
        200_000_000,
        "first_residual",
        [
            vmem(2, fields, planes, ny, nz),
            vmem(blocks // 2, 2, 2, 3 * fields + planes, 8, nz),
            vmem(planes, fields, ny, nz),
            vmem(fields, 3 * ny, nz),
            sems(2),
            sems(2),
        ],
        (ANY, VMEM),
    )(info, pack, adjoint_start, other, adjoint_source, spectral_radius, solve_z, solve_y)

    lines = lines.reshape(peers, 3 * fields + planes, 8, nz)
    lines = lax.all_to_all(lines, "grid", 0, 0, tiled=True)

    solve_x, ends_prev, ends_next, halo_prev, halo_next, solve_zb, mixes = call(
        tables_b_kernel,
        (
            shape(fields, rows_b, rows_b),
            shape(fields, 2 * nx, rows_b),
            shape(fields, 2 * nx, rows_b),
            shape(fields, 2 * nx, 2 * nx),
            shape(fields, 2 * nx, 2 * nx),
            shape(fields, nz, nz),
            shape(3, fields, fields),
        ),
        [SMEM, SMEM, VMEM] + [ANY] * 5,
        100_000_000,
        "tables_b",
        [vmem(nz, nz), vmem(rows_b, nx), vmem(nx, rows_b), vmem(nx, 2 * nx), vmem(8, nz), sems(5)],
        (VMEM,) * 6 + (SMEM,),
    )(info, pack, token, sine_z, jnp.asarray(left_x), jnp.asarray(left_x.T.copy()), jnp.asarray(right_2), spec)

    to_prev, to_next = call(
        ends_kernel,
        (shape(fields, 2 * nx, nz), shape(fields, 2 * nx, nz)),
        [VMEM] * 3,
        50_000_000,
        "solve_ends",
    )(lines, ends_prev, ends_next)

    up = [(spot(s, b), spot(s, b + 1)) for s in range(2) for b in range(blocks - 1)]
    down = [(j, i) for i, j in up]
    from_prev = lax.ppermute(to_next, "grid", up)
    from_next = lax.ppermute(to_prev, "grid", down)

    local = call(
        second_kernel,
        shape(fields, nx, 8, nz),
        [SMEM, SMEM] + [VMEM] * 3,
        300_000_000,
        "second_residual",
        [vmem(fields, nx, 8, nz) for _ in range(3)],
    )(info, mixes, lines, solve_x, solve_zb)

    step, token = call(
        halo_kernel,
        (shape(peers, 3 * fields, 8, nz), shape(8, nz)),
        [SMEM] + [VMEM] * 6,
        50_000_000,
        "halo_rows",
        [vmem(peers, 3 * fields, 8, nz), sems(fields)],
        (ANY, VMEM),
    )(mixes, local, from_prev, from_next, halo_prev, halo_next, solve_zb)

    step = lax.all_to_all(step, "grid", 0, 0, tiled=True)

    solve_y = call(
        tables_y_kernel,
        shape(2, fields, ny, ny),
        [SMEM, VMEM, ANY, ANY],
        50_000_000,
        "tables_y",
        [vmem(ny, ny), vmem(8, nz), sems(2)],
    )(pack, token, sine_y, spec)

    adjoint, mine = call(
        update_kernel,
        (shape(2, fields, planes, ny, nz), shape(2, fields, ny, nz)),
        [SMEM, SMEM] + [VMEM] * 3,
        60_000_000,
        "update",
        [vmem(fields, ny, 2 * nz)],
    )(info, pack, adjoint_start, step, solve_y)

    other = lax.ppermute(mine, "grid", cores)

    inside = call(
        inside_kernel,
        shape(3, planes, ny, nz),
        [SMEM, SMEM] + [VMEM] * 4,
        60_000_000,
        "inside_terms",
        [vmem(fields, ny, nz)],
    )(info, pack, adjoint, outer, step, solve_y)

    tiles = 3 * planes * ny // 8
    each = -(-tiles // conds)
    pieces = call(
        terms_kernel,
        shape(conds, each * 8, nz),
        [SMEM, SMEM] + [VMEM] * 3,
        10_000_000,
        "terms",
    )(info, pack, mine, other, inside)
    pieces = lax.all_to_all(pieces, "cond", 0, 0, tiled=True)
    scale = 1.0 / (conds * condition_weights.shape[0])
    pieces = call(
        functools.partial(sum_kernel, scale),
        shape(conds, each * 8, nz),
        [VMEM],
        1_000_000,
        "sum_conditions",
    )(pieces)
    pieces = lax.all_to_all(pieces, "cond", 0, 0, tiled=True)
    total = pieces.reshape(conds * each * 8, nz)[: tiles * 8].reshape(3, planes, ny, nz)
    return (adjoint, total)


def solution(mesh):
    in_specs = (
        P("cond", None, "grid", None, None),
        P("cond", None, "grid", None, None),
        P("grid", None, None),
        P("cond", None, None),
        P("cond", None, None),
        P("cond", None, None),
        P("cond", None, None),
        P("cond", None, None),
        P("cond"),
    )
    out_specs = (P("cond", None, "grid", None, None), P(None, "grid", None, None))
    return jax.shard_map(body, mesh=mesh, in_specs=in_specs, out_specs=out_specs, check_vma=False)
```

```python
import functools
import math

import jax
import jax.numpy as jnp
import numpy as np
from jax import lax
from jax.experimental import pallas as pl
from jax.experimental.pallas import tpu as pltpu
from jax.sharding import PartitionSpec as P

F32 = jnp.float32
FIELDS = 5
VMEM = pl.BlockSpec(memory_space=pltpu.VMEM)
SMEM = pl.BlockSpec(memory_space=pltpu.SMEM)
LIMIT = 20 * 1024 * 1024
ANY = pl.BlockSpec(memory_space=pl.ANY)
COUP, LEFT, RIGHT, RATE, SENS = 0, 5, 10, 15, 18


def split(v):
    high = v.astype(jnp.bfloat16)
    return high, (v - high.astype(F32)).astype(jnp.bfloat16)


def dot(a, b):
    one = functools.partial(jnp.dot, preferred_element_type=F32)
    (a_high, a_low), (b_high, b_low) = split(a), split(b)
    return one(a_high, b_high) + (one(a_high, b_low) + one(a_low, b_high))


def exact(a, b):
    return jnp.dot(a, b, precision=lax.Precision.HIGHEST, preferred_element_type=F32)


def sine_tables(length):
    counter = np.arange(1, length + 1, dtype=np.float64)
    sine = math.sqrt(2.0 / (length + 1)) * np.sin(
        counter[:, None] * counter[None, :] * (math.pi / (length + 1))
    )
    spectrum = 2.0 - 2.0 * np.cos(counter * (math.pi / (length + 1)))
    return sine.astype(np.float32), (spectrum + spectrum * spectrum).astype(np.float32)


def call(kernel, outs, in_specs, flops, name, scratch=(), out_specs=None):
    return pl.pallas_call(
        kernel,
        out_shape=outs,
        in_specs=in_specs,
        out_specs=out_specs or jax.tree.map(lambda _: VMEM, outs),
        scratch_shapes=list(scratch),
        compiler_params=pltpu.CompilerParams(vmem_limit_bytes=LIMIT),
        cost_estimate=pl.CostEstimate(flops=flops, bytes_accessed=4_000_000, transcendentals=0),
        name=name,
    )


def shape(*dims):
    return jax.ShapeDtypeStruct(dims, F32)


def vmem(*dims):
    return pltpu.VMEM(dims, F32)


def fetch(sources, targets, sems):
    copies = [pltpu.make_async_copy(a, b, sems.at[i]) for i, (a, b) in enumerate(zip(sources, targets))]
    for copy in copies:
        copy.start()
    return copies


def shifted(v, axis, step):
    size = v.shape[axis]
    rolled = pltpu.roll(v, (-step) % size, axis)
    at = lax.broadcasted_iota(jnp.int32, v.shape, axis)
    return jnp.where(at == (size - 1 if step > 0 else 0), 0.0, rolled)


def mixed(weight, values):
    total = weight(0) * values[0]
    for g in range(1, FIELDS):
        total = total + weight(g) * values[g]
    return total


def spot(c, b):
    return (b // 2) * 4 + c * 2 + b % 2


def tables_kernel(pack, sine_z_in, sine_y_in, spec_in, solve_z, solve_y, sine_z, sine_y, spec, sems):
    for copy in fetch((sine_z_in, sine_y_in, spec_in), (sine_z, sine_y, spec), sems):
        copy.wait()
    ny = sine_y.shape[0]
    for c in range(2):
        for f in range(FIELDS):
            denom = 1.0 + pack[c, f, RATE + 2] * spec[0:1]
            solve_z[c, f] = exact(sine_z[...] / denom, sine_z[...])
            denom = 1.0 + pack[c, f, RATE + 1] * spec[1:2, :ny]
            solve_y[c, f] = exact(sine_y[...] / denom, sine_y[...])


def tables_y_kernel(pack, token, sine_y_in, spec_in, solve_y, sine_y, spec, sems):
    for copy in fetch((sine_y_in, spec_in), (sine_y, spec), sems):
        copy.wait()
    ny = sine_y.shape[0]
    for c in range(2):
        for f in range(FIELDS):
            denom = 1.0 + pack[c, f, RATE + 1] * spec[1:2, :ny]
            solve_y[c, f] = exact(sine_y[...] / denom, sine_y[...])


def tables_b_kernel(info, pack, token, sine_z_in, left_in, right_in, right_2_in, spec_in,
                    solve_x, ends_prev, ends_next, halo_prev, halo_next, solve_z, mixes,
                    sine_z, left, right, right_2, spec, sems):
    copies = fetch(
        (sine_z_in, left_in, right_in, right_2_in, spec_in), (sine_z, left, right, right_2, spec), sems
    )
    mine = info[1]
    for f in range(FIELDS):
        for g in range(FIELDS):
            near, far = 0.0, 0.0
            for h in range(FIELDS):
                near = near + pack[mine, f, LEFT + h] * pack[mine, h, RIGHT + g]
                inner = 0.0
                for i in range(FIELDS):
                    inner = inner + pack[mine, h, COUP + i] * pack[mine, i, RIGHT + g]
                far = far + pack[mine, f, LEFT + h] * inner
            mixes[0, f, g] = near
            mixes[1, f, g] = far
        mixes[2, f, 0] = pack[mine, f, RATE + 1]
    for copy in copies:
        copy.wait()
    n, nx = left.shape
    row, col = (lax.broadcasted_iota(jnp.int32, (n, n), i) for i in range(2))
    same = (row & 7) == (col & 7)
    row, col = (lax.broadcasted_iota(jnp.int32, (2 * nx, n), i) for i in range(2))
    prev_rows = (row & 1) == (col & 7)
    next_rows = (row & 1) + 6 == (col & 7)
    row, col = (lax.broadcasted_iota(jnp.int32, (2 * nx, 2 * nx), i) for i in range(2))
    from_last = ((row & 1) == 0) & ((col & 1) == 1)
    from_first = ((row & 1) == 1) & ((col & 1) == 0)
    for f in range(FIELDS):
        denom = 1.0 + pack[mine, f, RATE] * spec[2:3, :nx]
        scaled = left[...] / denom
        solve_x[f] = jnp.where(same, exact(scaled, right[...]), 0.0)
        scaled_2 = right_2[...].T / denom
        both = exact(scaled_2, right[...])
        ends_prev[f] = jnp.where(prev_rows, both, 0.0)
        ends_next[f] = jnp.where(next_rows, both, 0.0)
        both = exact(scaled_2, right_2[...])
        halo_prev[f] = jnp.where(from_last, both, 0.0)
        halo_next[f] = jnp.where(from_first, both, 0.0)
        denom = 1.0 + pack[mine, f, RATE + 2] * spec[0:1]
        solve_z[f] = exact(sine_z[...] / denom, sine_z[...])


def planes_kernel(info, adjoint, outer, inner, sems):
    me = info[0]
    for copy in fetch((adjoint.at[:, :, me], adjoint.at[:, :, 1 - me]), (outer, inner), sems):
        copy.wait()


def local_kernel(info, pack, adjoint, inner, source_in, radius, solve_z, solve_y, made, source, lapped, stage, sems):
    copies = fetch([source_in.at[c] for c in range(2)], [source.at[c] for c in range(2)], sems)
    ny = adjoint.shape[3]
    blocks = ny // 8
    me = info[0]
    sides = (me.astype(F32), (1 - me).astype(F32))
    for c in range(2):
        for x in range(2):
            for f in range(FIELDS):
                v = adjoint[c, f, x]
                beside = adjoint[c, f, 1 - x] + inner[c, f] * sides[x]
                beside = beside + shifted(v, 0, 1) + shifted(v, 0, -1)
                beside = beside + shifted(v, 1, 1) + shifted(v, 1, -1)
                lapped[x, f] = 6.0 * v - beside
        copies[c].wait()
        for x in range(2):
            sr = radius[x]
            residual = []
            for f in range(FIELDS):
                r = source[c, f, x] - sr * adjoint[c, f, x]
                for g in range(FIELDS):
                    r = r - pack[c, f, COUP + g] * lapped[x, g]
                residual.append(r)
            for f in range(FIELDS):
                stage[f, x * ny : x * ny + ny] = mixed(lambda g: pack[c, f, LEFT + g], residual)
        for f in range(FIELDS):
            r = dot(stage[f], solve_z[c, f])
            r = jnp.concatenate([r[x * ny : x * ny + ny] for x in range(2)], axis=1)
            r = dot(solve_y[c, f], r)
            for x in range(2):
                for b in range(blocks):
                    made[b // 2, c, b % 2, 2 * f + x] = r[8 * b : 8 * b + 8, 128 * x : 128 * x + 128]
        for x in range(2):
            for b in range(blocks):
                made[b // 2, c, b % 2, 2 * FIELDS + x] = radius[x, 8 * b : 8 * b + 8]


def outer_kernel(info, pack, local, outer, solve_z, solve_y, out, token, made, stage, sems):
    ny = outer.shape[2]
    me = info[0]
    token[...] = jnp.zeros(token.shape, F32)
    stores = []
    for c in range(2):
        made[:, c] = local[:, c]
        parts = [mixed(lambda g: pack[c, f, COUP + g], [outer[c, g] for g in range(FIELDS)]) for f in range(FIELDS)]
        for f in range(FIELDS):
            r = mixed(lambda g: pack[c, f, LEFT + g], parts)
            stage[f] = dot(solve_y[c, f], dot(r, solve_z[c, f]))
        for f in range(FIELDS):
            for b in range(ny // 8):
                made[b // 2, c, b % 2, 2 * f + me] += stage[f, 8 * b : 8 * b + 8]
        stores.append(pltpu.make_async_copy(made.at[:, c], out.at[:, c], sems.at[c]))
        stores[-1].start()
    for copy in stores:
        copy.wait()


def ends_kernel(lines, ends_prev, ends_next, to_prev, to_next):
    for f in range(FIELDS):
        w = lines[:, 2 * f : 2 * f + 2].reshape(-1, 128)
        to_prev[f] = dot(ends_prev[f], w)
        to_next[f] = dot(ends_next[f], w)


def second_kernel(info, mixes, lines, solve_x, solve_z, out, solved, lapped, kept):
    nx = out.shape[1]
    full = (nx, 8, 128)
    row = lax.broadcasted_iota(jnp.int32, full, 1)
    has_prev, has_next = info[2].astype(F32), info[3].astype(F32)
    zero = jnp.zeros((1, 8, 128), F32)
    for f in range(FIELDS):
        u = dot(solve_x[f], lines[:, 2 * f : 2 * f + 2].reshape(nx * 8, 128)).reshape(full)
        solved[f] = u
        up = jnp.where(row == 7, 0.0, pltpu.roll(u, 7, 1))
        down = jnp.where(row == 0, 0.0, pltpu.roll(u, 1, 1))
        ku = 2.0 * u - up - down
        k_up = jnp.where(row == 7, -has_next * u, pltpu.roll(ku, 7, 1))
        k_down = jnp.where(row == 0, -has_prev * u, pltpu.roll(ku, 1, 1))
        kku = 2.0 * ku - k_up - k_down
        kept[f] = 2.0 * (u + mixes[2, f, 0] * (ku + kku))
        beside = jnp.concatenate([zero, u[:-1]], axis=0) + jnp.concatenate([u[1:], zero], axis=0)
        flat = u.reshape(nx * 8, 128)
        beside = beside + (shifted(flat, 1, 1) + shifted(flat, 1, -1)).reshape(full)
        lapped[f] = 4.0 * u + ku - beside
    sr = lines[:, 2 * FIELDS :].reshape(full)
    for f in range(FIELDS):
        near = mixed(lambda g: mixes[0, f, g], solved)
        far = mixed(lambda g: mixes[1, f, g], lapped)
        v = (sr * near + far).reshape(nx * 8, 128)
        v = dot(solve_x[f], dot(v, solve_z[f]))
        out[f] = kept[f] - v.reshape(full)


def halo_kernel(mixes, local, from_prev, from_next, halo_prev, halo_next, solve_z, out, token, made, sems):
    nx = local.shape[1]
    full = (nx, 8, 128)
    row = lax.broadcasted_iota(jnp.int32, full, 1)
    odd = (lax.broadcasted_iota(jnp.int32, (2 * nx, 128), 0) & 1) == 1
    zero = jnp.zeros((1, 8, 128), F32)
    token[...] = jnp.zeros(token.shape, F32)
    stores = []
    for f in range(FIELDS):
        first, last = from_prev[f], from_next[f]
        far = jnp.concatenate(
            [mixed(lambda g: mixes[1, f, g], from_prev), mixed(lambda g: mixes[1, f, g], from_next)], axis=0
        )
        far = dot(far, solve_z[f])
        far_prev, far_next = far[: 2 * nx], far[2 * nx :]
        scale = 2.0 * mixes[2, f, 0]
        add_prev = jnp.where(odd, first, first - 5.0 * pltpu.roll(first, 2 * nx - 1, 0))
        add_next = jnp.where(odd, last - 5.0 * pltpu.roll(last, 1, 0), last)
        add_prev = scale * add_prev + dot(halo_prev[f], far_prev)
        add_next = scale * add_next + dot(halo_next[f], far_next)
        spread = lambda v, at: jnp.stack(
            [pltpu.roll(v.reshape(nx // 4, 8, 128), (at - 2 * j) % 8, 1) for j in range(4)], axis=1
        ).reshape(full)
        q = local[f] + jnp.where(
            row < 2, spread(add_prev, 0), jnp.where(row >= 6, spread(add_next, 6), 0.0)
        )
        chips = q.reshape(nx // 4, 4, 8, 128)
        outer_0 = jnp.concatenate([zero, chips[:-1, 3]], axis=0)
        outer_1 = jnp.concatenate([chips[1:, 0], zero], axis=0)
        made[:, 3 * f : 3 * f + 3] = jnp.stack(
            [chips[:, 0], chips[:, 1], outer_0, chips[:, 2], chips[:, 3], outer_1], axis=1
        ).reshape(nx // 2, 3, 8, 128)
        part = pl.ds(3 * f, 3)
        stores.append(pltpu.make_async_copy(made.at[:, part], out.at[:, part], sems.at[f]))
        stores[-1].start()
    for copy in stores:
        copy.wait()


def gathered(solved, c, tile, blocks):
    return jnp.concatenate([solved[spot(c, b), tile] for b in range(blocks)], axis=0)


def update_kernel(info, pack, adjoint, solved, solve_y, out, inner, step):
    ny = adjoint.shape[3]
    me = info[0]
    for c in range(2):
        for f in range(FIELDS):
            q = jnp.concatenate([gathered(solved, c, 3 * f + x, ny // 8) for x in range(2)], axis=1)
            step[f] = dot(solve_y[c, f], q)
        steps = [[step[g, :, 128 * x : 128 * x + 128] for g in range(FIELDS)] for x in range(2)]
        for f in range(FIELDS):
            planes = [
                adjoint[c, f, x] + mixed(lambda g: pack[c, f, RIGHT + g], steps[x]) for x in range(2)
            ]
            for x in range(2):
                out[c, f, x] = planes[x]
            inner[c, f] = jnp.where(me == 0, planes[1], planes[0])


def inside_kernel(info, pack, adjoint, start_outer, solved, solve_y, terms, step):
    ny = adjoint.shape[3]
    me = info[0]
    totals = [[0.0, 0.0] for _ in range(3)]
    for c in range(2):
        for f in range(FIELDS):
            step[f] = dot(solve_y[c, f], gathered(solved, c, 3 * f + 2, ny // 8))
        for f in range(FIELDS):
            outer = start_outer[c, f] + mixed(lambda g: pack[c, f, RIGHT + g], step)
            w = [pack[c, f, SENS + k] for k in range(3)]
            v = [adjoint[c, f, x] for x in range(2)]
            pair = v[0] * v[1]
            edge = jnp.where(me == 0, v[0], v[1]) * outer
            at_0, at_1 = jnp.where(me == 0, edge, 0.0), jnp.where(me == 0, 0.0, edge)
            totals[0][0] += w[0] * (pair - at_0)
            totals[0][1] += w[0] * (at_1 - pair)
            for x in range(2):
                for k in range(2):
                    totals[k + 1][x] += w[k + 1] * (v[x] * (shifted(v[x], k, 1) - shifted(v[x], k, -1)))
    for k in range(3):
        for x in range(2):
            terms[k, x] = totals[k][x]


def terms_kernel(info, pack, mine, other, inside, out):
    me = info[0]
    ny = mine.shape[2]
    each = out.shape[1] // 8

    def store(k, x, v):
        for i in range(ny // 8):
            piece, at = divmod((k * 2 + x) * (ny // 8) + i, each)
            out[piece, 8 * at : 8 * at + 8] = v[8 * i : 8 * i + 8]

    total = 0.0
    for c in range(2):
        for f in range(FIELDS):
            total += pack[c, f, SENS] * (mine[c, f] * other[c, f])
    store(0, 0, inside[0, 0] - jnp.where(me == 0, 0.0, total))
    store(0, 1, inside[0, 1] + jnp.where(me == 0, total, 0.0))
    for k in range(1, 3):
        for x in range(2):
            store(k, x, inside[k, x])
    for tile in range(6 * ny // 8, out.shape[0] * each):
        piece, at = divmod(tile, each)
        out[piece, 8 * at : 8 * at + 8] = jnp.zeros((8, out.shape[2]), F32)


def sum_kernel(scale, pieces, out):
    total = pieces[0]
    for i in range(1, pieces.shape[0]):
        total = total + pieces[i]
    total = total * scale
    for i in range(out.shape[0]):
        out[i] = total


def body(
    adjoint_source,
    adjoint_start,
    spectral_radius,
    coupling,
    left_vectors,
    right_vectors,
    implicit_scales,
    sensitivity_map,
    condition_weights,
):
    peers = lax.axis_size("grid")
    conds = lax.axis_size("cond")
    _, fields, planes, ny, nz = adjoint_start.shape
    nx = peers * planes
    rows_b = nx * 8
    blocks = peers // 2
    sems = lambda n: pltpu.SemaphoreType.DMA((n,))

    me = lax.axis_index("grid")
    core = me % 2
    side = (me // 2) % 2
    place = (me // 4) * 2 + core
    info = jnp.stack([core, side, place > 0, place < blocks - 1]).astype(jnp.int32)

    cores = [(i, i ^ 1) for i in range(peers)]
    chips = [(i, i + 1) for i in range(1, peers - 1, 2)]
    chips = chips + [(j, i) for i, j in chips]
    outer, inner = call(
        planes_kernel,
        (shape(2, fields, ny, nz), shape(2, fields, ny, nz)),
        [SMEM, ANY],
        1000,
        "planes",
        [sems(2)],
        (ANY, ANY),
    )(info, adjoint_start)
    outer = lax.ppermute(outer, "grid", chips)
    inner = lax.ppermute(inner, "grid", cores)

    sine_z, spec_z = sine_tables(nz)
    sine_y, spec_y = sine_tables(ny)
    sine_x, spec_x = sine_tables(nx)
    spec = np.zeros((8, nz), np.float32)
    spec[0], spec[1, :ny], spec[2, :nx] = spec_z, spec_y, spec_x
    left_x = np.repeat(sine_x, 8, axis=0)
    right_2 = np.repeat(sine_x, 2, axis=0).T.copy()
    spec, sine_z, sine_y = jnp.asarray(spec), jnp.asarray(sine_z), jnp.asarray(sine_y)

    weights = condition_weights.astype(F32)[:, None, None]
    pack = jnp.concatenate(
        [
            coupling,
            left_vectors,
            right_vectors,
            implicit_scales,
            jnp.swapaxes(sensitivity_map, 1, 2) * weights,
        ],
        axis=2,
    )

    solve_z, solve_y = call(
        tables_kernel,
        (shape(2, fields, nz, nz), shape(2, fields, ny, ny)),
        [SMEM, ANY, ANY, ANY],
        100_000_000,
        "solve_tables",
        [vmem(nz, nz), vmem(ny, ny), vmem(8, nz), sems(3)],
    )(pack, sine_z, sine_y, spec)

    tiles = 2 * fields + planes
    local = call(
        local_kernel,
        shape(blocks // 2, 2, 2, tiles, 8, nz),
        [SMEM, SMEM, VMEM, VMEM, ANY, VMEM, VMEM, VMEM],
        200_000_000,
        "first_residual",
        [
            vmem(2, fields, planes, ny, nz),
            vmem(planes, fields, ny, nz),
            vmem(fields, 2 * ny, nz),
            sems(2),
        ],
    )(info, pack, adjoint_start, inner, adjoint_source, spectral_radius, solve_z, solve_y)

    lines, token = call(
        outer_kernel,
        (shape(blocks // 2, 2, 2, tiles, 8, nz), shape(8, nz)),
        [SMEM, SMEM] + [VMEM] * 4,
        50_000_000,
        "outer_plane",
        [vmem(blocks // 2, 2, 2, tiles, 8, nz), vmem(fields, ny, nz), sems(2)],
        (ANY, VMEM),
    )(info, pack, local, outer, solve_z, solve_y)

    lines = lines.reshape(peers, tiles, 8, nz)
    lines = lax.all_to_all(lines, "grid", 0, 0, tiled=True)

    solve_x, ends_prev, ends_next, halo_prev, halo_next, solve_zb, mixes = call(
        tables_b_kernel,
        (
            shape(fields, rows_b, rows_b),
            shape(fields, 2 * nx, rows_b),
            shape(fields, 2 * nx, rows_b),
            shape(fields, 2 * nx, 2 * nx),
            shape(fields, 2 * nx, 2 * nx),
            shape(fields, nz, nz),
            shape(3, fields, fields),
        ),
        [SMEM, SMEM, VMEM] + [ANY] * 5,
        100_000_000,
        "tables_b",
        [vmem(nz, nz), vmem(rows_b, nx), vmem(nx, rows_b), vmem(nx, 2 * nx), vmem(8, nz), sems(5)],
        (VMEM,) * 6 + (SMEM,),
    )(info, pack, token, sine_z, jnp.asarray(left_x), jnp.asarray(left_x.T.copy()), jnp.asarray(right_2), spec)

    to_prev, to_next = call(
        ends_kernel,
        (shape(fields, 2 * nx, nz), shape(fields, 2 * nx, nz)),
        [VMEM] * 3,
        50_000_000,
        "solve_ends",
    )(lines, ends_prev, ends_next)

    up = [(spot(s, b), spot(s, b + 1)) for s in range(2) for b in range(blocks - 1)]
    down = [(j, i) for i, j in up]
    from_prev = lax.ppermute(to_next, "grid", up)
    from_next = lax.ppermute(to_prev, "grid", down)

    local = call(
        second_kernel,
        shape(fields, nx, 8, nz),
        [SMEM, SMEM] + [VMEM] * 3,
        300_000_000,
        "second_residual",
        [vmem(fields, nx, 8, nz) for _ in range(3)],
    )(info, mixes, lines, solve_x, solve_zb)

    step, token = call(
        halo_kernel,
        (shape(peers, 3 * fields, 8, nz), shape(8, nz)),
        [SMEM] + [VMEM] * 6,
        50_000_000,
        "halo_rows",
        [vmem(peers, 3 * fields, 8, nz), sems(fields)],
        (ANY, VMEM),
    )(mixes, local, from_prev, from_next, halo_prev, halo_next, solve_zb)

    step = lax.all_to_all(step, "grid", 0, 0, tiled=True)

    solve_y = call(
        tables_y_kernel,
        shape(2, fields, ny, ny),
        [SMEM, VMEM, ANY, ANY],
        50_000_000,
        "tables_y",
        [vmem(ny, ny), vmem(8, nz), sems(2)],
    )(pack, token, sine_y, spec)

    adjoint, mine = call(
        update_kernel,
        (shape(2, fields, planes, ny, nz), shape(2, fields, ny, nz)),
        [SMEM, SMEM] + [VMEM] * 3,
        60_000_000,
        "update",
        [vmem(fields, ny, 2 * nz)],
    )(info, pack, adjoint_start, step, solve_y)

    other = lax.ppermute(mine, "grid", cores)

    inside = call(
        inside_kernel,
        shape(3, planes, ny, nz),
        [SMEM, SMEM] + [VMEM] * 4,
        60_000_000,
        "inside_terms",
        [vmem(fields, ny, nz)],
    )(info, pack, adjoint, outer, step, solve_y)

    tiles = 3 * planes * ny // 8
    each = -(-tiles // conds)
    pieces = call(
        terms_kernel,
        shape(conds, each * 8, nz),
        [SMEM, SMEM] + [VMEM] * 3,
        10_000_000,
        "terms",
    )(info, pack, mine, other, inside)
    pieces = lax.all_to_all(pieces, "cond", 0, 0, tiled=True)
    scale = 1.0 / (conds * condition_weights.shape[0])
    pieces = call(
        functools.partial(sum_kernel, scale),
        shape(conds, each * 8, nz),
        [VMEM],
        1_000_000,
        "sum_conditions",
    )(pieces)
    pieces = lax.all_to_all(pieces, "cond", 0, 0, tiled=True)
    total = pieces.reshape(conds * each * 8, nz)[: tiles * 8].reshape(3, planes, ny, nz)
    return (adjoint, total)


def solution(mesh):
    in_specs = (
        P("cond", None, "grid", None, None),
        P("cond", None, "grid", None, None),
        P("grid", None, None),
        P("cond", None, None),
        P("cond", None, None),
        P("cond", None, None),
        P("cond", None, None),
        P("cond", None, None),
        P("cond"),
    )
    out_specs = (P("cond", None, "grid", None, None), P(None, "grid", None, None))
    return jax.shard_map(body, mesh=mesh, in_specs=in_specs, out_specs=out_specs, check_vma=False)
```

```python
import functools
import math

import jax
import jax.numpy as jnp
from jax import lax
from jax.experimental import pallas as pl
from jax.experimental.pallas import tpu as pltpu
from jax.sharding import PartitionSpec as P

F32 = jnp.float32
FIELDS = 5
VMEM = pl.BlockSpec(memory_space=pltpu.VMEM)
SMEM = pl.BlockSpec(memory_space=pltpu.SMEM)
LIMIT = 20 * 1024 * 1024
ANY = pl.BlockSpec(memory_space=pl.ANY)
HBM = pl.BlockSpec(memory_space=pltpu.HBM)
COUP, LEFT, RIGHT, RATE, SENS = 0, 5, 10, 15, 18


def split(v):
    high = v.astype(jnp.bfloat16)
    return high, (v - high.astype(F32)).astype(jnp.bfloat16)


def dot(a, b):
    one = functools.partial(jnp.dot, preferred_element_type=F32)
    (a_high, a_low), (b_high, b_low) = split(a), split(b)
    return one(a_high, b_high) + (one(a_high, b_low) + one(a_low, b_high))


def exact(a, b):
    return jnp.dot(a, b, precision=lax.Precision.HIGHEST, preferred_element_type=F32)


def counters(length, repeat):
    return lax.broadcasted_iota(jnp.int32, (length * repeat,), 0) // repeat + 1


def sine_table(length, repeat_rows=1, repeat_columns=1):
    product = counters(length, repeat_rows)[:, None] * counters(length, repeat_columns)[None, :]
    product = product % (2 * (length + 1))
    return math.sqrt(2.0 / (length + 1)) * jnp.sin(product.astype(F32) * (math.pi / (length + 1)))


def spectrum(length):
    half = jnp.sin(counters(length, 1).astype(F32) * (math.pi / (2 * (length + 1))))
    lam = 4.0 * half * half
    return (lam + lam * lam)[None, :]


def call(kernel, outs, in_specs, flops, name, scratch=(), out_specs=None):
    return pl.pallas_call(
        kernel,
        out_shape=outs,
        in_specs=in_specs,
        out_specs=out_specs or jax.tree.map(lambda _: VMEM, outs),
        scratch_shapes=list(scratch),
        compiler_params=pltpu.CompilerParams(vmem_limit_bytes=LIMIT),
        cost_estimate=pl.CostEstimate(flops=flops, bytes_accessed=4_000_000, transcendentals=0),
        name=name,
    )


def shape(*dims):
    return jax.ShapeDtypeStruct(dims, F32)


def vmem(*dims):
    return pltpu.VMEM(dims, F32)


def fetch(sources, targets, sems):
    copies = [pltpu.make_async_copy(a, b, sems.at[i]) for i, (a, b) in enumerate(zip(sources, targets))]
    for copy in copies:
        copy.start()
    return copies


def shifted(v, axis, step):
    size = v.shape[axis]
    rolled = pltpu.roll(v, (-step) % size, axis)
    at = lax.broadcasted_iota(jnp.int32, v.shape, axis)
    return jnp.where(at == (size - 1 if step > 0 else 0), 0.0, rolled)


def mixed(weight, values):
    total = weight(0) * values[0]
    for g in range(1, FIELDS):
        total = total + weight(g) * values[g]
    return total


def spot(c, b):
    return (b // 2) * 4 + c * 2 + b % 2


def tables_kernel(pack, sine_z, spec_z, sine_y, spec_y, solve_z, solve_y):
    for c in range(2):
        for f in range(FIELDS):
            denom = 1.0 + pack[c, f, RATE + 2] * spec_z[...]
            solve_z[c, f] = exact(sine_z[...] / denom, sine_z[...])
            denom = 1.0 + pack[c, f, RATE + 1] * spec_y[...]
            solve_y[c, f] = exact(sine_y[...] / denom, sine_y[...])


def tables_y_kernel(pack, token, sine_y, spec_y, solve_y):
    for c in range(2):
        for f in range(FIELDS):
            denom = 1.0 + pack[c, f, RATE + 1] * spec_y[...]
            solve_y[c, f] = exact(sine_y[...] / denom, sine_y[...])


def tables_b_kernel(info, pack, token, outer, sine_z, spec_z, left, right, left_2, right_2, spec_x,
                    solve_x, ends_prev, ends_next, halo_prev, halo_next, solve_z, mixes):
    mine = info[1]
    for f in range(FIELDS):
        for g in range(FIELDS):
            near, far = 0.0, 0.0
            for h in range(FIELDS):
                near = near + pack[mine, f, LEFT + h] * pack[mine, h, RIGHT + g]
                inner = 0.0
                for i in range(FIELDS):
                    inner = inner + pack[mine, h, COUP + i] * pack[mine, i, RIGHT + g]
                far = far + pack[mine, f, LEFT + h] * inner
            mixes[0, f, g] = near
            mixes[1, f, g] = far
        mixes[2, f, 0] = pack[mine, f, RATE + 1]
    n, nx = left.shape
    row, col = (lax.broadcasted_iota(jnp.int32, (n, n), i) for i in range(2))
    same = (row & 7) == (col & 7)
    row, col = (lax.broadcasted_iota(jnp.int32, (2 * nx, n), i) for i in range(2))
    prev_rows = (row & 1) == (col & 7)
    next_rows = (row & 1) + 6 == (col & 7)
    row, col = (lax.broadcasted_iota(jnp.int32, (2 * nx, 2 * nx), i) for i in range(2))
    from_last = ((row & 1) == 0) & ((col & 1) == 1)
    from_first = ((row & 1) == 1) & ((col & 1) == 0)
    for f in range(FIELDS):
        denom = 1.0 + pack[mine, f, RATE] * spec_x[...]
        scaled = left[...] / denom
        solve_x[f] = jnp.where(same, exact(scaled, right[...]), 0.0)
        scaled_2 = left_2[...] / denom
        both = exact(scaled_2, right[...])
        ends_prev[f] = jnp.where(prev_rows, both, 0.0)
        ends_next[f] = jnp.where(next_rows, both, 0.0)
        both = exact(scaled_2, right_2[...])
        halo_prev[f] = jnp.where(from_last, both, 0.0)
        halo_next[f] = jnp.where(from_first, both, 0.0)
        denom = 1.0 + pack[mine, f, RATE + 2] * spec_z[...]
        solve_z[f] = exact(sine_z[...] / denom, sine_z[...])


def planes_kernel(info, adjoint, outer, inner, sems):
    me = info[0]
    for copy in fetch((adjoint.at[:, :, me], adjoint.at[:, :, 1 - me]), (outer, inner), sems):
        copy.wait()


def first_kernel(info, pack, adjoint, other, source_in, radius, solve_z, solve_y, out, token,
                 source, made, lapped, stage, sems, out_sems):
    copies = fetch([source_in.at[c] for c in range(2)], [source.at[c] for c in range(2)], sems)
    ny = adjoint.shape[3]
    blocks = ny // 8
    me = info[0]
    before, after = me.astype(F32), (1 - me).astype(F32)
    token[...] = jnp.zeros(token.shape, F32)
    stores = []
    for c in range(2):
        residual = {}
        for x in range(2):
            for f in range(FIELDS):
                v = adjoint[c, f, x]
                beside = adjoint[c, f, 1 - x]
                beside = beside + other[c, f] * (before if x == 0 else after)
                beside = beside + shifted(v, 0, 1) + shifted(v, 0, -1)
                beside = beside + shifted(v, 1, 1) + shifted(v, 1, -1)
                lapped[x, f] = 6.0 * v - beside
        copies[c].wait()
        for x in range(2):
            sr = radius[x]
            residual = []
            for f in range(FIELDS):
                r = source[c, f, x] - sr * adjoint[c, f, x]
                for g in range(FIELDS):
                    r = r - pack[c, f, COUP + g] * lapped[x, g]
                residual.append(r)
            for f in range(FIELDS):
                stage[f, x * ny : x * ny + ny] = mixed(lambda g: pack[c, f, LEFT + g], residual)
        outer = [adjoint[c, g, me] for g in range(FIELDS)]
        outer = [mixed(lambda g: pack[c, f, COUP + g], outer) for f in range(FIELDS)]
        for f in range(FIELDS):
            stage[f, 2 * ny : 3 * ny] = mixed(lambda g: pack[c, f, LEFT + g], outer)
        for f in range(FIELDS):
            r = dot(stage[f], solve_z[c, f])
            r = jnp.concatenate([r[p * ny : p * ny + ny] for p in range(3)], axis=1)
            r = dot(solve_y[c, f], r)
            for p in range(3):
                for b in range(blocks):
                    made[b // 2, c, b % 2, 3 * f + p] = r[8 * b : 8 * b + 8, 128 * p : 128 * p + 128]
        for x in range(2):
            for b in range(blocks):
                made[b // 2, c, b % 2, 3 * FIELDS + x] = radius[x, 8 * b : 8 * b + 8]
        stores.append(pltpu.make_async_copy(made.at[:, c], out.at[:, c], out_sems.at[c]))
        stores[-1].start()
    for copy in stores:
        copy.wait()


def assembled(lines, f):
    zero = jnp.zeros((1, 8, 128), F32)
    w = lines[:, 3 * f : 3 * f + 3].reshape(lines.shape[0] // 2, 6, 8, 128)
    plane_0 = w[:, 0] + jnp.concatenate([zero, w[:-1, 5]], axis=0)
    plane_3 = w[:, 4] + jnp.concatenate([w[1:, 2], zero], axis=0)
    return jnp.stack([plane_0, w[:, 1], w[:, 3], plane_3], axis=1)


def ends_kernel(lines, ends_prev, ends_next, to_prev, to_next):
    for f in range(FIELDS):
        w = assembled(lines, f).reshape(-1, 128)
        to_prev[f] = dot(ends_prev[f], w)
        to_next[f] = dot(ends_next[f], w)


def second_kernel(info, mixes, lines, solve_x, solve_z, out, solved, lapped, kept):
    nx = out.shape[1]
    full = (nx, 8, 128)
    row = lax.broadcasted_iota(jnp.int32, full, 1)
    has_prev, has_next = info[2].astype(F32), info[3].astype(F32)
    zero = jnp.zeros((1, 8, 128), F32)
    for f in range(FIELDS):
        u = dot(solve_x[f], assembled(lines, f).reshape(nx * 8, 128)).reshape(full)
        solved[f] = u
        up = jnp.where(row == 7, 0.0, pltpu.roll(u, 7, 1))
        down = jnp.where(row == 0, 0.0, pltpu.roll(u, 1, 1))
        ku = 2.0 * u - up - down
        k_up = jnp.where(row == 7, -has_next * u, pltpu.roll(ku, 7, 1))
        k_down = jnp.where(row == 0, -has_prev * u, pltpu.roll(ku, 1, 1))
        kku = 2.0 * ku - k_up - k_down
        kept[f] = 2.0 * (u + mixes[2, f, 0] * (ku + kku))
        beside = jnp.concatenate([zero, u[:-1]], axis=0) + jnp.concatenate([u[1:], zero], axis=0)
        flat = u.reshape(nx * 8, 128)
        beside = beside + (shifted(flat, 1, 1) + shifted(flat, 1, -1)).reshape(full)
        lapped[f] = 4.0 * u + ku - beside
    sr = lines[:, 3 * FIELDS :].reshape(full)
    for f in range(FIELDS):
        near = mixed(lambda g: mixes[0, f, g], solved)
        far = mixed(lambda g: mixes[1, f, g], lapped)
        v = (sr * near + far).reshape(nx * 8, 128)
        v = dot(solve_x[f], dot(v, solve_z[f]))
        out[f] = kept[f] - v.reshape(full)


def halo_kernel(mixes, local, from_prev, from_next, halo_prev, halo_next, solve_z, out, token, made, sems):
    nx = local.shape[1]
    full = (nx, 8, 128)
    row = lax.broadcasted_iota(jnp.int32, full, 1)
    odd = (lax.broadcasted_iota(jnp.int32, (2 * nx, 128), 0) & 1) == 1
    zero = jnp.zeros((1, 8, 128), F32)
    token[...] = jnp.zeros(token.shape, F32)
    stores = []
    for f in range(FIELDS):
        first, last = from_prev[f], from_next[f]
        far = jnp.concatenate(
            [mixed(lambda g: mixes[1, f, g], from_prev), mixed(lambda g: mixes[1, f, g], from_next)], axis=0
        )
        far = dot(far, solve_z[f])
        far_prev, far_next = far[: 2 * nx], far[2 * nx :]
        scale = 2.0 * mixes[2, f, 0]
        add_prev = jnp.where(odd, first, first - 5.0 * pltpu.roll(first, 2 * nx - 1, 0))
        add_next = jnp.where(odd, last - 5.0 * pltpu.roll(last, 1, 0), last)
        add_prev = scale * add_prev + dot(halo_prev[f], far_prev)
        add_next = scale * add_next + dot(halo_next[f], far_next)
        spread = lambda v, at: jnp.stack(
            [pltpu.roll(v.reshape(nx // 4, 8, 128), (at - 2 * j) % 8, 1) for j in range(4)], axis=1
        ).reshape(full)
        q = local[f] + jnp.where(
            row < 2, spread(add_prev, 0), jnp.where(row >= 6, spread(add_next, 6), 0.0)
        )
        chips = q.reshape(nx // 4, 4, 8, 128)
        outer_0 = jnp.concatenate([zero, chips[:-1, 3]], axis=0)
        outer_1 = jnp.concatenate([chips[1:, 0], zero], axis=0)
        made[:, 3 * f : 3 * f + 3] = jnp.stack(
            [chips[:, 0], chips[:, 1], outer_0, chips[:, 2], chips[:, 3], outer_1], axis=1
        ).reshape(nx // 2, 3, 8, 128)
        part = pl.ds(3 * f, 3)
        stores.append(pltpu.make_async_copy(made.at[:, part], out.at[:, part], sems.at[f]))
        stores[-1].start()
    for copy in stores:
        copy.wait()


def gathered(solved, c, tile, blocks):
    return jnp.concatenate([solved[spot(c, b), tile] for b in range(blocks)], axis=0)


def update_kernel(info, pack, adjoint, solved, solve_y, out, inner, step):
    ny = adjoint.shape[3]
    me = info[0]
    for c in range(2):
        for f in range(FIELDS):
            q = jnp.concatenate([gathered(solved, c, 3 * f + x, ny // 8) for x in range(2)], axis=1)
            step[f] = dot(solve_y[c, f], q)
        steps = [[step[g, :, 128 * x : 128 * x + 128] for g in range(FIELDS)] for x in range(2)]
        for f in range(FIELDS):
            planes = [
                adjoint[c, f, x] + mixed(lambda g: pack[c, f, RIGHT + g], steps[x]) for x in range(2)
            ]
            for x in range(2):
                out[c, f, x] = planes[x]
            inner[c, f] = jnp.where(me == 0, planes[1], planes[0])


def inside_kernel(info, pack, adjoint, start_outer, solved, solve_y, terms, step):
    ny = adjoint.shape[3]
    me = info[0]
    totals = [[0.0, 0.0] for _ in range(3)]
    for c in range(2):
        for f in range(FIELDS):
            step[f] = dot(solve_y[c, f], gathered(solved, c, 3 * f + 2, ny // 8))
        for f in range(FIELDS):
            outer = start_outer[c, f] + mixed(lambda g: pack[c, f, RIGHT + g], step)
            w = [pack[c, f, SENS + k] for k in range(3)]
            v = [adjoint[c, f, x] for x in range(2)]
            pair = v[0] * v[1]
            edge = jnp.where(me == 0, v[0], v[1]) * outer
            at_0, at_1 = jnp.where(me == 0, edge, 0.0), jnp.where(me == 0, 0.0, edge)
            totals[0][0] += w[0] * (pair - at_0)
            totals[0][1] += w[0] * (at_1 - pair)
            for x in range(2):
                for k in range(2):
                    totals[k + 1][x] += w[k + 1] * (v[x] * (shifted(v[x], k, 1) - shifted(v[x], k, -1)))
    for k in range(3):
        for x in range(2):
            terms[k, x] = totals[k][x]


def terms_kernel(info, pack, mine, other, inside, out):
    me = info[0]
    ny = mine.shape[2]
    each = out.shape[1]

    def store(k, x, v):
        for i in range(ny // 4):
            piece, at = divmod((k * 2 + x) * (ny // 4) + i, each)
            out[piece, at] = v[4 * i : 4 * i + 4]

    total = 0.0
    for c in range(2):
        for f in range(FIELDS):
            total += pack[c, f, SENS] * (mine[c, f] * other[c, f])
    store(0, 0, inside[0, 0] - jnp.where(me == 0, 0.0, total))
    store(0, 1, inside[0, 1] + jnp.where(me == 0, total, 0.0))
    for k in range(1, 3):
        for x in range(2):
            store(k, x, inside[k, x])
    for i in range(6 * ny // 4, out.shape[0] * each):
        piece, at = divmod(i, each)
        out[piece, at] = jnp.zeros(out.shape[2:], F32)


def sum_kernel(scale, pieces, out):
    total = pieces[0]
    for i in range(1, pieces.shape[0]):
        total = total + pieces[i]
    total = total * scale
    for i in range(out.shape[0]):
        out[i] = total


def body(
    adjoint_source,
    adjoint_start,
    spectral_radius,
    coupling,
    left_vectors,
    right_vectors,
    implicit_scales,
    sensitivity_map,
    condition_weights,
):
    peers = lax.axis_size("grid")
    conds = lax.axis_size("cond")
    _, fields, planes, ny, nz = adjoint_start.shape
    nx = peers * planes
    rows_b = nx * 8
    blocks = peers // 2
    sems = lambda n: pltpu.SemaphoreType.DMA((n,))

    me = lax.axis_index("grid")
    core = me % 2
    side = (me // 2) % 2
    place = (me // 4) * 2 + core
    info = jnp.stack([core, side, place > 0, place < blocks - 1]).astype(jnp.int32)

    cores = [(i, i ^ 1) for i in range(peers)]
    chips = [(i, i + 1) for i in range(1, peers - 1, 2)]
    chips = chips + [(j, i) for i, j in chips]
    outer, other = call(
        planes_kernel,
        (shape(2, fields, ny, nz), shape(2, fields, ny, nz)),
        [SMEM, ANY],
        1000,
        "planes",
        [sems(2)],
        (ANY, ANY),
    )(info, adjoint_start)
    other = lax.ppermute(other, "grid", cores)
    outer = lax.ppermute(outer, "grid", chips)

    sine_z, spec_z = sine_table(nz), spectrum(nz)
    sine_y, spec_y = sine_table(ny), spectrum(ny)

    weights = condition_weights.astype(F32)[:, None, None]
    pack = jnp.zeros((2, fields, 24), F32)
    for at, part in (
        (COUP, coupling),
        (LEFT, left_vectors),
        (RIGHT, right_vectors),
        (RATE, implicit_scales),
        (SENS, jnp.swapaxes(sensitivity_map, 1, 2) * weights),
    ):
        pack = pack + jnp.pad(part, ((0, 0), (0, 0), (at, 24 - at - part.shape[2])))

    solve_z, solve_y = call(
        tables_kernel,
        (shape(2, fields, nz, nz), shape(2, fields, ny, ny)),
        [SMEM] + [VMEM] * 4,
        100_000_000,
        "solve_tables",
    )(pack, sine_z, spec_z, sine_y, spec_y)

    lines, token = call(
        first_kernel,
        (shape(blocks // 2, 2, 2, 3 * fields + planes, 8, nz), shape(8, nz)),
        [SMEM, SMEM, VMEM, VMEM, HBM, VMEM, VMEM, VMEM],
        200_000_000,
        "first_residual",
        [
            vmem(2, fields, planes, ny, nz),
            vmem(blocks // 2, 2, 2, 3 * fields + planes, 8, nz),
            vmem(planes, fields, ny, nz),
            vmem(fields, 3 * ny, nz),
            sems(2),
            sems(2),
        ],
        (ANY, VMEM),
    )(info, pack, adjoint_start, other, adjoint_source, spectral_radius, solve_z, solve_y)

    lines = lines.reshape(peers, 3 * fields + planes, 8, nz)
    lines = lax.all_to_all(lines, "grid", 0, 0, tiled=True)

    solve_x, ends_prev, ends_next, halo_prev, halo_next, solve_zb, mixes = call(
        tables_b_kernel,
        (
            shape(fields, rows_b, rows_b),
            shape(fields, 2 * nx, rows_b),
            shape(fields, 2 * nx, rows_b),
            shape(fields, 2 * nx, 2 * nx),
            shape(fields, 2 * nx, 2 * nx),
            shape(fields, nz, nz),
            shape(3, fields, fields),
        ),
        [SMEM, SMEM, VMEM, ANY] + [VMEM] * 7,
        100_000_000,
        "tables_b",
        (),
        (VMEM,) * 6 + (SMEM,),
    )(
        info, pack, token, outer, sine_z, spec_z,
        sine_table(nx, 8, 1), sine_table(nx, 1, 8), sine_table(nx, 2, 1), sine_table(nx, 1, 2), spectrum(nx),
    )

    to_prev, to_next = call(
        ends_kernel,
        (shape(fields, 2 * nx, nz), shape(fields, 2 * nx, nz)),
        [VMEM] * 3,
        50_000_000,
        "solve_ends",
    )(lines, ends_prev, ends_next)

    up = [(spot(s, b), spot(s, b + 1)) for s in range(2) for b in range(blocks - 1)]
    down = [(j, i) for i, j in up]
    from_prev = lax.ppermute(to_next, "grid", up)
    from_next = lax.ppermute(to_prev, "grid", down)

    local = call(
        second_kernel,
        shape(fields, nx, 8, nz),
        [SMEM, SMEM] + [VMEM] * 3,
        300_000_000,
        "second_residual",
        [vmem(fields, nx, 8, nz) for _ in range(3)],
    )(info, mixes, lines, solve_x, solve_zb)

    step, token = call(
        halo_kernel,
        (shape(peers, 3 * fields, 8, nz), shape(8, nz)),
        [SMEM] + [VMEM] * 6,
        50_000_000,
        "halo_rows",
        [vmem(peers, 3 * fields, 8, nz), sems(fields)],
        (ANY, VMEM),
    )(mixes, local, from_prev, from_next, halo_prev, halo_next, solve_zb)

    step = lax.all_to_all(step, "grid", 0, 0, tiled=True)

    solve_y = call(
        tables_y_kernel,
        shape(2, fields, ny, ny),
        [SMEM, VMEM, VMEM, VMEM],
        50_000_000,
        "tables_y",
    )(pack, token, sine_y, spec_y)

    adjoint, mine = call(
        update_kernel,
        (shape(2, fields, planes, ny, nz), shape(2, fields, ny, nz)),
        [SMEM, SMEM] + [VMEM] * 3,
        60_000_000,
        "update",
        [vmem(fields, ny, 2 * nz)],
    )(info, pack, adjoint_start, step, solve_y)

    other = lax.ppermute(mine, "grid", cores)

    inside = call(
        inside_kernel,
        shape(3, planes, ny, nz),
        [SMEM, SMEM] + [VMEM] * 4,
        60_000_000,
        "inside_terms",
        [vmem(fields, ny, nz)],
    )(info, pack, adjoint, outer, step, solve_y)

    tiles = 3 * planes * ny // 4
    each = -(-tiles // conds)
    pieces = call(
        terms_kernel,
        shape(conds, each, 4, nz),
        [SMEM, SMEM] + [VMEM] * 3,
        10_000_000,
        "terms",
    )(info, pack, mine, other, inside)
    pieces = lax.all_to_all(pieces, "cond", 0, 0, tiled=True)
    scale = 1.0 / (conds * condition_weights.shape[0])
    pieces = call(
        functools.partial(sum_kernel, scale),
        shape(conds, each, 4, nz),
        [VMEM],
        1_000_000,
        "sum_conditions",
    )(pieces)
    pieces = lax.all_to_all(pieces, "cond", 0, 0, tiled=True)
    total = pieces.reshape(conds * each * 4, nz)[: tiles * 4].reshape(3, planes, ny, nz)
    return (adjoint, total)


def solution(mesh):
    in_specs = (
        P("cond", None, "grid", None, None),
        P("cond", None, "grid", None, None),
        P("grid", None, None),
        P("cond", None, None),
        P("cond", None, None),
        P("cond", None, None),
        P("cond", None, None),
        P("cond", None, None),
        P("cond"),
    )
    out_specs = (P("cond", None, "grid", None, None), P(None, "grid", None, None))
    return jax.shard_map(body, mesh=mesh, in_specs=in_specs, out_specs=out_specs, check_vma=False)
```

```python
import functools
import math

import jax
import jax.numpy as jnp
from jax import lax
from jax.experimental import pallas as pl
from jax.experimental.pallas import tpu as pltpu
from jax.sharding import PartitionSpec as P

F32 = jnp.float32
FIELDS = 5
VMEM = pl.BlockSpec(memory_space=pltpu.VMEM)
SMEM = pl.BlockSpec(memory_space=pltpu.SMEM)
LIMIT = 20 * 1024 * 1024
ANY = pl.BlockSpec(memory_space=pl.ANY)
HBM = pl.BlockSpec(memory_space=pltpu.HBM)


def split(v):
    high = v.astype(jnp.bfloat16)
    return high, (v - high.astype(F32)).astype(jnp.bfloat16)


def dot(a, b):
    one = functools.partial(jnp.dot, preferred_element_type=F32)
    (a_high, a_low), (b_high, b_low) = split(a), split(b)
    return one(a_high, b_high) + (one(a_high, b_low) + one(a_low, b_high))


def exact(a, b):
    return jnp.dot(a, b, precision=lax.Precision.HIGHEST, preferred_element_type=F32)


def counters(length, repeat):
    return lax.broadcasted_iota(jnp.int32, (length * repeat,), 0) // repeat + 1


def sine_table(length, repeat_rows=1, repeat_columns=1):
    product = counters(length, repeat_rows)[:, None] * counters(length, repeat_columns)[None, :]
    product = product % (2 * (length + 1))
    return math.sqrt(2.0 / (length + 1)) * jnp.sin(product.astype(F32) * (math.pi / (length + 1)))


def spectrum(length):
    half = jnp.sin(counters(length, 1).astype(F32) * (math.pi / (2 * (length + 1))))
    lam = 4.0 * half * half
    return (lam + lam * lam)[None, :]


def call(kernel, outs, in_specs, flops, name, scratch=(), out_specs=None):
    return pl.pallas_call(
        kernel,
        out_shape=outs,
        in_specs=in_specs,
        out_specs=out_specs or jax.tree.map(lambda _: VMEM, outs),
        scratch_shapes=list(scratch),
        compiler_params=pltpu.CompilerParams(vmem_limit_bytes=LIMIT),
        cost_estimate=pl.CostEstimate(flops=flops, bytes_accessed=4_000_000, transcendentals=0),
        name=name,
    )


def shape(*dims):
    return jax.ShapeDtypeStruct(dims, F32)


def vmem(*dims):
    return pltpu.VMEM(dims, F32)


def fetch(sources, targets, sems):
    copies = [pltpu.make_async_copy(a, b, sems.at[i]) for i, (a, b) in enumerate(zip(sources, targets))]
    for copy in copies:
        copy.start()
    return copies


def shifted(v, axis, step):
    size = v.shape[axis]
    rolled = pltpu.roll(v, (-step) % size, axis)
    at = lax.broadcasted_iota(jnp.int32, v.shape, axis)
    return jnp.where(at == (size - 1 if step > 0 else 0), 0.0, rolled)


def mixed(weight, values):
    total = weight(0) * values[0]
    for g in range(1, FIELDS):
        total = total + weight(g) * values[g]
    return total


def spot(c, b):
    return (b // 2) * 4 + c * 2 + b % 2


def tables_kernel(rates, sine_z, spec_z, sine_y, spec_y, solve_z, solve_y):
    for c in range(2):
        for f in range(FIELDS):
            denom = 1.0 + rates[2, c, f] * spec_z[...]
            solve_z[c, f] = exact(sine_z[...] / denom, sine_z[...])
            denom = 1.0 + rates[1, c, f] * spec_y[...]
            solve_y[c, f] = exact(sine_y[...] / denom, sine_y[...])


def tables_y_kernel(rates, token, sine_y, spec_y, solve_y):
    for c in range(2):
        for f in range(FIELDS):
            denom = 1.0 + rates[1, c, f] * spec_y[...]
            solve_y[c, f] = exact(sine_y[...] / denom, sine_y[...])


def tables_b_kernel(info, coup, left_map, right_map, rates, token, sine_z, spec_z, left, right, left_2, right_2, spec_x,
                    solve_x, ends_prev, ends_next, halo_prev, halo_next, solve_z, mixes):
    mine = info[1]
    for f in range(FIELDS):
        for g in range(FIELDS):
            near, far = 0.0, 0.0
            for h in range(FIELDS):
                near = near + left_map[f, mine, h] * right_map[h, mine, g]
                inner = 0.0
                for i in range(FIELDS):
                    inner = inner + coup[h, mine, i] * right_map[i, mine, g]
                far = far + left_map[f, mine, h] * inner
            mixes[0, f, g] = near
            mixes[1, f, g] = far
        mixes[2, f, 0] = rates[1, mine, f]
    n, nx = left.shape
    row, col = (lax.broadcasted_iota(jnp.int32, (n, n), i) for i in range(2))
    same = (row & 7) == (col & 7)
    row, col = (lax.broadcasted_iota(jnp.int32, (2 * nx, n), i) for i in range(2))
    prev_rows = (row & 1) == (col & 7)
    next_rows = (row & 1) + 6 == (col & 7)
    row, col = (lax.broadcasted_iota(jnp.int32, (2 * nx, 2 * nx), i) for i in range(2))
    from_last = ((row & 1) == 0) & ((col & 1) == 1)
    from_first = ((row & 1) == 1) & ((col & 1) == 0)
    for f in range(FIELDS):
        denom = 1.0 + rates[0, mine, f] * spec_x[...]
        scaled = left[...] / denom
        solve_x[f] = jnp.where(same, exact(scaled, right[...]), 0.0)
        scaled_2 = left_2[...] / denom
        both = exact(scaled_2, right[...])
        ends_prev[f] = jnp.where(prev_rows, both, 0.0)
        ends_next[f] = jnp.where(next_rows, both, 0.0)
        both = exact(scaled_2, right_2[...])
        halo_prev[f] = jnp.where(from_last, both, 0.0)
        halo_next[f] = jnp.where(from_first, both, 0.0)
        denom = 1.0 + rates[2, mine, f] * spec_z[...]
        solve_z[f] = exact(sine_z[...] / denom, sine_z[...])


def plane_kernel(info, adjoint, inner, sem):
    copy = pltpu.make_async_copy(adjoint.at[:, :, 1 - info[0]], inner, sem)
    copy.start()
    copy.wait()


def first_kernel(info, coup, left, adjoint, other, source_in, radius, solve_z, solve_y, out, token,
                 source, made, lapped, stage, sems, out_sems):
    copies = fetch([source_in.at[c] for c in range(2)], [source.at[c] for c in range(2)], sems)
    ny = adjoint.shape[3]
    blocks = ny // 8
    me = info[0]
    before, after = me.astype(F32), (1 - me).astype(F32)
    token[...] = jnp.zeros(token.shape, F32)
    stores = []
    for c in range(2):
        residual = {}
        for x in range(2):
            for f in range(FIELDS):
                v = adjoint[c, f, x]
                beside = adjoint[c, f, 1 - x]
                beside = beside + other[c, f] * (before if x == 0 else after)
                beside = beside + shifted(v, 0, 1) + shifted(v, 0, -1)
                beside = beside + shifted(v, 1, 1) + shifted(v, 1, -1)
                lapped[x, f] = 6.0 * v - beside
        copies[c].wait()
        for x in range(2):
            sr = radius[x]
            residual = []
            for f in range(FIELDS):
                r = source[c, f, x] - sr * adjoint[c, f, x]
                for g in range(FIELDS):
                    r = r - coup[f, c, g] * lapped[x, g]
                residual.append(r)
            for f in range(FIELDS):
                stage[f, x * ny : x * ny + ny] = mixed(lambda g: left[f, c, g], residual)
        outer = [adjoint[c, g, me] for g in range(FIELDS)]
        outer = [mixed(lambda g: coup[f, c, g], outer) for f in range(FIELDS)]
        for f in range(FIELDS):
            stage[f, 2 * ny : 3 * ny] = mixed(lambda g: left[f, c, g], outer)
        for f in range(FIELDS):
            r = dot(stage[f], solve_z[c, f])
            r = jnp.concatenate([r[p * ny : p * ny + ny] for p in range(3)], axis=1)
            r = dot(solve_y[c, f], r)
            for p in range(3):
                for b in range(blocks):
                    made[b // 2, c, b % 2, 3 * f + p] = r[8 * b : 8 * b + 8, 128 * p : 128 * p + 128]
        for x in range(2):
            for b in range(blocks):
                made[b // 2, c, b % 2, 3 * FIELDS + x] = radius[x, 8 * b : 8 * b + 8]
        stores.append(pltpu.make_async_copy(made.at[:, c], out.at[:, c], out_sems.at[c]))
        stores[-1].start()
    for copy in stores:
        copy.wait()


def assembled(lines, f):
    zero = jnp.zeros((1, 8, 128), F32)
    w = lines[:, 3 * f : 3 * f + 3].reshape(lines.shape[0] // 2, 6, 8, 128)
    plane_0 = w[:, 0] + jnp.concatenate([zero, w[:-1, 5]], axis=0)
    plane_3 = w[:, 4] + jnp.concatenate([w[1:, 2], zero], axis=0)
    return jnp.stack([plane_0, w[:, 1], w[:, 3], plane_3], axis=1)


def ends_kernel(lines, ends_prev, ends_next, to_prev, to_next):
    for f in range(FIELDS):
        w = assembled(lines, f).reshape(-1, 128)
        to_prev[f] = dot(ends_prev[f], w)
        to_next[f] = dot(ends_next[f], w)


def second_kernel(info, mixes, lines, solve_x, solve_z, out, solved, lapped, kept):
    nx = out.shape[1]
    full = (nx, 8, 128)
    row = lax.broadcasted_iota(jnp.int32, full, 1)
    has_prev, has_next = info[2].astype(F32), info[3].astype(F32)
    zero = jnp.zeros((1, 8, 128), F32)
    for f in range(FIELDS):
        u = dot(solve_x[f], assembled(lines, f).reshape(nx * 8, 128)).reshape(full)
        solved[f] = u
        up = jnp.where(row == 7, 0.0, pltpu.roll(u, 7, 1))
        down = jnp.where(row == 0, 0.0, pltpu.roll(u, 1, 1))
        ku = 2.0 * u - up - down
        k_up = jnp.where(row == 7, -has_next * u, pltpu.roll(ku, 7, 1))
        k_down = jnp.where(row == 0, -has_prev * u, pltpu.roll(ku, 1, 1))
        kku = 2.0 * ku - k_up - k_down
        kept[f] = 2.0 * (u + mixes[2, f, 0] * (ku + kku))
        beside = jnp.concatenate([zero, u[:-1]], axis=0) + jnp.concatenate([u[1:], zero], axis=0)
        flat = u.reshape(nx * 8, 128)
        beside = beside + (shifted(flat, 1, 1) + shifted(flat, 1, -1)).reshape(full)
        lapped[f] = 4.0 * u + ku - beside
    sr = lines[:, 3 * FIELDS :].reshape(full)
    for f in range(FIELDS):
        near = mixed(lambda g: mixes[0, f, g], solved)
        far = mixed(lambda g: mixes[1, f, g], lapped)
        v = (sr * near + far).reshape(nx * 8, 128)
        v = dot(solve_x[f], dot(v, solve_z[f]))
        out[f] = kept[f] - v.reshape(full)


def halo_kernel(mixes, local, from_prev, from_next, halo_prev, halo_next, solve_z, out, token, made, sems):
    nx = local.shape[1]
    full = (nx, 8, 128)
    row = lax.broadcasted_iota(jnp.int32, full, 1)
    odd = (lax.broadcasted_iota(jnp.int32, (2 * nx, 128), 0) & 1) == 1
    token[...] = jnp.zeros(token.shape, F32)
    stores = []
    for f in range(FIELDS):
        first, last = from_prev[f], from_next[f]
        far = jnp.concatenate(
            [mixed(lambda g: mixes[1, f, g], from_prev), mixed(lambda g: mixes[1, f, g], from_next)], axis=0
        )
        far = dot(far, solve_z[f])
        far_prev, far_next = far[: 2 * nx], far[2 * nx :]
        scale = 2.0 * mixes[2, f, 0]
        add_prev = jnp.where(odd, first, first - 5.0 * pltpu.roll(first, 2 * nx - 1, 0))
        add_next = jnp.where(odd, last - 5.0 * pltpu.roll(last, 1, 0), last)
        add_prev = scale * add_prev + dot(halo_prev[f], far_prev)
        add_next = scale * add_next + dot(halo_next[f], far_next)
        spread = lambda v, at: jnp.stack(
            [pltpu.roll(v.reshape(nx // 4, 8, 128), (at - 2 * j) % 8, 1) for j in range(4)], axis=1
        ).reshape(full)
        q = local[f] + jnp.where(
            row < 2, spread(add_prev, 0), jnp.where(row >= 6, spread(add_next, 6), 0.0)
        )
        made[:, 2 * f : 2 * f + 2] = q.reshape(nx // 2, 2, 8, 128)
        part = pl.ds(2 * f, 2)
        stores.append(pltpu.make_async_copy(made.at[:, part], out.at[:, part], sems.at[f]))
        stores[-1].start()
    for copy in stores:
        copy.wait()


def gathered(solved, c, tile, blocks):
    return jnp.concatenate([solved[spot(c, b), tile] for b in range(blocks)], axis=0)


def update_kernel(info, right, adjoint, solved, solve_y, out, inner, outer, step):
    ny = adjoint.shape[3]
    me = info[0]
    for c in range(2):
        for f in range(FIELDS):
            q = jnp.concatenate([gathered(solved, c, 2 * f + x, ny // 8) for x in range(2)], axis=1)
            step[f] = dot(solve_y[c, f], q)
        steps = [[step[g, :, 128 * x : 128 * x + 128] for g in range(FIELDS)] for x in range(2)]
        for f in range(FIELDS):
            planes = [adjoint[c, f, x] + mixed(lambda g: right[f, c, g], steps[x]) for x in range(2)]
            for x in range(2):
                out[c, f, x] = planes[x]
            inner[c, f] = jnp.where(me == 0, planes[1], planes[0])
            outer[c, f] = jnp.where(me == 0, planes[0], planes[1])


def inside_kernel(smap, weights, adjoint, terms):
    totals = [[0.0, 0.0] for _ in range(3)]
    for c in range(2):
        weight = weights[c].astype(F32)
        for f in range(FIELDS):
            w = [weight * smap[k, c, f] for k in range(3)]
            v = [adjoint[c, f, x] for x in range(2)]
            pair = w[0] * (v[0] * v[1])
            totals[0][0] += pair
            totals[0][1] -= pair
            for x in range(2):
                for k in range(2):
                    totals[k + 1][x] += w[k + 1] * (v[x] * (shifted(v[x], k, 1) - shifted(v[x], k, -1)))
    for k in range(3):
        for x in range(2):
            terms[k, x] = totals[k][x]


def terms_kernel(info, smap, weights, inner, other_inner, outer, other_outer, inside, out):
    me = info[0]
    ny = inner.shape[2]
    each = out.shape[1]

    def store(k, x, v):
        for i in range(ny // 4):
            piece, at = divmod((k * 2 + x) * (ny // 4) + i, each)
            out[piece, at] = v[4 * i : 4 * i + 4]

    with_core, with_chip = 0.0, 0.0
    for c in range(2):
        weight = weights[c].astype(F32)
        for f in range(FIELDS):
            w = weight * smap[0, c, f]
            with_core += w * (inner[c, f] * other_inner[c, f])
            with_chip += w * (outer[c, f] * other_outer[c, f])
    store(0, 0, inside[0, 0] - jnp.where(me == 0, with_chip, with_core))
    store(0, 1, inside[0, 1] + jnp.where(me == 0, with_core, with_chip))
    for k in range(1, 3):
        for x in range(2):
            store(k, x, inside[k, x])
    for i in range(6 * ny // 4, out.shape[0] * each):
        piece, at = divmod(i, each)
        out[piece, at] = jnp.zeros(out.shape[2:], F32)


def sum_kernel(scale, pieces, out):
    total = pieces[0]
    for i in range(1, pieces.shape[0]):
        total = total + pieces[i]
    total = total * scale
    for i in range(out.shape[0]):
        out[i] = total


def body(
    adjoint_source,
    adjoint_start,
    spectral_radius,
    coupling,
    left_vectors,
    right_vectors,
    implicit_scales,
    sensitivity_map,
    condition_weights,
):
    peers = lax.axis_size("grid")
    conds = lax.axis_size("cond")
    _, fields, planes, ny, nz = adjoint_start.shape
    nx = peers * planes
    rows_b = nx * 8
    blocks = peers // 2
    sems = lambda n: pltpu.SemaphoreType.DMA((n,))

    me = lax.axis_index("grid")
    core = me % 2
    side = (me // 2) % 2
    place = (me // 4) * 2 + core
    info = jnp.stack([core, side, place > 0, place < blocks - 1]).astype(jnp.int32)

    cores = [(i, i ^ 1) for i in range(peers)]
    chips = [(i, i + 1) for i in range(1, peers - 1, 2)]
    chips = chips + [(j, i) for i, j in chips]
    other = call(
        plane_kernel,
        shape(2, fields, ny, nz),
        [SMEM, ANY],
        1000,
        "inner_plane",
        [pltpu.SemaphoreType.DMA(())],
        ANY,
    )(info, adjoint_start)
    other = lax.ppermute(other, "grid", cores)

    sine_z, spec_z = sine_table(nz), spectrum(nz)
    sine_y, spec_y = sine_table(ny), spectrum(ny)

    coup, left_map, right_map, smap = (
        jnp.swapaxes(v, 0, 1) for v in (coupling, left_vectors, right_vectors, sensitivity_map)
    )
    rates = jnp.transpose(implicit_scales, (2, 0, 1))

    solve_z, solve_y = call(
        tables_kernel,
        (shape(2, fields, nz, nz), shape(2, fields, ny, ny)),
        [SMEM] + [VMEM] * 4,
        100_000_000,
        "solve_tables",
    )(rates, sine_z, spec_z, sine_y, spec_y)

    lines, token = call(
        first_kernel,
        (shape(blocks // 2, 2, 2, 3 * fields + planes, 8, nz), shape(8, nz)),
        [SMEM, SMEM, SMEM, VMEM, VMEM, HBM, VMEM, VMEM, VMEM],
        200_000_000,
        "first_residual",
        [
            vmem(2, fields, planes, ny, nz),
            vmem(blocks // 2, 2, 2, 3 * fields + planes, 8, nz),
            vmem(planes, fields, ny, nz),
            vmem(fields, 3 * ny, nz),
            sems(2),
            sems(2),
        ],
        (ANY, VMEM),
    )(info, coup, left_map, adjoint_start, other, adjoint_source, spectral_radius, solve_z, solve_y)

    lines = lines.reshape(peers, 3 * fields + planes, 8, nz)
    lines = lax.all_to_all(lines, "grid", 0, 0, tiled=True)

    solve_x, ends_prev, ends_next, halo_prev, halo_next, solve_zb, mixes = call(
        tables_b_kernel,
        (
            shape(fields, rows_b, rows_b),
            shape(fields, 2 * nx, rows_b),
            shape(fields, 2 * nx, rows_b),
            shape(fields, 2 * nx, 2 * nx),
            shape(fields, 2 * nx, 2 * nx),
            shape(fields, nz, nz),
            shape(3, fields, fields),
        ),
        [SMEM] * 5 + [VMEM] * 8,
        100_000_000,
        "tables_b",
        (),
        (VMEM,) * 6 + (SMEM,),
    )(
        info, coup, left_map, right_map, rates, token, sine_z, spec_z,
        sine_table(nx, 8, 1), sine_table(nx, 1, 8), sine_table(nx, 2, 1), sine_table(nx, 1, 2), spectrum(nx),
    )

    to_prev, to_next = call(
        ends_kernel,
        (shape(fields, 2 * nx, nz), shape(fields, 2 * nx, nz)),
        [VMEM] * 3,
        50_000_000,
        "solve_ends",
    )(lines, ends_prev, ends_next)

    up = [(spot(s, b), spot(s, b + 1)) for s in range(2) for b in range(blocks - 1)]
    down = [(j, i) for i, j in up]
    from_prev = lax.ppermute(to_next, "grid", up)
    from_next = lax.ppermute(to_prev, "grid", down)

    local = call(
        second_kernel,
        shape(fields, nx, 8, nz),
        [SMEM, SMEM] + [VMEM] * 3,
        300_000_000,
        "second_residual",
        [vmem(fields, nx, 8, nz) for _ in range(3)],
    )(info, mixes, lines, solve_x, solve_zb)

    step, token = call(
        halo_kernel,
        (shape(peers, planes * fields, 8, nz), shape(8, nz)),
        [SMEM] + [VMEM] * 6,
        50_000_000,
        "halo_rows",
        [vmem(peers, planes * fields, 8, nz), sems(fields)],
        (ANY, VMEM),
    )(mixes, local, from_prev, from_next, halo_prev, halo_next, solve_zb)

    step = lax.all_to_all(step, "grid", 0, 0, tiled=True)

    solve_y = call(
        tables_y_kernel,
        shape(2, fields, ny, ny),
        [SMEM, VMEM, VMEM, VMEM],
        50_000_000,
        "tables_y",
    )(rates, token, sine_y, spec_y)

    slab = shape(2, fields, ny, nz)
    adjoint, inner, outer = call(
        update_kernel,
        (shape(2, fields, planes, ny, nz), slab, slab),
        [SMEM, SMEM] + [VMEM] * 3,
        60_000_000,
        "update",
        [vmem(fields, ny, 2 * nz)],
    )(info, right_map, adjoint_start, step, solve_y)

    other_outer = lax.ppermute(outer, "grid", chips)
    other_inner = lax.ppermute(inner, "grid", cores)

    inside = call(
        inside_kernel,
        shape(3, planes, ny, nz),
        [SMEM, SMEM, VMEM],
        60_000_000,
        "inside_terms",
    )(smap, condition_weights, adjoint)

    tiles = 3 * planes * ny // 4
    each = -(-tiles // conds)
    pieces = call(
        terms_kernel,
        shape(conds, each, 4, nz),
        [SMEM] * 3 + [VMEM] * 5,
        10_000_000,
        "terms",
    )(info, smap, condition_weights, inner, other_inner, outer, other_outer, inside)
    pieces = lax.all_to_all(pieces, "cond", 0, 0, tiled=True)
    scale = 1.0 / (conds * condition_weights.shape[0])
    pieces = call(
        functools.partial(sum_kernel, scale),
        shape(conds, each, 4, nz),
        [VMEM],
        1_000_000,
        "sum_conditions",
    )(pieces)
    pieces = lax.all_to_all(pieces, "cond", 0, 0, tiled=True)
    total = pieces.reshape(conds * each * 4, nz)[: tiles * 4].reshape(3, planes, ny, nz)
    return (adjoint, total)


def solution(mesh):
    in_specs = (
        P("cond", None, "grid", None, None),
        P("cond", None, "grid", None, None),
        P("grid", None, None),
        P("cond", None, None),
        P("cond", None, None),
        P("cond", None, None),
        P("cond", None, None),
        P("cond", None, None),
        P("cond"),
    )
    out_specs = (P("cond", None, "grid", None, None), P(None, "grid", None, None))
    return jax.shard_map(body, mesh=mesh, in_specs=in_specs, out_specs=out_specs, check_vma=False)
```

```python
import functools
import math

import jax
import jax.numpy as jnp
from jax import lax
from jax.experimental import pallas as pl
from jax.experimental.pallas import tpu as pltpu
from jax.sharding import PartitionSpec as P

F32 = jnp.float32
FIELDS = 5
VMEM = pl.BlockSpec(memory_space=pltpu.VMEM)
SMEM = pl.BlockSpec(memory_space=pltpu.SMEM)
LIMIT = 20 * 1024 * 1024
ANY = pl.BlockSpec(memory_space=pl.ANY)
HBM = pl.BlockSpec(memory_space=pltpu.HBM)


def split(v):
    high = v.astype(jnp.bfloat16)
    return high, (v - high.astype(F32)).astype(jnp.bfloat16)


def dot(a, b):
    one = functools.partial(jnp.dot, preferred_element_type=F32)
    (a_high, a_low), (b_high, b_low) = split(a), split(b)
    return one(a_high, b_high) + (one(a_high, b_low) + one(a_low, b_high))


def exact(a, b):
    return jnp.dot(a, b, precision=lax.Precision.HIGHEST, preferred_element_type=F32)


def counters(length, repeat):
    return lax.broadcasted_iota(jnp.int32, (length * repeat,), 0) // repeat + 1


def sine_table(length, repeat_rows=1, repeat_columns=1):
    product = counters(length, repeat_rows)[:, None] * counters(length, repeat_columns)[None, :]
    product = product % (2 * (length + 1))
    return math.sqrt(2.0 / (length + 1)) * jnp.sin(product.astype(F32) * (math.pi / (length + 1)))


def spectrum(length):
    half = jnp.sin(counters(length, 1).astype(F32) * (math.pi / (2 * (length + 1))))
    lam = 4.0 * half * half
    return (lam + lam * lam)[None, :]


def call(kernel, outs, in_specs, flops, name, scratch=(), out_specs=None):
    return pl.pallas_call(
        kernel,
        out_shape=outs,
        in_specs=in_specs,
        out_specs=out_specs or jax.tree.map(lambda _: VMEM, outs),
        scratch_shapes=list(scratch),
        compiler_params=pltpu.CompilerParams(vmem_limit_bytes=LIMIT),
        cost_estimate=pl.CostEstimate(flops=flops, bytes_accessed=4_000_000, transcendentals=0),
        name=name,
    )


def shape(*dims):
    return jax.ShapeDtypeStruct(dims, F32)


def vmem(*dims):
    return pltpu.VMEM(dims, F32)


def fetch(sources, targets, sems):
    copies = [pltpu.make_async_copy(a, b, sems.at[i]) for i, (a, b) in enumerate(zip(sources, targets))]
    for copy in copies:
        copy.start()
    return copies


def shifted(v, axis, step):
    size = v.shape[axis]
    rolled = pltpu.roll(v, (-step) % size, axis)
    at = lax.broadcasted_iota(jnp.int32, v.shape, axis)
    return jnp.where(at == (size - 1 if step > 0 else 0), 0.0, rolled)


def mixed(weight, values):
    total = weight(0) * values[0]
    for g in range(1, FIELDS):
        total = total + weight(g) * values[g]
    return total


def spot(c, b):
    return (b // 2) * 4 + c * 2 + b % 2


def tables_kernel(rates, sine_z, spec_z, sine_y, spec_y, solve_z, solve_y):
    for c in range(2):
        for f in range(FIELDS):
            denom = 1.0 + rates[2, c, f] * spec_z[...]
            solve_z[c, f] = exact(sine_z[...] / denom, sine_z[...])
            denom = 1.0 + rates[1, c, f] * spec_y[...]
            solve_y[c, f] = exact(sine_y[...] / denom, sine_y[...])


def tables_y_kernel(info, rates, token, sine_y, spec_y, solve_y):
    for f in range(FIELDS):
        denom = 1.0 + rates[1, info[1], f] * spec_y[...]
        solve_y[f] = exact(sine_y[...] / denom, sine_y[...])


def tables_b_kernel(info, coup, left_map, right_map, rates, token, sine_z, spec_z, left, right, left_2, right_2, spec_x,
                    solve_x, ends_prev, ends_next, halo_prev, halo_next, solve_z, mixes):
    mine = info[1]
    for f in range(FIELDS):
        for g in range(FIELDS):
            near, far = 0.0, 0.0
            for h in range(FIELDS):
                near = near + left_map[f, mine, h] * right_map[h, mine, g]
                inner = 0.0
                for i in range(FIELDS):
                    inner = inner + coup[h, mine, i] * right_map[i, mine, g]
                far = far + left_map[f, mine, h] * inner
            mixes[0, f, g] = near
            mixes[1, f, g] = far
        mixes[2, f, 0] = rates[1, mine, f]
    n, nx = left.shape
    row, col = (lax.broadcasted_iota(jnp.int32, (n, n), i) for i in range(2))
    same = (row & 7) == (col & 7)
    row, col = (lax.broadcasted_iota(jnp.int32, (2 * nx, n), i) for i in range(2))
    prev_rows = (row & 1) == (col & 7)
    next_rows = (row & 1) + 6 == (col & 7)
    row, col = (lax.broadcasted_iota(jnp.int32, (2 * nx, 2 * nx), i) for i in range(2))
    from_last = ((row & 1) == 0) & ((col & 1) == 1)
    from_first = ((row & 1) == 1) & ((col & 1) == 0)
    for f in range(FIELDS):
        denom = 1.0 + rates[0, mine, f] * spec_x[...]
        scaled = left[...] / denom
        solve_x[f] = jnp.where(same, exact(scaled, right[...]), 0.0)
        scaled_2 = left_2[...] / denom
        both = exact(scaled_2, right[...])
        ends_prev[f] = jnp.where(prev_rows, both, 0.0)
        ends_next[f] = jnp.where(next_rows, both, 0.0)
        both = exact(scaled_2, right_2[...])
        halo_prev[f] = jnp.where(from_last, both, 0.0)
        halo_next[f] = jnp.where(from_first, both, 0.0)
        denom = 1.0 + rates[2, mine, f] * spec_z[...]
        solve_z[f] = exact(sine_z[...] / denom, sine_z[...])


def plane_kernel(info, adjoint, inner, sem):
    copy = pltpu.make_async_copy(adjoint.at[:, :, 1 - info[0]], inner, sem)
    copy.start()
    copy.wait()


def first_kernel(info, coup, left, adjoint, other, source_in, radius, solve_z, solve_y, out, token,
                 source, made, lapped, stage, sems, out_sems):
    copies = fetch([source_in.at[c] for c in range(2)], [source.at[c] for c in range(2)], sems)
    ny = adjoint.shape[3]
    blocks = ny // 8
    me = info[0]
    before, after = me.astype(F32), (1 - me).astype(F32)
    token[...] = jnp.zeros(token.shape, F32)
    stores = []
    for c in range(2):
        residual = {}
        for x in range(2):
            for f in range(FIELDS):
                v = adjoint[c, f, x]
                beside = adjoint[c, f, 1 - x]
                beside = beside + other[c, f] * (before if x == 0 else after)
                beside = beside + shifted(v, 0, 1) + shifted(v, 0, -1)
                beside = beside + shifted(v, 1, 1) + shifted(v, 1, -1)
                lapped[x, f] = 6.0 * v - beside
        copies[c].wait()
        for x in range(2):
            sr = radius[x]
            residual = []
            for f in range(FIELDS):
                r = source[c, f, x] - sr * adjoint[c, f, x]
                for g in range(FIELDS):
                    r = r - coup[f, c, g] * lapped[x, g]
                residual.append(r)
            for f in range(FIELDS):
                stage[f, x * ny : x * ny + ny] = mixed(lambda g: left[f, c, g], residual)
        outer = [adjoint[c, g, me] for g in range(FIELDS)]
        outer = [mixed(lambda g: coup[f, c, g], outer) for f in range(FIELDS)]
        for f in range(FIELDS):
            stage[f, 2 * ny : 3 * ny] = mixed(lambda g: left[f, c, g], outer)
        for f in range(FIELDS):
            r = dot(stage[f], solve_z[c, f])
            r = jnp.concatenate([r[p * ny : p * ny + ny] for p in range(3)], axis=1)
            r = dot(solve_y[c, f], r)
            for p in range(3):
                for b in range(blocks):
                    made[b // 2, c, b % 2, 3 * f + p] = r[8 * b : 8 * b + 8, 128 * p : 128 * p + 128]
        for x in range(2):
            for b in range(blocks):
                made[b // 2, c, b % 2, 3 * FIELDS + x] = radius[x, 8 * b : 8 * b + 8]
        stores.append(pltpu.make_async_copy(made.at[:, c], out.at[:, c], out_sems.at[c]))
        stores[-1].start()
    for copy in stores:
        copy.wait()


def assembled(lines, f):
    zero = jnp.zeros((1, 8, 128), F32)
    w = lines[:, 3 * f : 3 * f + 3].reshape(lines.shape[0] // 2, 6, 8, 128)
    plane_0 = w[:, 0] + jnp.concatenate([zero, w[:-1, 5]], axis=0)
    plane_3 = w[:, 4] + jnp.concatenate([w[1:, 2], zero], axis=0)
    return jnp.stack([plane_0, w[:, 1], w[:, 3], plane_3], axis=1)


def ends_kernel(info, lines, ends_prev, ends_next, adjoint, to_prev, to_next, give, sem):
    copy = pltpu.make_async_copy(adjoint.at[1 - info[1]], give, sem)
    copy.start()
    for f in range(FIELDS):
        w = assembled(lines, f).reshape(-1, 128)
        to_prev[f] = dot(ends_prev[f], w)
        to_next[f] = dot(ends_next[f], w)
    copy.wait()


def second_kernel(info, mixes, lines, solve_x, solve_z, out, solved, lapped, kept):
    nx = out.shape[1]
    full = (nx, 8, 128)
    row = lax.broadcasted_iota(jnp.int32, full, 1)
    has_prev, has_next = info[2].astype(F32), info[3].astype(F32)
    zero = jnp.zeros((1, 8, 128), F32)
    for f in range(FIELDS):
        u = dot(solve_x[f], assembled(lines, f).reshape(nx * 8, 128)).reshape(full)
        solved[f] = u
        up = jnp.where(row == 7, 0.0, pltpu.roll(u, 7, 1))
        down = jnp.where(row == 0, 0.0, pltpu.roll(u, 1, 1))
        ku = 2.0 * u - up - down
        k_up = jnp.where(row == 7, -has_next * u, pltpu.roll(ku, 7, 1))
        k_down = jnp.where(row == 0, -has_prev * u, pltpu.roll(ku, 1, 1))
        kku = 2.0 * ku - k_up - k_down
        kept[f] = 2.0 * (u + mixes[2, f, 0] * (ku + kku))
        beside = jnp.concatenate([zero, u[:-1]], axis=0) + jnp.concatenate([u[1:], zero], axis=0)
        flat = u.reshape(nx * 8, 128)
        beside = beside + (shifted(flat, 1, 1) + shifted(flat, 1, -1)).reshape(full)
        lapped[f] = 4.0 * u + ku - beside
    sr = lines[:, 3 * FIELDS :].reshape(full)
    for f in range(FIELDS):
        near = mixed(lambda g: mixes[0, f, g], solved)
        far = mixed(lambda g: mixes[1, f, g], lapped)
        v = (sr * near + far).reshape(nx * 8, 128)
        v = dot(solve_x[f], dot(v, solve_z[f]))
        out[f] = kept[f] - v.reshape(full)


def halo_kernel(mixes, local, from_prev, from_next, halo_prev, halo_next, solve_z, out, token, made, sems):
    nx = local.shape[1]
    full = (nx, 8, 128)
    row = lax.broadcasted_iota(jnp.int32, full, 1)
    odd = (lax.broadcasted_iota(jnp.int32, (2 * nx, 128), 0) & 1) == 1
    token[...] = jnp.zeros(token.shape, F32)
    stores = []
    for f in range(FIELDS):
        first, last = from_prev[f], from_next[f]
        far = jnp.concatenate(
            [mixed(lambda g: mixes[1, f, g], from_prev), mixed(lambda g: mixes[1, f, g], from_next)], axis=0
        )
        far = dot(far, solve_z[f])
        far_prev, far_next = far[: 2 * nx], far[2 * nx :]
        scale = 2.0 * mixes[2, f, 0]
        add_prev = jnp.where(odd, first, first - 5.0 * pltpu.roll(first, 2 * nx - 1, 0))
        add_next = jnp.where(odd, last - 5.0 * pltpu.roll(last, 1, 0), last)
        add_prev = scale * add_prev + dot(halo_prev[f], far_prev)
        add_next = scale * add_next + dot(halo_next[f], far_next)
        spread = lambda v, at: jnp.stack(
            [pltpu.roll(v.reshape(nx // 4, 8, 128), (at - 2 * j) % 8, 1) for j in range(4)], axis=1
        ).reshape(full)
        q = local[f] + jnp.where(
            row < 2, spread(add_prev, 0), jnp.where(row >= 6, spread(add_next, 6), 0.0)
        )
        q = q.reshape(nx // 8, 2, 2, 2, 8, 128)
        for core in range(2):
            for half in range(2):
                at = 4 * f + 2 * half
                made[:, core, at : at + 2] = q[:, half, core]
        part = pl.ds(4 * f, 4)
        stores.append(pltpu.make_async_copy(made.at[:, :, part], out.at[:, :, part], sems.at[f]))
        stores[-1].start()
    for copy in stores:
        copy.wait()


def update_kernel(info, right, adjoint, got, solved, solve_y, new, own, back, inner, outer, step):
    ny = adjoint.shape[3]
    core, side = info[0], info[1]
    for f in range(FIELDS):
        q = [
            jnp.concatenate([solved[b, 4 * f + p] for b in range(ny // 8)], axis=0) for p in range(4)
        ]
        step[f] = dot(solve_y[f], jnp.concatenate(q, axis=1))
    steps = [[step[g, :, 128 * p : 128 * p + 128] for g in range(FIELDS)] for p in range(4)]
    for f in range(FIELDS):
        a = []
        for p in range(4):
            start = jnp.where(side == p // 2, adjoint[side, f, p % 2], got[f, p % 2])
            a.append(start + mixed(lambda g: right[f, side, g], steps[p]))
            new[f, p] = a[p]
        for i in range(2):
            own[f, i] = jnp.where(side == 0, a[i], a[2 + i])
            back[f, i] = jnp.where(side == 0, a[2 + i], a[i])
        for i in range(3):
            inner[f, i] = jnp.where(core == 0, a[i + 1], a[i])
        outer[f] = jnp.where(core == 0, a[0], a[3])


def inside_kernel(info, smap, weights, new, terms):
    side = info[1]
    weight = weights[side].astype(F32)
    totals = [[0.0] * 4 for _ in range(3)]
    for f in range(FIELDS):
        w = [weight * smap[k, side, f] for k in range(3)]
        v = [new[f, p] for p in range(4)]
        for h in range(2):
            pair = w[0] * (v[2 * h] * v[2 * h + 1])
            totals[0][2 * h] += pair
            totals[0][2 * h + 1] -= pair
        for p in range(4):
            for k in range(2):
                totals[k + 1][p] += w[k + 1] * (v[p] * (shifted(v[p], k, 1) - shifted(v[p], k, -1)))
    for k in range(3):
        for p in range(4):
            terms[k, p] = totals[k][p]


def terms_kernel(info, smap, weights, inner, other_inner, outer, other_outer, inside, back, out, give, sem):
    copy = pltpu.make_async_copy(back, give, sem)
    copy.start()
    core, side = info[0], info[1]
    ny = inner.shape[2]
    each = out.shape[1]
    half = out.shape[0] // 2

    def store(k, p, v):
        for i in range(ny // 4):
            piece, at = divmod((k * 2 + p % 2) * (ny // 4) + i, each)
            out[(p // 2) * half + piece, at] = v[4 * i : 4 * i + 4]

    weight = weights[side].astype(F32)
    between, beyond = [0.0] * 3, 0.0
    for f in range(FIELDS):
        w = weight * smap[0, side, f]
        for i in range(3):
            between[i] += w * (inner[f, i] * other_inner[f, i])
        beyond += w * (outer[f] * other_outer[f])
    edges = ((beyond, between[0]), (between[0], between[1]), (between[1], between[2]), (between[2], beyond))
    for p in range(4):
        edge = jnp.where(core == 0, edges[p][0], edges[p][1])
        store(0, p, inside[0, p] + edge if p % 2 else inside[0, p] - edge)
        for k in range(1, 3):
            store(k, p, inside[k, p])
    for i in range(6 * ny // 4, half * each):
        piece, at = divmod(i, each)
        for h in range(2):
            out[h * half + piece, at] = jnp.zeros(out.shape[2:], F32)
    copy.wait()


def join_kernel(info, own, got, token, out, sems):
    side = info[1]
    for copy in fetch((own, got), (out.at[side], out.at[1 - side]), sems):
        copy.wait()


def sum_kernel(scale, pieces, out):
    total = pieces[0]
    for i in range(1, pieces.shape[0]):
        total = total + pieces[i]
    total = total * scale
    for i in range(out.shape[0]):
        out[i] = total


def body(
    adjoint_source,
    adjoint_start,
    spectral_radius,
    coupling,
    left_vectors,
    right_vectors,
    implicit_scales,
    sensitivity_map,
    condition_weights,
):
    peers = lax.axis_size("grid")
    conds = lax.axis_size("cond")
    _, fields, planes, ny, nz = adjoint_start.shape
    nx = peers * planes
    rows_b = nx * 8
    blocks = peers // 2
    sems = lambda n: pltpu.SemaphoreType.DMA((n,))

    me = lax.axis_index("grid")
    core = me % 2
    side = (me // 2) % 2
    place = (me // 4) * 2 + core
    info = jnp.stack([core, side, place > 0, place < blocks - 1]).astype(jnp.int32)

    cores = [(i, i ^ 1) for i in range(peers)]
    halves = [(i, i ^ 2) for i in range(peers)]
    chips = [(i, i + 3) for i in range(peers - 4) if i % 2 == 1]
    chips = chips + [(j, i) for i, j in chips]
    half_groups = [[i for i in range(peers) if i // 2 % 2 == half] for half in range(2)]
    other = call(
        plane_kernel,
        shape(2, fields, ny, nz),
        [SMEM, ANY],
        1000,
        "inner_plane",
        [pltpu.SemaphoreType.DMA(())],
        ANY,
    )(info, adjoint_start)
    other = lax.ppermute(other, "grid", cores)

    sine_z, spec_z = sine_table(nz), spectrum(nz)
    sine_y, spec_y = sine_table(ny), spectrum(ny)

    coup, left_map, right_map, smap = (
        jnp.swapaxes(v, 0, 1) for v in (coupling, left_vectors, right_vectors, sensitivity_map)
    )
    rates = jnp.transpose(implicit_scales, (2, 0, 1))

    solve_z, solve_y = call(
        tables_kernel,
        (shape(2, fields, nz, nz), shape(2, fields, ny, ny)),
        [SMEM] + [VMEM] * 4,
        100_000_000,
        "solve_tables",
    )(rates, sine_z, spec_z, sine_y, spec_y)

    lines, token = call(
        first_kernel,
        (shape(blocks // 2, 2, 2, 3 * fields + planes, 8, nz), shape(8, nz)),
        [SMEM, SMEM, SMEM, VMEM, VMEM, HBM, VMEM, VMEM, VMEM],
        200_000_000,
        "first_residual",
        [
            vmem(2, fields, planes, ny, nz),
            vmem(blocks // 2, 2, 2, 3 * fields + planes, 8, nz),
            vmem(planes, fields, ny, nz),
            vmem(fields, 3 * ny, nz),
            sems(2),
            sems(2),
        ],
        (ANY, VMEM),
    )(info, coup, left_map, adjoint_start, other, adjoint_source, spectral_radius, solve_z, solve_y)

    lines = lines.reshape(peers, 3 * fields + planes, 8, nz)
    lines = lax.all_to_all(lines, "grid", 0, 0, tiled=True)

    solve_x, ends_prev, ends_next, halo_prev, halo_next, solve_zb, mixes = call(
        tables_b_kernel,
        (
            shape(fields, rows_b, rows_b),
            shape(fields, 2 * nx, rows_b),
            shape(fields, 2 * nx, rows_b),
            shape(fields, 2 * nx, 2 * nx),
            shape(fields, 2 * nx, 2 * nx),
            shape(fields, nz, nz),
            shape(3, fields, fields),
        ),
        [SMEM] * 5 + [VMEM] * 8,
        100_000_000,
        "tables_b",
        (),
        (VMEM,) * 6 + (SMEM,),
    )(
        info, coup, left_map, right_map, rates, token, sine_z, spec_z,
        sine_table(nx, 8, 1), sine_table(nx, 1, 8), sine_table(nx, 2, 1), sine_table(nx, 1, 2), spectrum(nx),
    )

    to_prev, to_next, give = call(
        ends_kernel,
        (shape(fields, 2 * nx, nz), shape(fields, 2 * nx, nz), shape(fields, planes, ny, nz)),
        [SMEM] + [VMEM] * 3 + [ANY],
        50_000_000,
        "solve_ends",
        [pltpu.SemaphoreType.DMA(())],
        (VMEM, VMEM, ANY),
    )(info, lines, ends_prev, ends_next, adjoint_start)
    got = lax.ppermute(give, "grid", halves)

    up = [(spot(s, b), spot(s, b + 1)) for s in range(2) for b in range(blocks - 1)]
    down = [(j, i) for i, j in up]
    from_prev = lax.ppermute(to_next, "grid", up)
    from_next = lax.ppermute(to_prev, "grid", down)

    local = call(
        second_kernel,
        shape(fields, nx, 8, nz),
        [SMEM, SMEM] + [VMEM] * 3,
        300_000_000,
        "second_residual",
        [vmem(fields, nx, 8, nz) for _ in range(3)],
    )(info, mixes, lines, solve_x, solve_zb)

    step, token = call(
        halo_kernel,
        (shape(nx // 8, 2, 4 * fields, 8, nz), shape(8, nz)),
        [SMEM] + [VMEM] * 6,
        50_000_000,
        "halo_rows",
        [vmem(nx // 8, 2, 4 * fields, 8, nz), sems(fields)],
        (ANY, VMEM),
    )(mixes, local, from_prev, from_next, halo_prev, halo_next, solve_zb)

    step = step.reshape(blocks, 4 * fields, 8, nz)
    step = lax.all_to_all(step, "grid", 0, 0, axis_index_groups=half_groups, tiled=True)

    solve_y = call(
        tables_y_kernel,
        shape(fields, ny, ny),
        [SMEM, SMEM, VMEM, VMEM, VMEM],
        50_000_000,
        "tables_y",
    )(info, rates, token, sine_y, spec_y)

    new, own, back, inner, outer = call(
        update_kernel,
        (
            shape(fields, 4, ny, nz),
            shape(fields, planes, ny, nz),
            shape(fields, planes, ny, nz),
            shape(fields, 3, ny, nz),
            shape(fields, ny, nz),
        ),
        [SMEM, SMEM] + [VMEM] * 4,
        60_000_000,
        "update",
        [vmem(fields, ny, 4 * nz)],
    )(info, right_map, adjoint_start, got, step, solve_y)

    other_outer = lax.ppermute(outer, "grid", chips)
    other_inner = lax.ppermute(inner, "grid", cores)

    inside = call(
        inside_kernel,
        shape(3, 4, ny, nz),
        [SMEM, SMEM, SMEM, VMEM],
        60_000_000,
        "inside_terms",
    )(info, smap, condition_weights, new)

    tiles = 3 * planes * ny // 4
    each = -(-tiles // conds)
    pieces, back = call(
        terms_kernel,
        (shape(2 * conds, each, 4, nz), shape(fields, planes, ny, nz)),
        [SMEM] * 3 + [VMEM] * 5 + [ANY],
        10_000_000,
        "terms",
        [pltpu.SemaphoreType.DMA(())],
        (VMEM, ANY),
    )(info, smap, condition_weights, inner, other_inner, outer, other_outer, inside, back)

    groups = [
        [i * peers + x + 2 * half for half in range(2) for i in range(conds)]
        for x in range(peers)
        if x // 2 % 2 == 0
    ]
    pieces = lax.all_to_all(pieces, ("cond", "grid"), 0, 0, axis_index_groups=groups, tiled=True)
    back = lax.ppermute(back, "grid", halves)
    scale = 1.0 / (conds * condition_weights.shape[0])
    pieces = call(
        functools.partial(sum_kernel, scale),
        shape(conds, each, 4, nz),
        [VMEM],
        1_000_000,
        "sum_conditions",
    )(pieces)
    token = pieces
    pieces = lax.all_to_all(pieces, "cond", 0, 0, tiled=True)
    adjoint = call(
        join_kernel,
        shape(2, fields, planes, ny, nz),
        [SMEM, ANY, ANY, ANY],
        1000,
        "join",
        [sems(2)],
        ANY,
    )(info, own, back, token)
    total = pieces.reshape(conds * each * 4, nz)[: tiles * 4].reshape(3, planes, ny, nz)
    return (adjoint, total)


def solution(mesh):
    in_specs = (
        P("cond", None, "grid", None, None),
        P("cond", None, "grid", None, None),
        P("grid", None, None),
        P("cond", None, None),
        P("cond", None, None),
        P("cond", None, None),
        P("cond", None, None),
        P("cond", None, None),
        P("cond"),
    )
    out_specs = (P("cond", None, "grid", None, None), P(None, "grid", None, None))
    return jax.shard_map(body, mesh=mesh, in_specs=in_specs, out_specs=out_specs, check_vma=False)
```

```python
import functools
import math

import jax
import jax.numpy as jnp
from jax import lax
from jax.experimental import pallas as pl
from jax.experimental.pallas import tpu as pltpu
from jax.sharding import PartitionSpec as P

F32 = jnp.float32
FIELDS = 5
VMEM = pl.BlockSpec(memory_space=pltpu.VMEM)
SMEM = pl.BlockSpec(memory_space=pltpu.SMEM)
LIMIT = 20 * 1024 * 1024
ANY = pl.BlockSpec(memory_space=pl.ANY)
HBM = pl.BlockSpec(memory_space=pltpu.HBM)


def split(v):
    high = v.astype(jnp.bfloat16)
    return high, (v - high.astype(F32)).astype(jnp.bfloat16)


def dot(a, b):
    one = functools.partial(jnp.dot, preferred_element_type=F32)
    (a_high, a_low), (b_high, b_low) = split(a), split(b)
    return one(a_high, b_high) + (one(a_high, b_low) + one(a_low, b_high))


def exact(a, b):
    return jnp.dot(a, b, precision=lax.Precision.HIGHEST, preferred_element_type=F32)


def counters(length, repeat):
    return lax.broadcasted_iota(jnp.int32, (length * repeat,), 0) // repeat + 1


def sine_table(length, repeat_rows=1, repeat_columns=1):
    product = counters(length, repeat_rows)[:, None] * counters(length, repeat_columns)[None, :]
    product = product % (2 * (length + 1))
    return math.sqrt(2.0 / (length + 1)) * jnp.sin(product.astype(F32) * (math.pi / (length + 1)))


def spectrum(length):
    half = jnp.sin(counters(length, 1).astype(F32) * (math.pi / (2 * (length + 1))))
    lam = 4.0 * half * half
    return (lam + lam * lam)[None, :]


def call(kernel, outs, in_specs, flops, name, scratch=(), out_specs=None):
    return pl.pallas_call(
        kernel,
        out_shape=outs,
        in_specs=in_specs,
        out_specs=out_specs or jax.tree.map(lambda _: VMEM, outs),
        scratch_shapes=list(scratch),
        compiler_params=pltpu.CompilerParams(vmem_limit_bytes=LIMIT),
        cost_estimate=pl.CostEstimate(flops=flops, bytes_accessed=4_000_000, transcendentals=0),
        name=name,
    )


def shape(*dims):
    return jax.ShapeDtypeStruct(dims, F32)


def vmem(*dims):
    return pltpu.VMEM(dims, F32)


def fetch(sources, targets, sems):
    copies = [pltpu.make_async_copy(a, b, sems.at[i]) for i, (a, b) in enumerate(zip(sources, targets))]
    for copy in copies:
        copy.start()
    return copies


def shifted(v, axis, step):
    size = v.shape[axis]
    rolled = pltpu.roll(v, (-step) % size, axis)
    at = lax.broadcasted_iota(jnp.int32, v.shape, axis)
    return jnp.where(at == (size - 1 if step > 0 else 0), 0.0, rolled)


def mixed(weight, values):
    total = weight(0) * values[0]
    for g in range(1, FIELDS):
        total = total + weight(g) * values[g]
    return total


def spot(c, b):
    return (b // 2) * 4 + c * 2 + b % 2


def tables_kernel(rates, sine_z, spec_z, sine_y, spec_y, solve_z, solve_y):
    for c in range(2):
        for f in range(FIELDS):
            denom = 1.0 + rates[2, c, f] * spec_z[...]
            solve_z[c, f] = exact(sine_z[...] / denom, sine_z[...])
            denom = 1.0 + rates[1, c, f] * spec_y[...]
            solve_y[c, f] = exact(sine_y[...] / denom, sine_y[...])


def tables_y_kernel(rates, token, sine_y, spec_y, solve_y):
    for c in range(2):
        for f in range(FIELDS):
            denom = 1.0 + rates[1, c, f] * spec_y[...]
            solve_y[c, f] = exact(sine_y[...] / denom, sine_y[...])


def tables_b_kernel(info, coup, left_map, right_map, rates, token, sine_z, spec_z, left, right, left_2, right_2, spec_x,
                    solve_x, halo_prev, halo_next, solve_z, mixes):
    mine = info[1]
    for f in range(FIELDS):
        for g in range(FIELDS):
            near, far = 0.0, 0.0
            for h in range(FIELDS):
                near = near + left_map[f, mine, h] * right_map[h, mine, g]
                inner = 0.0
                for i in range(FIELDS):
                    inner = inner + coup[h, mine, i] * right_map[i, mine, g]
                far = far + left_map[f, mine, h] * inner
            mixes[0, f, g] = near
            mixes[1, f, g] = far
        mixes[2, f, 0] = rates[1, mine, f]
    n, nx = left.shape
    row, col = (lax.broadcasted_iota(jnp.int32, (n, n), i) for i in range(2))
    same = (row & 7) == (col & 7)
    row, col = (lax.broadcasted_iota(jnp.int32, (2 * nx, 2 * nx), i) for i in range(2))
    from_last = ((row & 1) == 0) & ((col & 1) == 1)
    from_first = ((row & 1) == 1) & ((col & 1) == 0)
    for f in range(FIELDS):
        denom = 1.0 + rates[0, mine, f] * spec_x[...]
        scaled = left[...] / denom
        solve_x[f] = jnp.where(same, exact(scaled, right[...]), 0.0)
        scaled_2 = left_2[...] / denom
        both = exact(scaled_2, right_2[...])
        halo_prev[f] = jnp.where(from_last, both, 0.0)
        halo_next[f] = jnp.where(from_first, both, 0.0)
        denom = 1.0 + rates[2, mine, f] * spec_z[...]
        solve_z[f] = exact(sine_z[...] / denom, sine_z[...])


def first_kernel(info, coup, left, adjoint, other, source_in, radius, solve_z, solve_y, out, token,
                 source, made, lapped, stage, sems, out_sems):
    copies = fetch([source_in.at[c] for c in range(2)], [source.at[c] for c in range(2)], sems)
    ny = adjoint.shape[3]
    blocks = ny // 8
    me = info[0]
    before, after = me.astype(F32), (1 - me).astype(F32)
    token[...] = jnp.zeros(token.shape, F32)
    stores = []
    for c in range(2):
        residual = {}
        for x in range(2):
            for f in range(FIELDS):
                v = adjoint[c, f, x]
                beside = adjoint[c, f, 1 - x]
                beside = beside + (other[c, f, 1] * before if x == 0 else other[c, f, 0] * after)
                beside = beside + shifted(v, 0, 1) + shifted(v, 0, -1)
                beside = beside + shifted(v, 1, 1) + shifted(v, 1, -1)
                lapped[x, f] = 6.0 * v - beside
        copies[c].wait()
        for x in range(2):
            sr = radius[x]
            residual = []
            for f in range(FIELDS):
                r = source[c, f, x] - sr * adjoint[c, f, x]
                for g in range(FIELDS):
                    r = r - coup[f, c, g] * lapped[x, g]
                residual.append(r)
            for f in range(FIELDS):
                stage[f, x * ny : x * ny + ny] = mixed(lambda g: left[f, c, g], residual)
        outer = [adjoint[c, g, me] for g in range(FIELDS)]
        outer = [mixed(lambda g: coup[f, c, g], outer) for f in range(FIELDS)]
        for f in range(FIELDS):
            stage[f, 2 * ny : 3 * ny] = mixed(lambda g: left[f, c, g], outer)
        for f in range(FIELDS):
            r = dot(stage[f], solve_z[c, f])
            r = jnp.concatenate([r[p * ny : p * ny + ny] for p in range(3)], axis=1)
            r = dot(solve_y[c, f], r)
            for p in range(3):
                for b in range(blocks):
                    made[b // 2, c, b % 2, 3 * f + p] = r[8 * b : 8 * b + 8, 128 * p : 128 * p + 128]
        for x in range(2):
            for b in range(blocks):
                made[b // 2, c, b % 2, 3 * FIELDS + x] = radius[x, 8 * b : 8 * b + 8]
        stores.append(pltpu.make_async_copy(made.at[:, c], out.at[:, c], out_sems.at[c]))
        stores[-1].start()
    for copy in stores:
        copy.wait()


def assembled(lines, f):
    zero = jnp.zeros((1, 8, 128), F32)
    w = lines[:, 3 * f : 3 * f + 3].reshape(lines.shape[0] // 2, 6, 8, 128)
    plane_0 = w[:, 0] + jnp.concatenate([zero, w[:-1, 5]], axis=0)
    plane_3 = w[:, 4] + jnp.concatenate([w[1:, 2], zero], axis=0)
    return jnp.stack([plane_0, w[:, 1], w[:, 3], plane_3], axis=1)


def ends_kernel(lines, solve_x, to_prev, to_next):
    n = solve_x.shape[1]
    for f in range(FIELDS):
        u = dot(solve_x[f], assembled(lines, f).reshape(n, 128))
        quad = u.reshape(n // 32, 4, 8, 128)
        for j in range(4):
            to_prev[f, :, 2 * j : 2 * j + 2, :] = quad[:, j, 0:2, :]
            to_next[f, :, 2 * j : 2 * j + 2, :] = quad[:, j, 6:8, :]


def second_kernel(info, mixes, lines, solve_x, solve_z, out, solved, lapped, kept):
    nx = out.shape[1]
    full = (nx, 8, 128)
    row = lax.broadcasted_iota(jnp.int32, full, 1)
    has_prev, has_next = info[2].astype(F32), info[3].astype(F32)
    zero = jnp.zeros((1, 8, 128), F32)
    for f in range(FIELDS):
        u = dot(solve_x[f], assembled(lines, f).reshape(nx * 8, 128)).reshape(full)
        solved[f] = u
        up = jnp.where(row == 7, 0.0, pltpu.roll(u, 7, 1))
        down = jnp.where(row == 0, 0.0, pltpu.roll(u, 1, 1))
        ku = 2.0 * u - up - down
        k_up = jnp.where(row == 7, -has_next * u, pltpu.roll(ku, 7, 1))
        k_down = jnp.where(row == 0, -has_prev * u, pltpu.roll(ku, 1, 1))
        kku = 2.0 * ku - k_up - k_down
        kept[f] = 2.0 * (u + mixes[2, f, 0] * (ku + kku))
        beside = jnp.concatenate([zero, u[:-1]], axis=0) + jnp.concatenate([u[1:], zero], axis=0)
        flat = u.reshape(nx * 8, 128)
        beside = beside + (shifted(flat, 1, 1) + shifted(flat, 1, -1)).reshape(full)
        lapped[f] = 4.0 * u + ku - beside
    sr = lines[:, 3 * FIELDS :].reshape(full)
    for f in range(FIELDS):
        near = mixed(lambda g: mixes[0, f, g], solved)
        far = mixed(lambda g: mixes[1, f, g], lapped)
        v = (sr * near + far).reshape(nx * 8, 128)
        v = dot(solve_x[f], dot(v, solve_z[f]))
        out[f] = kept[f] - v.reshape(full)


def halo_kernel(mixes, local, from_prev, from_next, halo_prev, halo_next, solve_z, out, token, made, sems):
    nx = local.shape[1]
    full = (nx, 8, 128)
    row = lax.broadcasted_iota(jnp.int32, full, 1)
    odd = (lax.broadcasted_iota(jnp.int32, (2 * nx, 128), 0) & 1) == 1
    token[...] = jnp.zeros(token.shape, F32)
    stores = []
    for f in range(FIELDS):
        first, last = from_prev[f], from_next[f]
        far = jnp.concatenate(
            [mixed(lambda g: mixes[1, f, g], from_prev), mixed(lambda g: mixes[1, f, g], from_next)], axis=0
        )
        far = dot(far, solve_z[f])
        far_prev, far_next = far[: 2 * nx], far[2 * nx :]
        scale = 2.0 * mixes[2, f, 0]
        add_prev = jnp.where(odd, first, first - 5.0 * pltpu.roll(first, 2 * nx - 1, 0))
        add_next = jnp.where(odd, last - 5.0 * pltpu.roll(last, 1, 0), last)
        add_prev = scale * add_prev + dot(halo_prev[f], far_prev)
        add_next = scale * add_next + dot(halo_next[f], far_next)
        spread = lambda v, at: jnp.stack(
            [pltpu.roll(v.reshape(nx // 4, 8, 128), (at - 2 * j) % 8, 1) for j in range(4)], axis=1
        ).reshape(full)
        q = local[f] + jnp.where(
            row < 2, spread(add_prev, 0), jnp.where(row >= 6, spread(add_next, 6), 0.0)
        )
        made[:, 2 * f : 2 * f + 2] = q.reshape(nx // 2, 2, 8, 128)
        part = pl.ds(2 * f, 2)
        stores.append(pltpu.make_async_copy(made.at[:, part], out.at[:, part], sems.at[f]))
        stores[-1].start()
    for copy in stores:
        copy.wait()


def gathered(solved, c, tile, blocks):
    return jnp.concatenate([solved[spot(c, b), tile] for b in range(blocks)], axis=0)


def update_kernel(info, right, adjoint, solved, solve_y, out, inner, outer, step):
    ny = adjoint.shape[3]
    me = info[0]
    for c in range(2):
        for f in range(FIELDS):
            q = jnp.concatenate([gathered(solved, c, 2 * f + x, ny // 8) for x in range(2)], axis=1)
            step[f] = dot(solve_y[c, f], q)
        steps = [[step[g, :, 128 * x : 128 * x + 128] for g in range(FIELDS)] for x in range(2)]
        for f in range(FIELDS):
            planes = [adjoint[c, f, x] + mixed(lambda g: right[f, c, g], steps[x]) for x in range(2)]
            for x in range(2):
                out[c, f, x] = planes[x]
            inner[c, f] = jnp.where(me == 0, planes[1], planes[0])
            outer[c, f] = jnp.where(me == 0, planes[0], planes[1])


def inside_kernel(smap, weights, adjoint, terms):
    totals = [[0.0, 0.0] for _ in range(3)]
    for c in range(2):
        weight = weights[c].astype(F32)
        for f in range(FIELDS):
            w = [weight * smap[k, c, f] for k in range(3)]
            v = [adjoint[c, f, x] for x in range(2)]
            pair = w[0] * (v[0] * v[1])
            totals[0][0] += pair
            totals[0][1] -= pair
            for x in range(2):
                for k in range(2):
                    totals[k + 1][x] += w[k + 1] * (v[x] * (shifted(v[x], k, 1) - shifted(v[x], k, -1)))
    for k in range(3):
        for x in range(2):
            terms[k, x] = totals[k][x]


def terms_kernel(info, smap, weights, outer, other_outer, inner, other_inner, inside, out):
    me = info[0]
    ny = inner.shape[2]
    each = out.shape[1]

    def store(k, x, v):
        for i in range(ny // 4):
            piece, at = divmod((k * 2 + x) * (ny // 4) + i, each)
            out[piece, at] = v[4 * i : 4 * i + 4]

    with_core, with_chip = 0.0, 0.0
    for c in range(2):
        weight = weights[c].astype(F32)
        for f in range(FIELDS):
            w = weight * smap[0, c, f]
            with_core += w * (inner[c, f] * other_inner[c, f])
            with_chip += w * (outer[c, f] * other_outer[c, f])
    store(0, 0, inside[0, 0] - jnp.where(me == 0, with_chip, with_core))
    store(0, 1, inside[0, 1] + jnp.where(me == 0, with_core, with_chip))
    for k in range(1, 3):
        for x in range(2):
            store(k, x, inside[k, x])
    for i in range(6 * ny // 4, out.shape[0] * each):
        piece, at = divmod(i, each)
        out[piece, at] = jnp.zeros(out.shape[2:], F32)


def sum_kernel(scale, pieces, out):
    total = pieces[0]
    for i in range(1, pieces.shape[0]):
        total = total + pieces[i]
    total = total * scale
    for i in range(out.shape[0]):
        out[i] = total


def body(
    adjoint_source,
    adjoint_start,
    spectral_radius,
    coupling,
    left_vectors,
    right_vectors,
    implicit_scales,
    sensitivity_map,
    condition_weights,
):
    peers = lax.axis_size("grid")
    conds = lax.axis_size("cond")
    _, fields, planes, ny, nz = adjoint_start.shape
    nx = peers * planes
    rows_b = nx * 8
    blocks = peers // 2
    sems = lambda n: pltpu.SemaphoreType.DMA((n,))

    me = lax.axis_index("grid")
    core = me % 2
    side = (me // 2) % 2
    place = (me // 4) * 2 + core
    info = jnp.stack([core, side, place > 0, place < blocks - 1]).astype(jnp.int32)

    cores = [(i, i ^ 1) for i in range(peers)]
    chips = [(i, i + 1) for i in range(1, peers - 1, 2)]
    chips = chips + [(j, i) for i, j in chips]
    other = lax.ppermute(adjoint_start, "grid", cores)

    sine_z, spec_z = sine_table(nz), spectrum(nz)
    sine_y, spec_y = sine_table(ny), spectrum(ny)

    coup, left_map, right_map, smap = (
        jnp.swapaxes(v, 0, 1) for v in (coupling, left_vectors, right_vectors, sensitivity_map)
    )
    rates = jnp.transpose(implicit_scales, (2, 0, 1))

    solve_z, solve_y = call(
        tables_kernel,
        (shape(2, fields, nz, nz), shape(2, fields, ny, ny)),
        [SMEM] + [VMEM] * 4,
        100_000_000,
        "solve_tables",
    )(rates, sine_z, spec_z, sine_y, spec_y)

    lines, token = call(
        first_kernel,
        (shape(blocks // 2, 2, 2, 3 * fields + planes, 8, nz), shape(8, nz)),
        [SMEM, SMEM, SMEM, VMEM, VMEM, HBM, VMEM, VMEM, VMEM],
        200_000_000,
        "first_residual",
        [
            vmem(2, fields, planes, ny, nz),
            vmem(blocks // 2, 2, 2, 3 * fields + planes, 8, nz),
            vmem(planes, fields, ny, nz),
            vmem(fields, 3 * ny, nz),
            sems(2),
            sems(2),
        ],
        (ANY, VMEM),
    )(info, coup, left_map, adjoint_start, other, adjoint_source, spectral_radius, solve_z, solve_y)

    lines = lines.reshape(peers, 3 * fields + planes, 8, nz)
    lines = lax.all_to_all(lines, "grid", 0, 0, tiled=True)

    solve_x, halo_prev, halo_next, solve_zb, mixes = call(
        tables_b_kernel,
        (
            shape(fields, rows_b, rows_b),
            shape(fields, 2 * nx, 2 * nx),
            shape(fields, 2 * nx, 2 * nx),
            shape(fields, nz, nz),
            shape(3, fields, fields),
        ),
        [SMEM] * 5 + [VMEM] * 8,
        100_000_000,
        "tables_b",
        (),
        (VMEM,) * 4 + (SMEM,),
    )(
        info, coup, left_map, right_map, rates, token, sine_z, spec_z,
        sine_table(nx, 8, 1), sine_table(nx, 1, 8), sine_table(nx, 2, 1), sine_table(nx, 1, 2), spectrum(nx),
    )

    to_prev, to_next = call(
        ends_kernel,
        (shape(fields, nx // 4, 8, nz), shape(fields, nx // 4, 8, nz)),
        [VMEM] * 2,
        100_000_000,
        "solve_ends",
    )(lines, solve_x)
    to_prev, to_next = (v.reshape(fields, 2 * nx, nz) for v in (to_prev, to_next))

    up = [(spot(s, b), spot(s, b + 1)) for s in range(2) for b in range(blocks - 1)]
    down = [(j, i) for i, j in up]
    from_prev = lax.ppermute(to_next, "grid", up)
    from_next = lax.ppermute(to_prev, "grid", down)

    local = call(
        second_kernel,
        shape(fields, nx, 8, nz),
        [SMEM, SMEM] + [VMEM] * 3,
        300_000_000,
        "second_residual",
        [vmem(fields, nx, 8, nz) for _ in range(3)],
    )(info, mixes, lines, solve_x, solve_zb)

    step, token = call(
        halo_kernel,
        (shape(peers, planes * fields, 8, nz), shape(8, nz)),
        [SMEM] + [VMEM] * 6,
        50_000_000,
        "halo_rows",
        [vmem(peers, planes * fields, 8, nz), sems(fields)],
        (ANY, VMEM),
    )(mixes, local, from_prev, from_next, halo_prev, halo_next, solve_zb)

    step = lax.all_to_all(step, "grid", 0, 0, tiled=True)

    solve_y = call(
        tables_y_kernel,
        shape(2, fields, ny, ny),
        [SMEM, VMEM, VMEM, VMEM],
        50_000_000,
        "tables_y",
    )(rates, token, sine_y, spec_y)

    slab = shape(2, fields, ny, nz)
    adjoint, inner, outer = call(
        update_kernel,
        (shape(2, fields, planes, ny, nz), slab, slab),
        [SMEM, SMEM] + [VMEM] * 3,
        60_000_000,
        "update",
        [vmem(fields, ny, 2 * nz)],
    )(info, right_map, adjoint_start, step, solve_y)

    other_inner = lax.ppermute(inner, "grid", cores)
    other_outer = lax.ppermute(outer, "grid", chips)

    inside = call(
        inside_kernel,
        shape(3, planes, ny, nz),
        [SMEM, SMEM, VMEM],
        60_000_000,
        "inside_terms",
    )(smap, condition_weights, adjoint)

    tiles = 3 * planes * ny // 4
    each = -(-tiles // conds)
    pieces = call(
        terms_kernel,
        shape(conds, each, 4, nz),
        [SMEM] * 3 + [VMEM] * 5,
        10_000_000,
        "terms",
    )(info, smap, condition_weights, outer, other_outer, inner, other_inner, inside)
    pieces = lax.all_to_all(pieces, "cond", 0, 0, tiled=True)
    scale = 1.0 / (conds * condition_weights.shape[0])
    pieces = call(
        functools.partial(sum_kernel, scale),
        shape(conds, each, 4, nz),
        [VMEM],
        1_000_000,
        "sum_conditions",
    )(pieces)
    pieces = lax.all_to_all(pieces, "cond", 0, 0, tiled=True)
    total = pieces.reshape(conds * each * 4, nz)[: tiles * 4].reshape(3, planes, ny, nz)
    return (adjoint, total)


def solution(mesh):
    in_specs = (
        P("cond", None, "grid", None, None),
        P("cond", None, "grid", None, None),
        P("grid", None, None),
        P("cond", None, None),
        P("cond", None, None),
        P("cond", None, None),
        P("cond", None, None),
        P("cond", None, None),
        P("cond"),
    )
    out_specs = (P("cond", None, "grid", None, None), P(None, "grid", None, None))
    return jax.shard_map(body, mesh=mesh, in_specs=in_specs, out_specs=out_specs, check_vma=False)
```

```python
import functools
import math

import jax
import jax.numpy as jnp
from jax import lax
from jax.experimental import pallas as pl
from jax.experimental.pallas import tpu as pltpu
from jax.sharding import PartitionSpec as P

F32 = jnp.float32
FIELDS = 5
VMEM = pl.BlockSpec(memory_space=pltpu.VMEM)
SMEM = pl.BlockSpec(memory_space=pltpu.SMEM)
LIMIT = 20 * 1024 * 1024
ANY = pl.BlockSpec(memory_space=pl.ANY)
HBM = pl.BlockSpec(memory_space=pltpu.HBM)


def split(v):
    high = v.astype(jnp.bfloat16)
    return high, (v - high.astype(F32)).astype(jnp.bfloat16)


def dot(a, b):
    one = functools.partial(jnp.dot, preferred_element_type=F32)
    (a_high, a_low), (b_high, b_low) = split(a), split(b)
    return one(a_high, b_high) + (one(a_high, b_low) + one(a_low, b_high))


def exact(a, b):
    return jnp.dot(a, b, precision=lax.Precision.HIGHEST, preferred_element_type=F32)


def counters(length, repeat):
    return lax.broadcasted_iota(jnp.int32, (length * repeat,), 0) // repeat + 1


def sine_table(length, repeat_rows=1, repeat_columns=1):
    product = counters(length, repeat_rows)[:, None] * counters(length, repeat_columns)[None, :]
    product = product % (2 * (length + 1))
    return math.sqrt(2.0 / (length + 1)) * jnp.sin(product.astype(F32) * (math.pi / (length + 1)))


def spectrum(length):
    half = jnp.sin(counters(length, 1).astype(F32) * (math.pi / (2 * (length + 1))))
    lam = 4.0 * half * half
    return (lam + lam * lam)[None, :]


def call(kernel, outs, in_specs, flops, name, scratch=(), out_specs=None):
    return pl.pallas_call(
        kernel,
        out_shape=outs,
        in_specs=in_specs,
        out_specs=out_specs or jax.tree.map(lambda _: VMEM, outs),
        scratch_shapes=list(scratch),
        compiler_params=pltpu.CompilerParams(vmem_limit_bytes=LIMIT),
        cost_estimate=pl.CostEstimate(flops=flops, bytes_accessed=4_000_000, transcendentals=0),
        name=name,
    )


def shape(*dims):
    return jax.ShapeDtypeStruct(dims, F32)


def vmem(*dims):
    return pltpu.VMEM(dims, F32)


def fetch(sources, targets, sems):
    copies = [pltpu.make_async_copy(a, b, sems.at[i]) for i, (a, b) in enumerate(zip(sources, targets))]
    for copy in copies:
        copy.start()
    return copies


def shifted(v, axis, step):
    size = v.shape[axis]
    rolled = pltpu.roll(v, (-step) % size, axis)
    at = lax.broadcasted_iota(jnp.int32, v.shape, axis)
    return jnp.where(at == (size - 1 if step > 0 else 0), 0.0, rolled)


def mixed(weight, values):
    total = weight(0) * values[0]
    for g in range(1, FIELDS):
        total = total + weight(g) * values[g]
    return total


def spot(c, b):
    return (b // 2) * 4 + c * 2 + b % 2


def tables_kernel(rates, sine_z, spec_z, sine_y, spec_y, solve_z, solve_y):
    for c in range(2):
        for f in range(FIELDS):
            denom = 1.0 + rates[2, c, f] * spec_z[...]
            solve_z[c, f] = exact(sine_z[...] / denom, sine_z[...])
            denom = 1.0 + rates[1, c, f] * spec_y[...]
            solve_y[c, f] = exact(sine_y[...] / denom, sine_y[...])


def tables_y_kernel(rates, token, sine_y, spec_y, solve_y):
    for c in range(2):
        for f in range(FIELDS):
            denom = 1.0 + rates[1, c, f] * spec_y[...]
            solve_y[c, f] = exact(sine_y[...] / denom, sine_y[...])


def tables_b_kernel(info, coup, left_map, right_map, rates, token, sine_z, spec_z, left, right, left_2, right_2, spec_x,
                    solve_x, halo_prev, halo_next, solve_z, mixes):
    mine = info[1]
    for f in range(FIELDS):
        for g in range(FIELDS):
            near, far = 0.0, 0.0
            for h in range(FIELDS):
                near = near + left_map[f, mine, h] * right_map[h, mine, g]
                inner = 0.0
                for i in range(FIELDS):
                    inner = inner + coup[h, mine, i] * right_map[i, mine, g]
                far = far + left_map[f, mine, h] * inner
            mixes[0, f, g] = near
            mixes[1, f, g] = far
        mixes[2, f, 0] = rates[1, mine, f]
    n, nx = left.shape
    row, col = (lax.broadcasted_iota(jnp.int32, (n, n), i) for i in range(2))
    same = (row & 7) == (col & 7)
    row, col = (lax.broadcasted_iota(jnp.int32, (2 * nx, 2 * nx), i) for i in range(2))
    from_last = ((row & 1) == 0) & ((col & 1) == 1)
    from_first = ((row & 1) == 1) & ((col & 1) == 0)
    for f in range(FIELDS):
        denom = 1.0 + rates[0, mine, f] * spec_x[...]
        scaled = left[...] / denom
        solve_x[f] = jnp.where(same, exact(scaled, right[...]), 0.0)
        scaled_2 = left_2[...] / denom
        both = exact(scaled_2, right_2[...])
        halo_prev[f] = jnp.where(from_last, both, 0.0)
        halo_next[f] = jnp.where(from_first, both, 0.0)
        denom = 1.0 + rates[2, mine, f] * spec_z[...]
        solve_z[f] = exact(sine_z[...] / denom, sine_z[...])


def plane_kernel(info, adjoint, inner, sem):
    copy = pltpu.make_async_copy(adjoint.at[:, :, 1 - info[0]], inner, sem)
    copy.start()
    copy.wait()


def first_kernel(info, coup, left, adjoint, other, source_in, radius, solve_z, solve_y, out, token,
                 source, made, lapped, stage, sems, out_sems):
    copies = fetch([source_in.at[c] for c in range(2)], [source.at[c] for c in range(2)], sems)
    ny = adjoint.shape[3]
    blocks = ny // 8
    me = info[0]
    before, after = me.astype(F32), (1 - me).astype(F32)
    token[...] = jnp.zeros(token.shape, F32)
    stores = []
    for c in range(2):
        residual = {}
        for x in range(2):
            for f in range(FIELDS):
                v = adjoint[c, f, x]
                beside = adjoint[c, f, 1 - x]
                beside = beside + other[c, f] * (before if x == 0 else after)
                beside = beside + shifted(v, 0, 1) + shifted(v, 0, -1)
                beside = beside + shifted(v, 1, 1) + shifted(v, 1, -1)
                lapped[x, f] = 6.0 * v - beside
        copies[c].wait()
        for x in range(2):
            sr = radius[x]
            residual = []
            for f in range(FIELDS):
                r = source[c, f, x] - sr * adjoint[c, f, x]
                for g in range(FIELDS):
                    r = r - coup[f, c, g] * lapped[x, g]
                residual.append(r)
            for f in range(FIELDS):
                stage[f, x * ny : x * ny + ny] = mixed(lambda g: left[f, c, g], residual)
        outer = [adjoint[c, g, me] for g in range(FIELDS)]
        outer = [mixed(lambda g: coup[f, c, g], outer) for f in range(FIELDS)]
        for f in range(FIELDS):
            stage[f, 2 * ny : 3 * ny] = mixed(lambda g: left[f, c, g], outer)
        for f in range(FIELDS):
            r = dot(stage[f], solve_z[c, f])
            r = jnp.concatenate([r[p * ny : p * ny + ny] for p in range(3)], axis=1)
            r = dot(solve_y[c, f], r)
            for p in range(3):
                for b in range(blocks):
                    made[b // 2, c, b % 2, 3 * f + p] = r[8 * b : 8 * b + 8, 128 * p : 128 * p + 128]
        for x in range(2):
            for b in range(blocks):
                made[b // 2, c, b % 2, 3 * FIELDS + x] = radius[x, 8 * b : 8 * b + 8]
        stores.append(pltpu.make_async_copy(made.at[:, c], out.at[:, c], out_sems.at[c]))
        stores[-1].start()
    for copy in stores:
        copy.wait()


def assembled(lines, f):
    zero = jnp.zeros((1, 8, 128), F32)
    w = lines[:, 3 * f : 3 * f + 3].reshape(lines.shape[0] // 2, 6, 8, 128)
    plane_0 = w[:, 0] + jnp.concatenate([zero, w[:-1, 5]], axis=0)
    plane_3 = w[:, 4] + jnp.concatenate([w[1:, 2], zero], axis=0)
    return jnp.stack([plane_0, w[:, 1], w[:, 3], plane_3], axis=1)


def ends_kernel(lines, solve_x, to_prev, to_next):
    n = solve_x.shape[1]
    for f in range(FIELDS):
        u = dot(solve_x[f], assembled(lines, f).reshape(n, 128))
        quad = u.reshape(n // 32, 4, 8, 128)
        for j in range(4):
            to_prev[f, :, 2 * j : 2 * j + 2, :] = quad[:, j, 0:2, :]
            to_next[f, :, 2 * j : 2 * j + 2, :] = quad[:, j, 6:8, :]


def second_kernel(info, mixes, lines, solve_x, solve_z, out, solved, lapped, kept):
    nx = out.shape[1]
    full = (nx, 8, 128)
    row = lax.broadcasted_iota(jnp.int32, full, 1)
    has_prev, has_next = info[2].astype(F32), info[3].astype(F32)
    zero = jnp.zeros((1, 8, 128), F32)
    for f in range(FIELDS):
        u = dot(solve_x[f], assembled(lines, f).reshape(nx * 8, 128)).reshape(full)
        solved[f] = u
        up = jnp.where(row == 7, 0.0, pltpu.roll(u, 7, 1))
        down = jnp.where(row == 0, 0.0, pltpu.roll(u, 1, 1))
        ku = 2.0 * u - up - down
        k_up = jnp.where(row == 7, -has_next * u, pltpu.roll(ku, 7, 1))
        k_down = jnp.where(row == 0, -has_prev * u, pltpu.roll(ku, 1, 1))
        kku = 2.0 * ku - k_up - k_down
        kept[f] = 2.0 * (u + mixes[2, f, 0] * (ku + kku))
        beside = jnp.concatenate([zero, u[:-1]], axis=0) + jnp.concatenate([u[1:], zero], axis=0)
        flat = u.reshape(nx * 8, 128)
        beside = beside + (shifted(flat, 1, 1) + shifted(flat, 1, -1)).reshape(full)
        lapped[f] = 4.0 * u + ku - beside
    sr = lines[:, 3 * FIELDS :].reshape(full)
    for f in range(FIELDS):
        near = mixed(lambda g: mixes[0, f, g], solved)
        far = mixed(lambda g: mixes[1, f, g], lapped)
        v = (sr * near + far).reshape(nx * 8, 128)
        v = dot(solve_x[f], dot(v, solve_z[f]))
        out[f] = kept[f] - v.reshape(full)


def halo_kernel(mixes, local, from_prev, from_next, halo_prev, halo_next, solve_z, out, token, made, sems):
    nx = local.shape[1]
    full = (nx, 8, 128)
    row = lax.broadcasted_iota(jnp.int32, full, 1)
    odd = (lax.broadcasted_iota(jnp.int32, (2 * nx, 128), 0) & 1) == 1
    token[...] = jnp.zeros(token.shape, F32)
    stores = []
    for f in range(FIELDS):
        first, last = from_prev[f], from_next[f]
        far = jnp.concatenate(
            [mixed(lambda g: mixes[1, f, g], from_prev), mixed(lambda g: mixes[1, f, g], from_next)], axis=0
        )
        far = dot(far, solve_z[f])
        far_prev, far_next = far[: 2 * nx], far[2 * nx :]
        scale = 2.0 * mixes[2, f, 0]
        add_prev = jnp.where(odd, first, first - 5.0 * pltpu.roll(first, 2 * nx - 1, 0))
        add_next = jnp.where(odd, last - 5.0 * pltpu.roll(last, 1, 0), last)
        add_prev = scale * add_prev + dot(halo_prev[f], far_prev)
        add_next = scale * add_next + dot(halo_next[f], far_next)
        spread = lambda v, at: jnp.stack(
            [pltpu.roll(v.reshape(nx // 4, 8, 128), (at - 2 * j) % 8, 1) for j in range(4)], axis=1
        ).reshape(full)
        q = local[f] + jnp.where(
            row < 2, spread(add_prev, 0), jnp.where(row >= 6, spread(add_next, 6), 0.0)
        )
        made[:, 2 * f : 2 * f + 2] = q.reshape(nx // 2, 2, 8, 128)
        part = pl.ds(2 * f, 2)
        stores.append(pltpu.make_async_copy(made.at[:, part], out.at[:, part], sems.at[f]))
        stores[-1].start()
    for copy in stores:
        copy.wait()


def gathered(solved, c, tile, blocks):
    return jnp.concatenate([solved[spot(c, b), tile] for b in range(blocks)], axis=0)


def update_kernel(info, right, adjoint, solved, solve_y, out, inner, outer, step):
    ny = adjoint.shape[3]
    me = info[0]
    for c in range(2):
        for f in range(FIELDS):
            q = jnp.concatenate([gathered(solved, c, 2 * f + x, ny // 8) for x in range(2)], axis=1)
            step[f] = dot(solve_y[c, f], q)
        steps = [[step[g, :, 128 * x : 128 * x + 128] for g in range(FIELDS)] for x in range(2)]
        for f in range(FIELDS):
            planes = [adjoint[c, f, x] + mixed(lambda g: right[f, c, g], steps[x]) for x in range(2)]
            for x in range(2):
                out[c, f, x] = planes[x]
            inner[c, f] = jnp.where(me == 0, planes[1], planes[0])
            outer[c, f] = jnp.where(me == 0, planes[0], planes[1])


def inside_kernel(smap, weights, adjoint, terms):
    totals = [[0.0, 0.0] for _ in range(3)]
    for c in range(2):
        weight = weights[c].astype(F32)
        for f in range(FIELDS):
            w = [weight * smap[k, c, f] for k in range(3)]
            v = [adjoint[c, f, x] for x in range(2)]
            pair = w[0] * (v[0] * v[1])
            totals[0][0] += pair
            totals[0][1] -= pair
            for x in range(2):
                for k in range(2):
                    totals[k + 1][x] += w[k + 1] * (v[x] * (shifted(v[x], k, 1) - shifted(v[x], k, -1)))
    for k in range(3):
        for x in range(2):
            terms[k, x] = totals[k][x]


def terms_kernel(info, smap, weights, outer, other_outer, inner, other_inner, inside, out):
    me = info[0]
    ny = inner.shape[2]
    each = out.shape[1]

    def store(k, x, v):
        for i in range(ny // 4):
            piece, at = divmod((k * 2 + x) * (ny // 4) + i, each)
            out[piece, at] = v[4 * i : 4 * i + 4]

    with_core, with_chip = 0.0, 0.0
    for c in range(2):
        weight = weights[c].astype(F32)
        for f in range(FIELDS):
            w = weight * smap[0, c, f]
            with_core += w * (inner[c, f] * other_inner[c, f])
            with_chip += w * (outer[c, f] * other_outer[c, f])
    store(0, 0, inside[0, 0] - jnp.where(me == 0, with_chip, with_core))
    store(0, 1, inside[0, 1] + jnp.where(me == 0, with_core, with_chip))
    for k in range(1, 3):
        for x in range(2):
            store(k, x, inside[k, x])
    for i in range(6 * ny // 4, out.shape[0] * each):
        piece, at = divmod(i, each)
        out[piece, at] = jnp.zeros(out.shape[2:], F32)


def sum_kernel(scale, pieces, out):
    total = pieces[0]
    for i in range(1, pieces.shape[0]):
        total = total + pieces[i]
    total = total * scale
    for i in range(out.shape[0]):
        out[i] = total


def body(
    adjoint_source,
    adjoint_start,
    spectral_radius,
    coupling,
    left_vectors,
    right_vectors,
    implicit_scales,
    sensitivity_map,
    condition_weights,
):
    peers = lax.axis_size("grid")
    conds = lax.axis_size("cond")
    _, fields, planes, ny, nz = adjoint_start.shape
    nx = peers * planes
    rows_b = nx * 8
    blocks = peers // 2
    sems = lambda n: pltpu.SemaphoreType.DMA((n,))

    me = lax.axis_index("grid")
    core = me % 2
    side = (me // 2) % 2
    place = (me // 4) * 2 + core
    info = jnp.stack([core, side, place > 0, place < blocks - 1]).astype(jnp.int32)

    cores = [(i, i ^ 1) for i in range(peers)]
    chips = [(i, i + 1) for i in range(1, peers - 1, 2)]
    chips = chips + [(j, i) for i, j in chips]
    other = call(
        plane_kernel,
        shape(2, fields, ny, nz),
        [SMEM, ANY],
        1000,
        "inner_plane",
        [pltpu.SemaphoreType.DMA(())],
        ANY,
    )(info, adjoint_start)
    other = lax.ppermute(other, "grid", cores)

    sine_z, spec_z = sine_table(nz), spectrum(nz)
    sine_y, spec_y = sine_table(ny), spectrum(ny)

    coup, left_map, right_map, smap = (
        jnp.swapaxes(v, 0, 1) for v in (coupling, left_vectors, right_vectors, sensitivity_map)
    )
    rates = jnp.transpose(implicit_scales, (2, 0, 1))

    solve_z, solve_y = call(
        tables_kernel,
        (shape(2, fields, nz, nz), shape(2, fields, ny, ny)),
        [SMEM] + [VMEM] * 4,
        100_000_000,
        "solve_tables",
    )(rates, sine_z, spec_z, sine_y, spec_y)

    lines, token = call(
        first_kernel,
        (shape(blocks // 2, 2, 2, 3 * fields + planes, 8, nz), shape(8, nz)),
        [SMEM, SMEM, SMEM, VMEM, VMEM, HBM, VMEM, VMEM, VMEM],
        200_000_000,
        "first_residual",
        [
            vmem(2, fields, planes, ny, nz),
            vmem(blocks // 2, 2, 2, 3 * fields + planes, 8, nz),
            vmem(planes, fields, ny, nz),
            vmem(fields, 3 * ny, nz),
            sems(2),
            sems(2),
        ],
        (ANY, VMEM),
    )(info, coup, left_map, adjoint_start, other, adjoint_source, spectral_radius, solve_z, solve_y)

    lines = lines.reshape(peers, 3 * fields + planes, 8, nz)
    lines = lax.all_to_all(lines, "grid", 0, 0, tiled=True)

    solve_x, halo_prev, halo_next, solve_zb, mixes = call(
        tables_b_kernel,
        (
            shape(fields, rows_b, rows_b),
            shape(fields, 2 * nx, 2 * nx),
            shape(fields, 2 * nx, 2 * nx),
            shape(fields, nz, nz),
            shape(3, fields, fields),
        ),
        [SMEM] * 5 + [VMEM] * 8,
        100_000_000,
        "tables_b",
        (),
        (VMEM,) * 4 + (SMEM,),
    )(
        info, coup, left_map, right_map, rates, token, sine_z, spec_z,
        sine_table(nx, 8, 1), sine_table(nx, 1, 8), sine_table(nx, 2, 1), sine_table(nx, 1, 2), spectrum(nx),
    )

    to_prev, to_next = call(
        ends_kernel,
        (shape(fields, nx // 4, 8, nz), shape(fields, nx // 4, 8, nz)),
        [VMEM] * 2,
        100_000_000,
        "solve_ends",
    )(lines, solve_x)
    to_prev, to_next = (v.reshape(fields, 2 * nx, nz) for v in (to_prev, to_next))

    up = [(spot(s, b), spot(s, b + 1)) for s in range(2) for b in range(blocks - 1)]
    down = [(j, i) for i, j in up]
    from_prev = lax.ppermute(to_next, "grid", up)
    from_next = lax.ppermute(to_prev, "grid", down)

    local = call(
        second_kernel,
        shape(fields, nx, 8, nz),
        [SMEM, SMEM] + [VMEM] * 3,
        300_000_000,
        "second_residual",
        [vmem(fields, nx, 8, nz) for _ in range(3)],
    )(info, mixes, lines, solve_x, solve_zb)

    step, token = call(
        halo_kernel,
        (shape(peers, planes * fields, 8, nz), shape(8, nz)),
        [SMEM] + [VMEM] * 6,
        50_000_000,
        "halo_rows",
        [vmem(peers, planes * fields, 8, nz), sems(fields)],
        (ANY, VMEM),
    )(mixes, local, from_prev, from_next, halo_prev, halo_next, solve_zb)

    step = lax.all_to_all(step, "grid", 0, 0, tiled=True)

    solve_y = call(
        tables_y_kernel,
        shape(2, fields, ny, ny),
        [SMEM, VMEM, VMEM, VMEM],
        50_000_000,
        "tables_y",
    )(rates, token, sine_y, spec_y)

    slab = shape(2, fields, ny, nz)
    adjoint, inner, outer = call(
        update_kernel,
        (shape(2, fields, planes, ny, nz), slab, slab),
        [SMEM, SMEM] + [VMEM] * 3,
        60_000_000,
        "update",
        [vmem(fields, ny, 2 * nz)],
    )(info, right_map, adjoint_start, step, solve_y)

    other_inner = lax.ppermute(inner, "grid", cores)
    other_outer = lax.ppermute(outer, "grid", chips)

    inside = call(
        inside_kernel,
        shape(3, planes, ny, nz),
        [SMEM, SMEM, VMEM],
        60_000_000,
        "inside_terms",
    )(smap, condition_weights, adjoint)

    tiles = 3 * planes * ny // 4
    each = -(-tiles // conds)
    pieces = call(
        terms_kernel,
        shape(conds, each, 4, nz),
        [SMEM] * 3 + [VMEM] * 5,
        10_000_000,
        "terms",
    )(info, smap, condition_weights, outer, other_outer, inner, other_inner, inside)
    pieces = lax.all_to_all(pieces, "cond", 0, 0, tiled=True)
    scale = 1.0 / (conds * condition_weights.shape[0])
    pieces = call(
        functools.partial(sum_kernel, scale),
        shape(conds, each, 4, nz),
        [VMEM],
        1_000_000,
        "sum_conditions",
    )(pieces)
    pieces = lax.all_to_all(pieces, "cond", 0, 0, tiled=True)
    total = pieces.reshape(conds * each * 4, nz)[: tiles * 4].reshape(3, planes, ny, nz)
    return (adjoint, total)


def solution(mesh):
    in_specs = (
        P("cond", None, "grid", None, None),
        P("cond", None, "grid", None, None),
        P("grid", None, None),
        P("cond", None, None),
        P("cond", None, None),
        P("cond", None, None),
        P("cond", None, None),
        P("cond", None, None),
        P("cond"),
    )
    out_specs = (P("cond", None, "grid", None, None), P(None, "grid", None, None))
    return jax.shard_map(body, mesh=mesh, in_specs=in_specs, out_specs=out_specs, check_vma=False)
```

```python
import functools
import math

import jax
import jax.numpy as jnp
from jax import lax
from jax.experimental import pallas as pl
from jax.experimental.pallas import tpu as pltpu
from jax.sharding import PartitionSpec as P

F32 = jnp.float32
FIELDS = 5
VMEM = pl.BlockSpec(memory_space=pltpu.VMEM)
SMEM = pl.BlockSpec(memory_space=pltpu.SMEM)
LIMIT = 20 * 1024 * 1024
ANY = pl.BlockSpec(memory_space=pl.ANY)
HBM = pl.BlockSpec(memory_space=pltpu.HBM)


def split(v):
    high = v.astype(jnp.bfloat16)
    return high, (v - high.astype(F32)).astype(jnp.bfloat16)


def dot(a, b):
    one = functools.partial(jnp.dot, preferred_element_type=F32)
    (a_high, a_low), (b_high, b_low) = (v if isinstance(v, tuple) else split(v) for v in (a, b))
    return one(a_high, b_high) + (one(a_high, b_low) + one(a_low, b_high))


def keep(ref, at, v):
    ref[(0, *at)], ref[(1, *at)] = split(v)


def kept_at(ref, *at):
    return ref[(0, *at)], ref[(1, *at)]


def exact(a, b):
    return jnp.dot(a, b, precision=lax.Precision.HIGHEST, preferred_element_type=F32)


def counters(length, repeat):
    return lax.broadcasted_iota(jnp.int32, (length * repeat,), 0) // repeat + 1


def sine_table(length, repeat_rows=1, repeat_columns=1):
    product = counters(length, repeat_rows)[:, None] * counters(length, repeat_columns)[None, :]
    product = product % (2 * (length + 1))
    return math.sqrt(2.0 / (length + 1)) * jnp.sin(product.astype(F32) * (math.pi / (length + 1)))


def spectrum(length):
    half = jnp.sin(counters(length, 1).astype(F32) * (math.pi / (2 * (length + 1))))
    lam = 4.0 * half * half
    return (lam + lam * lam)[None, :]


def call(kernel, outs, in_specs, flops, name, scratch=(), out_specs=None):
    return pl.pallas_call(
        kernel,
        out_shape=outs,
        in_specs=in_specs,
        out_specs=out_specs or jax.tree.map(lambda _: VMEM, outs),
        scratch_shapes=list(scratch),
        compiler_params=pltpu.CompilerParams(vmem_limit_bytes=LIMIT),
        cost_estimate=pl.CostEstimate(flops=flops, bytes_accessed=4_000_000, transcendentals=0),
        name=name,
    )


def shape(*dims):
    return jax.ShapeDtypeStruct(dims, F32)


def parts(*dims):
    return jax.ShapeDtypeStruct((2, *dims), jnp.bfloat16)


def vmem(*dims):
    return pltpu.VMEM(dims, F32)


def fetch(sources, targets, sems):
    copies = [pltpu.make_async_copy(a, b, sems.at[i]) for i, (a, b) in enumerate(zip(sources, targets))]
    for copy in copies:
        copy.start()
    return copies


def shifted(v, axis, step):
    size = v.shape[axis]
    rolled = pltpu.roll(v, (-step) % size, axis)
    at = lax.broadcasted_iota(jnp.int32, v.shape, axis)
    return jnp.where(at == (size - 1 if step > 0 else 0), 0.0, rolled)


def mixed(weight, values):
    total = weight(0) * values[0]
    for g in range(1, FIELDS):
        total = total + weight(g) * values[g]
    return total


def spot(c, b):
    return (b // 2) * 4 + c * 2 + b % 2


def tables_kernel(rates, sine_z, spec_z, sine_y, spec_y, solve_z, solve_y):
    for c in range(2):
        for f in range(FIELDS):
            denom = 1.0 + rates[2, c, f] * spec_z[...]
            keep(solve_z, (c, f), exact(sine_z[...] / denom, sine_z[...]))
            denom = 1.0 + rates[1, c, f] * spec_y[...]
            keep(solve_y, (c, f), exact(sine_y[...] / denom, sine_y[...]))


def tables_y_kernel(rates, token, sine_y, spec_y, solve_y):
    for c in range(2):
        for f in range(FIELDS):
            denom = 1.0 + rates[1, c, f] * spec_y[...]
            keep(solve_y, (c, f), exact(sine_y[...] / denom, sine_y[...]))


def tables_b_kernel(info, coup, left_map, right_map, rates, token, sine_z, spec_z, left, right, left_2, right_2, spec_x,
                    solve_x, halo_prev, halo_next, solve_z, mixes):
    mine = info[1]
    for f in range(FIELDS):
        for g in range(FIELDS):
            near, far = 0.0, 0.0
            for h in range(FIELDS):
                near = near + left_map[f, mine, h] * right_map[h, mine, g]
                inner = 0.0
                for i in range(FIELDS):
                    inner = inner + coup[h, mine, i] * right_map[i, mine, g]
                far = far + left_map[f, mine, h] * inner
            mixes[0, f, g] = near
            mixes[1, f, g] = far
        mixes[2, f, 0] = rates[1, mine, f]
    n, nx = left.shape
    row, col = (lax.broadcasted_iota(jnp.int32, (n, n), i) for i in range(2))
    same = (row & 7) == (col & 7)
    row, col = (lax.broadcasted_iota(jnp.int32, (2 * nx, 2 * nx), i) for i in range(2))
    from_last = ((row & 1) == 0) & ((col & 1) == 1)
    from_first = ((row & 1) == 1) & ((col & 1) == 0)
    for f in range(FIELDS):
        denom = 1.0 + rates[0, mine, f] * spec_x[...]
        scaled = left[...] / denom
        keep(solve_x, (f,), jnp.where(same, exact(scaled, right[...]), 0.0))
        scaled_2 = left_2[...] / denom
        both = exact(scaled_2, right_2[...])
        keep(halo_prev, (f,), jnp.where(from_last, both, 0.0))
        keep(halo_next, (f,), jnp.where(from_first, both, 0.0))
        denom = 1.0 + rates[2, mine, f] * spec_z[...]
        keep(solve_z, (f,), exact(sine_z[...] / denom, sine_z[...]))


def plane_kernel(info, adjoint, inner, sem):
    copy = pltpu.make_async_copy(adjoint.at[:, :, 1 - info[0]], inner, sem)
    copy.start()
    copy.wait()


def first_kernel(info, coup, left, adjoint, other, source_in, radius, solve_z, solve_y, out, token,
                 source, made, lapped, stage, sems, out_sems):
    copies = fetch([source_in.at[c] for c in range(2)], [source.at[c] for c in range(2)], sems)
    ny = adjoint.shape[3]
    blocks = ny // 8
    me = info[0]
    before, after = me.astype(F32), (1 - me).astype(F32)
    token[...] = jnp.zeros(token.shape, F32)
    stores = []
    for c in range(2):
        residual = {}
        for x in range(2):
            for f in range(FIELDS):
                v = adjoint[c, f, x]
                beside = adjoint[c, f, 1 - x]
                beside = beside + other[c, f] * (before if x == 0 else after)
                beside = beside + shifted(v, 0, 1) + shifted(v, 0, -1)
                beside = beside + shifted(v, 1, 1) + shifted(v, 1, -1)
                lapped[x, f] = 6.0 * v - beside
        copies[c].wait()
        for x in range(2):
            sr = radius[x]
            residual = []
            for f in range(FIELDS):
                r = source[c, f, x] - sr * adjoint[c, f, x]
                for g in range(FIELDS):
                    r = r - coup[f, c, g] * lapped[x, g]
                residual.append(r)
            for f in range(FIELDS):
                stage[f, x * ny : x * ny + ny] = mixed(lambda g: left[f, c, g], residual)
        outer = [adjoint[c, g, me] for g in range(FIELDS)]
        outer = [mixed(lambda g: coup[f, c, g], outer) for f in range(FIELDS)]
        for f in range(FIELDS):
            stage[f, 2 * ny : 3 * ny] = mixed(lambda g: left[f, c, g], outer)
        for f in range(FIELDS):
            r = dot(stage[f], kept_at(solve_z, c, f))
            r = jnp.concatenate([r[p * ny : p * ny + ny] for p in range(3)], axis=1)
            r = dot(kept_at(solve_y, c, f), r)
            for p in range(3):
                for b in range(blocks):
                    made[b // 2, c, b % 2, 3 * f + p] = r[8 * b : 8 * b + 8, 128 * p : 128 * p + 128]
        for x in range(2):
            for b in range(blocks):
                made[b // 2, c, b % 2, 3 * FIELDS + x] = radius[x, 8 * b : 8 * b + 8]
        stores.append(pltpu.make_async_copy(made.at[:, c], out.at[:, c], out_sems.at[c]))
        stores[-1].start()
    for copy in stores:
        copy.wait()


def assembled(lines, f):
    zero = jnp.zeros((1, 8, 128), F32)
    w = lines[:, 3 * f : 3 * f + 3].reshape(lines.shape[0] // 2, 6, 8, 128)
    plane_0 = w[:, 0] + jnp.concatenate([zero, w[:-1, 5]], axis=0)
    plane_3 = w[:, 4] + jnp.concatenate([w[1:, 2], zero], axis=0)
    return jnp.stack([plane_0, w[:, 1], w[:, 3], plane_3], axis=1)


def ends_kernel(lines, solve_x, to_prev, to_next):
    n = solve_x.shape[2]
    for f in range(FIELDS):
        u = dot(kept_at(solve_x, f), assembled(lines, f).reshape(n, 128))
        quad = u.reshape(n // 32, 4, 8, 128)
        for j in range(4):
            to_prev[f, :, 2 * j : 2 * j + 2, :] = quad[:, j, 0:2, :]
            to_next[f, :, 2 * j : 2 * j + 2, :] = quad[:, j, 6:8, :]


def second_kernel(info, mixes, lines, solve_x, solve_z, out, solved, lapped, kept):
    nx = out.shape[1]
    full = (nx, 8, 128)
    row = lax.broadcasted_iota(jnp.int32, full, 1)
    has_prev, has_next = info[2].astype(F32), info[3].astype(F32)
    zero = jnp.zeros((1, 8, 128), F32)
    for f in range(FIELDS):
        u = dot(kept_at(solve_x, f), assembled(lines, f).reshape(nx * 8, 128)).reshape(full)
        solved[f] = u
        up = jnp.where(row == 7, 0.0, pltpu.roll(u, 7, 1))
        down = jnp.where(row == 0, 0.0, pltpu.roll(u, 1, 1))
        ku = 2.0 * u - up - down
        k_up = jnp.where(row == 7, -has_next * u, pltpu.roll(ku, 7, 1))
        k_down = jnp.where(row == 0, -has_prev * u, pltpu.roll(ku, 1, 1))
        kku = 2.0 * ku - k_up - k_down
        kept[f] = 2.0 * (u + mixes[2, f, 0] * (ku + kku))
        beside = jnp.concatenate([zero, u[:-1]], axis=0) + jnp.concatenate([u[1:], zero], axis=0)
        flat = u.reshape(nx * 8, 128)
        beside = beside + (shifted(flat, 1, 1) + shifted(flat, 1, -1)).reshape(full)
        lapped[f] = 4.0 * u + ku - beside
    sr = lines[:, 3 * FIELDS :].reshape(full)
    for f in range(FIELDS):
        near = mixed(lambda g: mixes[0, f, g], solved)
        far = mixed(lambda g: mixes[1, f, g], lapped)
        v = (sr * near + far).reshape(nx * 8, 128)
        v = dot(kept_at(solve_x, f), dot(v, kept_at(solve_z, f)))
        out[f] = kept[f] - v.reshape(full)


def halo_kernel(mixes, local, from_prev, from_next, halo_prev, halo_next, solve_z, out, token, made, sems):
    nx = local.shape[1]
    full = (nx, 8, 128)
    row = lax.broadcasted_iota(jnp.int32, full, 1)
    odd = (lax.broadcasted_iota(jnp.int32, (2 * nx, 128), 0) & 1) == 1
    token[...] = jnp.zeros(token.shape, F32)
    stores = []
    for f in range(FIELDS):
        first, last = from_prev[f], from_next[f]
        far = jnp.concatenate(
            [mixed(lambda g: mixes[1, f, g], from_prev), mixed(lambda g: mixes[1, f, g], from_next)], axis=0
        )
        far = dot(far, kept_at(solve_z, f))
        far_prev, far_next = far[: 2 * nx], far[2 * nx :]
        scale = 2.0 * mixes[2, f, 0]
        add_prev = jnp.where(odd, first, first - 5.0 * pltpu.roll(first, 2 * nx - 1, 0))
        add_next = jnp.where(odd, last - 5.0 * pltpu.roll(last, 1, 0), last)
        add_prev = scale * add_prev + dot(kept_at(halo_prev, f), far_prev)
        add_next = scale * add_next + dot(kept_at(halo_next, f), far_next)
        spread = lambda v, at: jnp.stack(
            [pltpu.roll(v.reshape(nx // 4, 8, 128), (at - 2 * j) % 8, 1) for j in range(4)], axis=1
        ).reshape(full)
        q = local[f] + jnp.where(
            row < 2, spread(add_prev, 0), jnp.where(row >= 6, spread(add_next, 6), 0.0)
        )
        made[:, 2 * f : 2 * f + 2] = q.reshape(nx // 2, 2, 8, 128)
        part = pl.ds(2 * f, 2)
        stores.append(pltpu.make_async_copy(made.at[:, part], out.at[:, part], sems.at[f]))
        stores[-1].start()
    for copy in stores:
        copy.wait()


def gathered(solved, c, tile, blocks):
    return jnp.concatenate([solved[spot(c, b), tile] for b in range(blocks)], axis=0)


def update_kernel(info, right, adjoint, solved, solve_y, out, inner, outer, step):
    ny = adjoint.shape[3]
    me = info[0]
    for c in range(2):
        for f in range(FIELDS):
            q = jnp.concatenate([gathered(solved, c, 2 * f + x, ny // 8) for x in range(2)], axis=1)
            step[f] = dot(kept_at(solve_y, c, f), q)
        steps = [[step[g, :, 128 * x : 128 * x + 128] for g in range(FIELDS)] for x in range(2)]
        for f in range(FIELDS):
            planes = [adjoint[c, f, x] + mixed(lambda g: right[f, c, g], steps[x]) for x in range(2)]
            for x in range(2):
                out[c, f, x] = planes[x]
            inner[c, f] = jnp.where(me == 0, planes[1], planes[0])
            outer[c, f] = jnp.where(me == 0, planes[0], planes[1])


def inside_kernel(smap, weights, adjoint, terms):
    totals = [[0.0, 0.0] for _ in range(3)]
    for c in range(2):
        weight = weights[c].astype(F32)
        for f in range(FIELDS):
            w = [weight * smap[k, c, f] for k in range(3)]
            v = [adjoint[c, f, x] for x in range(2)]
            pair = w[0] * (v[0] * v[1])
            totals[0][0] += pair
            totals[0][1] -= pair
            for x in range(2):
                for k in range(2):
                    totals[k + 1][x] += w[k + 1] * (v[x] * (shifted(v[x], k, 1) - shifted(v[x], k, -1)))
    for k in range(3):
        for x in range(2):
            terms[k, x] = totals[k][x]


def terms_kernel(info, smap, weights, outer, other_outer, inner, other_inner, inside, out):
    me = info[0]
    ny = inner.shape[2]
    each = out.shape[1]

    def store(k, x, v):
        for i in range(ny // 4):
            piece, at = divmod((k * 2 + x) * (ny // 4) + i, each)
            out[piece, at] = v[4 * i : 4 * i + 4]

    with_core, with_chip = 0.0, 0.0
    for c in range(2):
        weight = weights[c].astype(F32)
        for f in range(FIELDS):
            w = weight * smap[0, c, f]
            with_core += w * (inner[c, f] * other_inner[c, f])
            with_chip += w * (outer[c, f] * other_outer[c, f])
    store(0, 0, inside[0, 0] - jnp.where(me == 0, with_chip, with_core))
    store(0, 1, inside[0, 1] + jnp.where(me == 0, with_core, with_chip))
    for k in range(1, 3):
        for x in range(2):
            store(k, x, inside[k, x])
    for i in range(6 * ny // 4, out.shape[0] * each):
        piece, at = divmod(i, each)
        out[piece, at] = jnp.zeros(out.shape[2:], F32)


def sum_kernel(scale, pieces, out):
    total = pieces[0]
    for i in range(1, pieces.shape[0]):
        total = total + pieces[i]
    total = total * scale
    for i in range(out.shape[0]):
        out[i] = total


def body(
    adjoint_source,
    adjoint_start,
    spectral_radius,
    coupling,
    left_vectors,
    right_vectors,
    implicit_scales,
    sensitivity_map,
    condition_weights,
):
    peers = lax.axis_size("grid")
    conds = lax.axis_size("cond")
    _, fields, planes, ny, nz = adjoint_start.shape
    nx = peers * planes
    rows_b = nx * 8
    blocks = peers // 2
    sems = lambda n: pltpu.SemaphoreType.DMA((n,))

    me = lax.axis_index("grid")
    core = me % 2
    side = (me // 2) % 2
    place = (me // 4) * 2 + core
    info = jnp.stack([core, side, place > 0, place < blocks - 1]).astype(jnp.int32)

    cores = [(i, i ^ 1) for i in range(peers)]
    chips = [(i, i + 1) for i in range(1, peers - 1, 2)]
    chips = chips + [(j, i) for i, j in chips]
    other = call(
        plane_kernel,
        shape(2, fields, ny, nz),
        [SMEM, ANY],
        1000,
        "inner_plane",
        [pltpu.SemaphoreType.DMA(())],
        ANY,
    )(info, adjoint_start)
    other = lax.ppermute(other, "grid", cores)

    sine_z, spec_z = sine_table(nz), spectrum(nz)
    sine_y, spec_y = sine_table(ny), spectrum(ny)

    coup, left_map, right_map, smap = (
        jnp.swapaxes(v, 0, 1) for v in (coupling, left_vectors, right_vectors, sensitivity_map)
    )
    rates = jnp.transpose(implicit_scales, (2, 0, 1))

    solve_z, solve_y = call(
        tables_kernel,
        (parts(2, fields, nz, nz), parts(2, fields, ny, ny)),
        [SMEM] + [VMEM] * 4,
        100_000_000,
        "solve_tables",
    )(rates, sine_z, spec_z, sine_y, spec_y)

    lines, token = call(
        first_kernel,
        (shape(blocks // 2, 2, 2, 3 * fields + planes, 8, nz), shape(8, nz)),
        [SMEM, SMEM, SMEM, VMEM, VMEM, HBM, VMEM, VMEM, VMEM],
        200_000_000,
        "first_residual",
        [
            vmem(2, fields, planes, ny, nz),
            vmem(blocks // 2, 2, 2, 3 * fields + planes, 8, nz),
            vmem(planes, fields, ny, nz),
            vmem(fields, 3 * ny, nz),
            sems(2),
            sems(2),
        ],
        (ANY, VMEM),
    )(info, coup, left_map, adjoint_start, other, adjoint_source, spectral_radius, solve_z, solve_y)

    lines = lines.reshape(peers, 3 * fields + planes, 8, nz)
    lines = lax.all_to_all(lines, "grid", 0, 0, tiled=True)

    solve_x, halo_prev, halo_next, solve_zb, mixes = call(
        tables_b_kernel,
        (
            parts(fields, rows_b, rows_b),
            parts(fields, 2 * nx, 2 * nx),
            parts(fields, 2 * nx, 2 * nx),
            parts(fields, nz, nz),
            shape(3, fields, fields),
        ),
        [SMEM] * 5 + [VMEM] * 8,
        100_000_000,
        "tables_b",
        (),
        (VMEM,) * 4 + (SMEM,),
    )(
        info, coup, left_map, right_map, rates, token, sine_z, spec_z,
        sine_table(nx, 8, 1), sine_table(nx, 1, 8), sine_table(nx, 2, 1), sine_table(nx, 1, 2), spectrum(nx),
    )

    to_prev, to_next = call(
        ends_kernel,
        (shape(fields, nx // 4, 8, nz), shape(fields, nx // 4, 8, nz)),
        [VMEM] * 2,
        100_000_000,
        "solve_ends",
    )(lines, solve_x)
    to_prev, to_next = (v.reshape(fields, 2 * nx, nz) for v in (to_prev, to_next))

    up = [(spot(s, b), spot(s, b + 1)) for s in range(2) for b in range(blocks - 1)]
    down = [(j, i) for i, j in up]
    from_prev = lax.ppermute(to_next, "grid", up)
    from_next = lax.ppermute(to_prev, "grid", down)

    local = call(
        second_kernel,
        shape(fields, nx, 8, nz),
        [SMEM, SMEM] + [VMEM] * 3,
        300_000_000,
        "second_residual",
        [vmem(fields, nx, 8, nz) for _ in range(3)],
    )(info, mixes, lines, solve_x, solve_zb)

    step, token = call(
        halo_kernel,
        (shape(peers, planes * fields, 8, nz), shape(8, nz)),
        [SMEM] + [VMEM] * 6,
        50_000_000,
        "halo_rows",
        [vmem(peers, planes * fields, 8, nz), sems(fields)],
        (ANY, VMEM),
    )(mixes, local, from_prev, from_next, halo_prev, halo_next, solve_zb)

    step = lax.all_to_all(step, "grid", 0, 0, tiled=True)

    solve_y = call(
        tables_y_kernel,
        parts(2, fields, ny, ny),
        [SMEM, VMEM, VMEM, VMEM],
        50_000_000,
        "tables_y",
    )(rates, token, sine_y, spec_y)

    slab = shape(2, fields, ny, nz)
    adjoint, inner, outer = call(
        update_kernel,
        (shape(2, fields, planes, ny, nz), slab, slab),
        [SMEM, SMEM] + [VMEM] * 3,
        60_000_000,
        "update",
        [vmem(fields, ny, 2 * nz)],
    )(info, right_map, adjoint_start, step, solve_y)

    other_inner = lax.ppermute(inner, "grid", cores)
    other_outer = lax.ppermute(outer, "grid", chips)

    inside = call(
        inside_kernel,
        shape(3, planes, ny, nz),
        [SMEM, SMEM, VMEM],
        60_000_000,
        "inside_terms",
    )(smap, condition_weights, adjoint)

    tiles = 3 * planes * ny // 4
    each = -(-tiles // conds)
    pieces = call(
        terms_kernel,
        shape(conds, each, 4, nz),
        [SMEM] * 3 + [VMEM] * 5,
        10_000_000,
        "terms",
    )(info, smap, condition_weights, outer, other_outer, inner, other_inner, inside)
    pieces = lax.all_to_all(pieces, "cond", 0, 0, tiled=True)
    scale = 1.0 / (conds * condition_weights.shape[0])
    pieces = call(
        functools.partial(sum_kernel, scale),
        shape(conds, each, 4, nz),
        [VMEM],
        1_000_000,
        "sum_conditions",
    )(pieces)
    pieces = lax.all_to_all(pieces, "cond", 0, 0, tiled=True)
    total = pieces.reshape(conds * each * 4, nz)[: tiles * 4].reshape(3, planes, ny, nz)
    return (adjoint, total)


def solution(mesh):
    in_specs = (
        P("cond", None, "grid", None, None),
        P("cond", None, "grid", None, None),
        P("grid", None, None),
        P("cond", None, None),
        P("cond", None, None),
        P("cond", None, None),
        P("cond", None, None),
        P("cond", None, None),
        P("cond"),
    )
    out_specs = (P("cond", None, "grid", None, None), P(None, "grid", None, None))
    return jax.shard_map(body, mesh=mesh, in_specs=in_specs, out_specs=out_specs, check_vma=False)
```
